32 devices in a mesh: section: 2 (over y), dp: 16 (over z, x, core).
Axes of the slice: x: 2, y: 2, z: 4, core: 2. Of those that a mesh axis runs over, the one named last changes fastest.
Arguments:
- tokens: bfloat16 [2, 4096, 576], P(None, 'dp'), may hold values from -6 to 6
- segments: int32 [2, 16, 256], P(None, 'dp'), may hold values from 0 to 3, never falling along the last dimension, each value on 1 to 128 neighbouring positions
- w_query: bfloat16 [2, 331776], P('section', 'dp'), may hold values from -0.375 to 0.375
- w_key: bfloat16 [2, 110592], P('section', 'dp'), may hold values from -0.375 to 0.375
- w_value: bfloat16 [2, 110592], P('section', 'dp'), may hold values from -0.25 to 0.25
- w_out: bfloat16 [2, 331776], P('section', 'dp'), may hold values from -0.75 to 0.75
- w_gate: bfloat16 [2, 884736], P('section', 'dp'), may hold values from -0.25 to 0.25
- w_up: bfloat16 [2, 884736], P('section', 'dp'), may hold values from -0.25 to 0.25
- w_down: bfloat16 [2, 884736], P('section', 'dp'), may hold values from -0.15625 to 0.15625
- attn_gain: float32 [2, 576], P('section'), may hold values from 0.5 to 1.5
- mlp_gain: float32 [2, 576], P('section'), may hold values from 0.5 to 1.5
- out_grad: bfloat16 [2, 4096, 576], P(None, 'dp'), may hold values from -6 to 6
Outputs:
- layer_out: bfloat16 [2, 2, 4096, 576], P('section', None, 'dp')
- input_grad: bfloat16 [2, 2, 4096, 576], P('section', None, 'dp')
- grad_w_query: float32 [2, 331776], P('section', 'dp')
- grad_w_key: float32 [2, 110592], P('section', 'dp')
- grad_w_value: float32 [2, 110592], P('section', 'dp')
- grad_w_out: float32 [2, 331776], P('section', 'dp')
- grad_w_gate: float32 [2, 884736], P('section', 'dp')
- grad_w_up: float32 [2, 884736], P('section', 'dp')
- grad_w_down: float32 [2, 884736], P('section', 'dp')
- grad_attn_gain: float32 [2, 576], P('section')
- grad_mlp_gain: float32 [2, 576], P('section')
The draws below stay inside these ranges and needn't reach their ends.
Inputs may be any that keep to these rules, and one draw needn't show every extreme that they name: `segments`: segment numbers never fall along a pack of 256 tokens; each document (a run of one number) has 1 to 128 tokens.
All inputs are finite; a program needn't handle non-finite values.
Results may differ from the reference program's by a relative error of at most 0.025.
The reference program's roundings to bfloat16 on the way count: a program that leaves them out, or rounds other values in their place, can miss the bound.
Values may be sent and summed in bfloat16 or wider, within the bound.
No kernel may reach another device: no remote copies, remote signals or barrier semaphores. Data moves between devices by JAX's collectives and lax.ppermute only.
A program may use at most 128 MiB of HBM per device.

```python
import math
import jax
import jax.numpy as jnp
import numpy as np
from jax import lax

D = 576
HEADS = 9
KV_HEADS = 3
HEAD = 64
FF = 1536
MICRO = 2
TOK_MB = 256
LAYERS = 2
PACKS = 16
TOKENS = 4096
QW = 576
KVW = 192


def steps_of(stream_key, shape, split, low, top_value):
    level = 1.0
    for axis_at, blocks in split:
        draws = jax.random.uniform(jax.random.fold_in(jax.random.fold_in(stream_key, 6), axis_at), (blocks,), jnp.float32, low / len(split), top_value / len(split))
        level = level * jnp.repeat(jnp.exp(draws), shape[axis_at] // blocks).reshape((-1,) + (1,) * (len(shape) - 1 - axis_at))
    return level


def split_up(amount, total, limit, skew):
    portions = [(1 << 20) // math.isqrt(standing ** skew) + 1 for standing in range(2, amount + 1)]
    spare, given = total - limit - (amount - 1), [1] * (amount - 1)
    while spare > 0:
        free = [i for i in range(amount - 1) if given[i] < limit]
        whole, left = sum([portions[i] for i in free]), spare
        for i in free:
            extra = min(limit - given[i], max(1, left * portions[i] // whole), spare)
            given[i] = given[i] + extra
            spare = spare - extra
    return np.array([limit] + given)


def ragged(own_key, number_of, total, reach, lean):
    if number_of == 2:
        one = jax.random.randint(own_key, (), max(1, total - reach), min(reach, total - 1) + 1)
        return jnp.stack([one, total - one])
    lengths = jnp.asarray(split_up(number_of, total, reach, lean), jnp.int32)
    couples = (number_of - 1) // 2
    donor, sink = lengths[1:1 + 2 * couples:2], lengths[2:2 + 2 * couples:2]
    slack = jnp.minimum(donor - 1, reach - sink)
    passed = jax.random.randint(jax.random.fold_in(own_key, 1), (couples,), 0, 1 << 20) % (slack + 1)
    lengths = lengths.at[1:1 + 2 * couples:2].set(donor - passed).at[2:2 + 2 * couples:2].set(sink + passed)
    return lengths[jax.random.permutation(jax.random.fold_in(own_key, 2), number_of)]


def scatter_about(rng, dims, scale, most, split=(), kind=jnp.bfloat16):
    level = steps_of(rng, dims, split, -0.22, 0.18) if split else 1.0
    drawn = jax.random.normal(rng, dims, jnp.float32) * scale * level
    return jnp.minimum(jnp.maximum(drawn, -most), most).astype(kind)


def setup_inputs(seed: int = 0) -> dict:
    splits = jax.random.split(jax.random.key(seed), 13)
    return {
        "tokens": scatter_about(splits[0], (MICRO, TOKENS, D), 1.0, 6.0, ((1, 16),)),
        "segments": jax.vmap(lambda own: jnp.searchsorted(jnp.cumsum(ragged(own, 4, TOK_MB, TOK_MB // 2, 2)), jnp.arange(TOK_MB), side="right"))(jax.random.split(splits[1], MICRO * PACKS)).reshape((MICRO, PACKS, TOK_MB)).astype(jnp.int32),
        "w_query": scatter_about(splits[2], (LAYERS, D * QW), (D // 2) ** -0.5, 0.375, ((0, 2), (1, 16))),
        "w_key": scatter_about(splits[3], (LAYERS, D * KVW), (D // 2) ** -0.5, 0.375, ((0, 2), (1, 16))),
        "w_value": scatter_about(splits[4], (LAYERS, D * KVW), D ** -0.5, 0.25, ((0, 2), (1, 16))),
        "w_out": scatter_about(splits[5], (LAYERS, QW * D), (QW // 8) ** -0.5, 0.75, ((0, 2), (1, 16))),
        "w_gate": scatter_about(splits[6], (LAYERS, D * FF), D ** -0.5, 0.25, ((0, 2), (1, 16))),
        "w_up": scatter_about(splits[7], (LAYERS, D * FF), D ** -0.5, 0.25, ((0, 2), (1, 16))),
        "w_down": scatter_about(splits[8], (LAYERS, FF * D), FF ** -0.5, 0.15625, ((0, 2), (1, 16))),
        "attn_gain": jnp.clip(1.0 + 0.1 * jax.random.normal(splits[9], (LAYERS, D), jnp.float32), 0.5, 1.5),
        "mlp_gain": jnp.clip(1.0 + 0.1 * jax.random.normal(splits[10], (LAYERS, D), jnp.float32), 0.5, 1.5),
        "out_grad": scatter_about(splits[11], (MICRO, TOKENS, D), 1.0, 6.0, ((1, 16),)),
    }


@jax.custom_vjp
def low(v):
    return lax.optimization_barrier(v.astype(jnp.bfloat16)).astype(jnp.float32)

@jax.custom_vjp
def low_back(v):
    return v

def low_keep(v):
    return (low(v), None)

def low_pass(kept, grad):
    return (grad,)

def back_keep(v):
    return (v, None)

def back_low(kept, grad):
    return (low(grad),)
low.defvjp(low_keep, low_pass)
low_back.defvjp(back_keep, back_low)
EPS = 1e-05
THETA = 100000.0
NEG = -1000000000.0
PREC = lax.Precision.HIGHEST

def rotate(values):
    half_dim = values.shape[-1] // 2
    return jnp.concatenate([-values[..., half_dim:], values[..., :half_dim]], -1)

def rope(values, cosine, sine_tab):
    return values * cosine + rotate(values) * sine_tab

def tables_for(seg_rows):
    count_t = seg_rows.shape[1]
    order_idx = jnp.arange(count_t, dtype=jnp.int32)
    same_doc = seg_rows[:, :, None] == seg_rows[:, None, :]
    before = (order_idx[None, :] < order_idx[:, None])[None]
    positions = lax.optimization_barrier(jnp.sum(jnp.where(same_doc & before, jnp.float32(1.0), jnp.float32(0.0)), axis=2))
    allowed = same_doc & (order_idx[None, :] <= order_idx[:, None])[None]
    inv_freq = jnp.exp(jnp.arange(HEAD // 2, dtype=jnp.float32) * (-2.0 * math.log(THETA) / HEAD))
    angles = positions[:, :, None] * inv_freq
    angles = jnp.concatenate([angles, angles], -1)
    return (jnp.cos(angles)[:, :, None, :], jnp.sin(angles)[:, :, None, :], allowed)

def rms_norm(stream, gain_row):
    return stream * lax.rsqrt(lax.optimization_barrier(jnp.mean(stream * stream, -1, keepdims=True)) + EPS) * gain_row

def layer(stream, matrices, gain_pair, tables):
    w_query, w_key, w_value, w_out, w_gate, w_up, w_down = matrices
    cosine, sine_tab, allowed = tables
    groups = stream.shape[0]
    count_t = stream.shape[1]
    repeat = HEADS // KV_HEADS
    normed_a = low(rms_norm(stream, gain_pair[0]))
    query_raw = low_back(jnp.einsum('gtd,de->gte', normed_a, w_query, precision=PREC))
    key_raw = low_back(jnp.einsum('gtd,de->gte', normed_a, w_key, precision=PREC))
    value_raw = low_back(jnp.einsum('gtd,de->gte', normed_a, w_value, precision=PREC))
    queries = low(rope(query_raw.reshape(groups, count_t, HEADS, HEAD), cosine, sine_tab))
    key_rot = low(rope(key_raw.reshape(groups, count_t, KV_HEADS, HEAD), cosine, sine_tab))
    value_low = low(value_raw).reshape(groups, count_t, KV_HEADS, HEAD)
    queries = queries.reshape(groups, count_t, KV_HEADS, repeat, HEAD)
    scores = jnp.einsum('gtkrh,gskh->gkrts', queries, key_rot, precision=PREC) * HEAD ** (-0.5)
    scores = jnp.where(allowed[:, None, None], low_back(scores), NEG)
    attend = low(jax.nn.softmax(scores, axis=-1))
    mixed_heads = jnp.einsum('gkrts,gskh->gtkrh', attend, value_low, precision=PREC)
    mixed_heads = low(low_back(mixed_heads.reshape(groups, count_t, QW)))
    middle = stream + low_back(jnp.einsum('gte,ed->gtd', mixed_heads, w_out, precision=PREC))
    normed_b = low(rms_norm(middle, gain_pair[1]))
    gate_raw = low_back(jnp.einsum('gtd,df->gtf', normed_b, w_gate, precision=PREC))
    up_raw = low_back(jnp.einsum('gtd,df->gtf', normed_b, w_up, precision=PREC))
    activated = low(jax.nn.silu(gate_raw) * up_raw)
    return middle + low_back(jnp.einsum('gtf,fd->gtd', activated, w_down, precision=PREC))

def reference(tokens, segments, w_query, w_key, w_value, w_out, w_gate, w_up, w_down, attn_gain, mlp_gain, out_grad):
    depth_n = w_query.shape[0]
    mat_shapes = ((D, QW), (D, KVW), (D, KVW), (QW, D), (D, FF), (D, FF), (FF, D))
    flat_arrays = (w_query, w_key, w_value, w_out, w_gate, w_up, w_down)
    matrices = tuple((flat_array.astype(jnp.float32).reshape((depth_n,) + mat_shape) for flat_array, mat_shape in zip(flat_arrays, mat_shapes)))
    gains = (attn_gain.astype(jnp.float32), mlp_gain.astype(jnp.float32))
    rows_all = MICRO * PACKS
    group_n = math.gcd(rows_all, 8)
    steps_n = rows_all // group_n
    stream_rows = tokens.astype(jnp.float32).reshape(steps_n, group_n, TOK_MB, D)
    seg_rows = segments.reshape(steps_n, group_n, TOK_MB)
    cot_rows = out_grad.astype(jnp.float32).reshape(steps_n, group_n, TOK_MB, D)

    def forward(stream, mats, gain_set, shifts, tables):
        layer_outs = []
        for layer_id in range(depth_n):
            stream = stream + shifts[layer_id]
            stream = layer(stream, tuple((member[layer_id] for member in mats)), (gain_set[0][layer_id], gain_set[1][layer_id]), tables)
            layer_outs.append(stream)
            if layer_id + 1 < depth_n:
                stream = low_back(low(stream))
        return (stream, jnp.stack(layer_outs))

    def one_group(carry, inputs):
        stream, seg_group, cotangent = inputs
        tables = tables_for(seg_group)
        shifts = jnp.zeros((depth_n,) + stream.shape, jnp.float32)

        def wrapped(mats, gain_set, shift_set):
            return forward(stream, mats, gain_set, shift_set, tables)
        final, pullback, layer_outs = jax.vjp(wrapped, matrices, gains, shifts, has_aux=True)
        grad_mats, grad_gains, grad_shifts = pullback(cotangent)
        carry = jax.tree.map(jnp.add, carry, (grad_mats, grad_gains))
        return (carry, (layer_outs.astype(jnp.bfloat16), grad_shifts.astype(jnp.bfloat16)))
    start_carry = jax.tree.map(jnp.zeros_like, (matrices, gains))
    totals, stacked = lax.scan(one_group, start_carry, (stream_rows, seg_rows, cot_rows))
    grad_mats, grad_gains = totals

    def arrange(blocks):
        moved = jnp.transpose(blocks, (1, 0, 2, 3, 4))
        return moved.reshape(depth_n, MICRO, PACKS * TOK_MB, D)
    layer_out = arrange(stacked[0])
    input_grad = arrange(stacked[1])
    flat_grads = tuple((member.reshape(depth_n, -1) for member in grad_mats))
    return (layer_out, input_grad, flat_grads[0], flat_grads[1], flat_grads[2], flat_grads[3], flat_grads[4], flat_grads[5], flat_grads[6], grad_gains[0], grad_gains[1])
```

```python
import functools
import math

import jax
import jax.numpy as jnp
from jax import lax
from jax.experimental import pallas as pl
from jax.experimental.pallas import tpu as pltpu
from jax.sharding import PartitionSpec as P

D = 576
HEADS = 9
KV_HEADS = 3
HEAD = 64
FF = 1536
TOK_MB = 256
QW = HEADS * HEAD
KVW = KV_HEADS * HEAD
REP = HEADS // KV_HEADS

EPS = 1e-05
THETA = 100000.0
NEG = -1000000000.0

PAD = 640
COL_K = QW
COL_O = QW + KVW
COL_V = COL_O + D
COL_VX = 1280
SKIP_V = COL_V - COL_VX

BF = jnp.bfloat16
F32 = jnp.float32

PARAMS = pltpu.CompilerParams(vmem_limit_bytes=50 * 1024 * 1024)


def dot(left, right):
    return lax.dot_general(left, right, (((1,), (0,)), ((), ())), preferred_element_type=F32)


def dot_nt(left, right):
    return lax.dot_general(left, right, (((1,), (1,)), ((), ())), preferred_element_type=F32)


def dot_tn(left, right):
    return lax.dot_general(left, right, (((0,), (0,)), ((), ())), preferred_element_type=F32)


def spread(rows, place):
    return dot(rows, place).astype(BF)


def collect(rows, place):
    high = rows.astype(BF)
    low = (rows - high.astype(F32)).astype(BF)
    return dot_nt(high, place) + dot_nt(low, place)


def turned(tile):
    lane = lax.broadcasted_iota(jnp.int32, tile.shape, 1)
    return jnp.where(lane % HEAD < HEAD // 2, pltpu.roll(tile, 128 - HEAD // 2, 1), pltpu.roll(tile, HEAD // 2, 1))


def inv_rms(stream):
    return lax.rsqrt(jnp.mean(stream * stream, -1, keepdims=True) + EPS)


def norm_back(stream, gain_row, grad_normed):
    scale_r = inv_rms(stream)
    weighted = grad_normed * gain_row
    grad_stream = scale_r * weighted - stream * scale_r**3 * jnp.mean(
        stream * weighted, -1, keepdims=True
    )
    grad_gain = jnp.sum(grad_normed * stream * scale_r, 0, keepdims=True)
    return (grad_stream, grad_gain)


CHUNK = 512


def forward_kernel(save, x_ref, att_ref, gate_ref, up_ref, down_ref, ga_ref, gb_ref, place_ref, cos_ref, sin_ref, mask_ref, out_ref, *saved):
    if save:
        na_ref, qk_ref, v_ref, lse_ref, mx_ref, mid_ref, nb_ref, g_ref, u_ref, act_ref = saved
    place = place_ref[...]
    stream = x_ref[...].astype(F32)
    normed_a = spread((stream * inv_rms(stream) * ga_ref[...]).astype(BF), place)
    raw = dot(normed_a, att_ref[:, :COL_O])
    cosine, sine = cos_ref[...], sin_ref[...]
    tiles = []
    for j in range(COL_O // 128):
        tile = raw[:, 128 * j : 128 * (j + 1)]
        tiles.append((tile * cosine + turned(tile) * sine).astype(BF))
    qk = jnp.concatenate(tiles, 1)
    value = dot(normed_a, att_ref[:, COL_VX:])[:, SKIP_V:].astype(BF)
    allowed = mask_ref[...] > 0.5
    mixed = []
    for h in range(HEADS):
        kv = h // REP
        query = qk[:, HEAD * h : HEAD * (h + 1)]
        key = qk[:, COL_K + HEAD * kv : COL_K + HEAD * (kv + 1)]
        scores = jnp.where(allowed, dot_nt(query, key) * HEAD ** (-0.5), NEG)
        row_max = jnp.max(scores, -1, keepdims=True)
        terms = jnp.exp(scores - row_max)
        total = jnp.sum(terms, -1, keepdims=True)
        attend = (terms * (1.0 / total)).astype(BF)
        mixed.append(dot(attend, value[:, HEAD * kv : HEAD * (kv + 1)]).astype(BF))
        if save:
            lse_ref[:, h : h + 1] = row_max + jnp.log(total)
    mixed_p = spread(jnp.concatenate(mixed, 1), place)
    middle = stream + dot(mixed_p, att_ref[:, COL_O : COL_O + D])
    normed_b = spread((middle * inv_rms(middle) * gb_ref[...]).astype(BF), place)
    result = middle
    for c in range(0, FF, CHUNK):
        gate = dot(normed_b, gate_ref[:, c : c + CHUNK])
        up = dot(normed_b, up_ref[:, c : c + CHUNK])
        act = (gate * jax.nn.sigmoid(gate) * up).astype(BF)
        result = result + dot(act, down_ref[c : c + CHUNK, :])
        if save:
            g_ref[:, c : c + CHUNK] = gate
            u_ref[:, c : c + CHUNK] = up
            act_ref[:, c : c + CHUNK] = act
    out_ref[...] = result.astype(BF)
    if save:
        na_ref[...] = normed_a
        qk_ref[...] = qk
        v_ref[...] = value
        mx_ref[...] = mixed_p
        mid_ref[...] = middle
        nb_ref[...] = normed_b


def backward_kernel(save, grad_ref, x_ref, att_ref, gate_ref, up_ref, down_ref, ga_ref, gb_ref, place_ref, cos_ref, sin_ref, mask_ref,
                    qk_ref, v_ref, lse_ref, mid_ref, g_ref, u_ref, in_ref, *kept):
    if save:
        dqk_ref, dv_ref, gattn_ref, dg_ref, du_ref, gains_ref = kept
    place = place_ref[...]
    grad_low = grad_ref[...]
    grad_out = grad_low.astype(F32)
    back_p = jnp.zeros((TOK_MB, PAD), F32)
    for c in range(0, FF, CHUNK):
        grad_act = dot_nt(grad_low, down_ref[c : c + CHUNK, :])
        gate = g_ref[:, c : c + CHUNK]
        up = u_ref[:, c : c + CHUNK]
        sig = jax.nn.sigmoid(gate)
        acts = grad_act * sig
        d_gate = (acts * up * (1.0 + gate * (1.0 - sig))).astype(BF)
        d_up = (acts * gate).astype(BF)
        back_p = back_p + dot_nt(d_gate, gate_ref[:, c : c + CHUNK]) + dot_nt(d_up, up_ref[:, c : c + CHUNK])
        if save:
            dg_ref[:, c : c + CHUNK] = d_gate
            du_ref[:, c : c + CHUNK] = d_up
    back_b, gain_b = norm_back(mid_ref[...], gb_ref[...], collect(back_p, place))
    grad_middle = grad_out + back_b
    grad_attn = grad_middle.astype(BF)
    grad_mixed = dot_nt(dot_nt(grad_attn, att_ref[:, COL_O : COL_O + D]).astype(BF), place).astype(BF)
    allowed = mask_ref[...] > 0.5
    d_query, d_key, d_value = [], [], []
    for kv in range(KV_HEADS):
        key = qk_ref[:, COL_K + HEAD * kv : COL_K + HEAD * (kv + 1)]
        value = v_ref[:, HEAD * kv : HEAD * (kv + 1)]
        sum_k, sum_v = None, None
        for h in range(kv * REP, (kv + 1) * REP):
            query = qk_ref[:, HEAD * h : HEAD * (h + 1)]
            grad_h = grad_mixed[:, HEAD * h : HEAD * (h + 1)]
            scores = jnp.where(allowed, dot_nt(query, key) * HEAD ** (-0.5), NEG)
            attend = jnp.exp(scores - lse_ref[:, h : h + 1])
            grad_attend = dot_nt(grad_h, value)
            inner = jnp.sum(attend * grad_attend, -1, keepdims=True)
            grad_scores = (attend * (grad_attend - inner)).astype(BF)
            part_v = dot_tn(attend.astype(BF), grad_h)
            part_k = dot_tn(grad_scores, query)
            sum_v = part_v if sum_v is None else sum_v + part_v
            sum_k = part_k if sum_k is None else sum_k + part_k
            d_query.append(dot(grad_scores, key) * HEAD ** (-0.5))
        d_key.append(sum_k * HEAD ** (-0.5))
        d_value.append(sum_v.astype(BF))
    raw = jnp.concatenate(d_query + d_key, 1)
    cosine, sine = cos_ref[...], sin_ref[...]
    tiles = []
    for j in range(COL_O // 128):
        tile = raw[:, 128 * j : 128 * (j + 1)]
        tiles.append((tile * cosine - turned(tile) * sine).astype(BF))
    d_qk = jnp.concatenate(tiles, 1)
    d_v = jnp.concatenate([jnp.zeros((TOK_MB, SKIP_V), BF)] + d_value, 1)
    back_p = dot_nt(d_qk, att_ref[:, :COL_O]) + dot_nt(d_v, att_ref[:, COL_VX:])
    back_a, gain_a = norm_back(x_ref[...].astype(F32), ga_ref[...], collect(back_p, place))
    in_ref[...] = (grad_middle + back_a).astype(BF)
    if save:
        dqk_ref[...] = d_qk
        dv_ref[...] = d_v
        gattn_ref[...] = grad_attn
        gains_ref[0:1, :] = gain_a
        gains_ref[1:2, :] = gain_b


def weights_kernel(*refs):
    ins, (att_out, gate_out, up_out, down_out) = refs[:-4], refs[-4:]
    half = len(ins) // 2
    pairs = [jnp.concatenate([one[...], two[...]], 0) for one, two in zip(ins[:half], ins[half:])]
    normed_a, mixed, normed_b, act, d_qk, d_v, grad_attn, d_gate, d_up, grad_down = pairs
    att_out[:, :COL_O] = dot_tn(normed_a, d_qk).astype(BF)
    att_out[:, COL_O:COL_VX] = dot_tn(mixed, grad_attn[:, : COL_VX - COL_O]).astype(BF)
    grad_v = dot_tn(normed_a, d_v)
    grad_o = dot_tn(mixed, grad_attn[:, COL_VX - COL_O :])
    grad_o = jnp.concatenate([grad_o, jnp.zeros((PAD, KVW), F32)], 1)
    att_out[:, COL_VX:] = (grad_v + grad_o).astype(BF)
    for c in range(0, FF, CHUNK):
        gate_out[:, c : c + CHUNK] = dot_tn(normed_b, d_gate[:, c : c + CHUNK]).astype(BF)
        up_out[:, c : c + CHUNK] = dot_tn(normed_b, d_up[:, c : c + CHUNK]).astype(BF)
        down_out[c : c + CHUNK, :] = dot_tn(act[:, c : c + CHUNK], grad_down).astype(BF)


def shape(*dims, dtype=BF):
    return jax.ShapeDtypeStruct(dims, dtype)


def run_forward(save, *operands):
    outs = [shape(TOK_MB, D)]
    if save:
        outs += [
            shape(TOK_MB, PAD),
            shape(TOK_MB, COL_O),
            shape(TOK_MB, KVW),
            shape(TOK_MB, 128, dtype=F32),
            shape(TOK_MB, PAD),
            shape(TOK_MB, D, dtype=F32),
            shape(TOK_MB, PAD),
            shape(TOK_MB, FF, dtype=F32),
            shape(TOK_MB, FF, dtype=F32),
            shape(TOK_MB, FF),
        ]
    return pl.pallas_call(
        functools.partial(forward_kernel, save), out_shape=outs, compiler_params=PARAMS, name="layer_forward"
    )(*operands)


def run_backward(save, *operands):
    outs = [shape(TOK_MB, D)]
    if save:
        outs += [
            shape(TOK_MB, COL_O),
            shape(TOK_MB, QW + D + 2 * KVW - COL_VX),
            shape(TOK_MB, D),
            shape(TOK_MB, FF),
            shape(TOK_MB, FF),
            shape(2, D, dtype=F32),
        ]
    return pl.pallas_call(
        functools.partial(backward_kernel, save), out_shape=outs, compiler_params=PARAMS, name="layer_backward"
    )(*operands)


def make_tables(seg_row):
    count_t = seg_row.shape[0]
    order_idx = jnp.arange(count_t, dtype=jnp.int32)
    same_doc = seg_row[:, None] == seg_row[None, :]
    before = order_idx[None, :] < order_idx[:, None]
    positions = jnp.sum(jnp.where(same_doc & before, jnp.float32(1.0), jnp.float32(0.0)), axis=1)
    allowed = same_doc & (order_idx[None, :] <= order_idx[:, None])
    inv_freq = jnp.exp(jnp.arange(HEAD // 2, dtype=jnp.float32) * (-2.0 * math.log(THETA) / HEAD))
    angles = positions[:, None] * inv_freq[None, :]
    cosine, sine = jnp.cos(angles), jnp.sin(angles)
    cosine = jnp.concatenate([cosine] * 4, -1)
    sine = jnp.concatenate([-sine, sine] * 2, -1)
    return (cosine, sine, allowed.astype(F32))


def placement(rows_each, rows_padded):
    row = lax.broadcasted_iota(jnp.int32, (D, PAD), 0)
    col = lax.broadcasted_iota(jnp.int32, (D, PAD), 1)
    return (col == row + (row // rows_each) * (rows_padded - rows_each)).astype(BF)


def gather_weights(shard, owners):
    w_query, w_key, w_value, w_out, w_gate, w_up, w_down = shard
    if D % owners == 0 and PAD % owners == 0 and FF % owners == 0:
        rows, padded = D // owners, PAD // owners
        att = jnp.concatenate(
            [w_query.reshape(rows, QW), w_key.reshape(rows, KVW), w_out.reshape(rows, D), w_value.reshape(rows, KVW)], 1
        )
        parts = [att, w_gate.reshape(rows, FF), w_up.reshape(rows, FF), w_down.reshape(rows, FF)]
        packed = jnp.concatenate([jnp.pad(part, ((0, padded - rows), (0, 0))) for part in parts], 0)
        whole = lax.all_gather(packed, "dp", axis=0, tiled=True).reshape(owners, 4, padded, FF)
        att, gate, up = (whole[:, i].reshape(PAD, FF) for i in range(3))
        down = whole[:, 3, :rows].reshape(FF, D)
        return att, gate, up, down, placement(rows, padded)
    w_query, w_key, w_value, w_out, w_gate, w_up, w_down = (
        lax.all_gather(member, "dp", axis=0, tiled=True) for member in (w_query[0], w_key[0], w_value[0], w_out[0], w_gate[0], w_up[0], w_down[0])
    )
    att = jnp.concatenate(
        [w_query.reshape(D, QW), w_key.reshape(D, KVW), w_out.reshape(QW, D), w_value.reshape(D, KVW)], 1
    )
    att, gate, up = (jnp.pad(m, ((0, PAD - D), (0, 0))) for m in (att, w_gate.reshape(D, FF), w_up.reshape(D, FF)))
    return att, gate, up, w_down.reshape(FF, D), placement(D, D)


def cut(att):
    return att[:, :QW], att[:, COL_K:COL_O], att[:, COL_V:], att[:, COL_O:COL_V]


def scatter_grads(grads, owners):
    att, gate, up, down = grads
    if D % owners == 0 and PAD % owners == 0 and FF % owners == 0:
        rows, padded = D // owners, PAD // owners
        down = jnp.pad(down.reshape(owners, rows, FF), ((0, 0), (0, padded - rows), (0, 0)))
        packed = jnp.stack([att.reshape(owners, padded, FF), gate.reshape(owners, padded, FF), up.reshape(owners, padded, FF), down], 1)
        packed = packed.reshape(owners * 4 * padded, FF)
        share = lax.psum_scatter(packed, "dp", scatter_dimension=0, tiled=True)
        share = share.reshape(4, padded, FF)[:, :rows].astype(F32)
        pieces = cut(share[0]) + (share[1], share[2], share[3])
        return tuple(piece.reshape(1, -1) for piece in pieces)
    pieces = cut(att[:D]) + (gate[:D], up[:D], down)
    return tuple(
        lax.psum_scatter(piece.reshape(owners, -1), "dp", scatter_dimension=0, tiled=True).astype(F32) for piece in pieces
    )


def shards(
    tokens,
    segments,
    w_query,
    w_key,
    w_value,
    w_out,
    w_gate,
    w_up,
    w_down,
    attn_gain,
    mlp_gain,
    out_grad,
):
    first = lax.axis_index("section") == 0
    owners = lax.axis_size("dp")
    *mats, place = gather_weights((w_query, w_key, w_value, w_out, w_gate, w_up, w_down), owners)
    tables = jax.vmap(make_tables)(segments[:, 0])

    def tables_of(own):
        return tuple(lax.dynamic_index_in_dim(t, own, 0, keepdims=False) for t in tables)

    def send_on(block):
        return lax.ppermute(block, "section", [(0, 1)])

    def send_back(block):
        return lax.ppermute(block, "section", [(1, 0)])

    common = (*mats, attn_gain, mlp_gain, place)
    one, two = tables_of(0), tables_of(jnp.where(first, 1, 0))
    four = tables_of(jnp.where(first, 0, 1))
    sent = run_forward(False, tokens[0], *common, *one)[0]
    x_two = jnp.where(first, tokens[1], send_on(sent))
    out_two, *stored_two = run_forward(True, x_two, *common, *two)
    arrived = send_on(out_two)

    def back(save, grad, x_rows, tables_at, stored):
        normed_a, qk, value, lse, mixed, middle, normed_b, gate, up, act = stored
        return run_backward(save, grad, x_rows, *common, *tables_at, qk, value, lse, middle, gate, up)

    grad_three = back(False, out_grad[0], x_two, two, stored_two)[0]
    arrived_grad = send_back(grad_three)
    x_four = jnp.where(first, tokens[0], arrived)
    out_four, *stored_four = run_forward(True, x_four, *common, *four)
    grad_at_five = jnp.where(first, arrived_grad, out_grad[1])
    in_five, *kept_five = back(True, grad_at_five, x_four, four, stored_four)
    grad_at_six = jnp.where(first, send_back(in_five), out_grad[0])
    in_six, *kept_six = back(True, grad_at_six, x_two, two, stored_two)

    def rows_of(stored, kept, grad):
        normed_a, qk, value, lse, mixed, middle, normed_b, gate, up, act = stored
        d_qk, d_v, grad_attn, d_gate, d_up, gains = kept
        return (normed_a, mixed, normed_b, act, d_qk, d_v, grad_attn, d_gate, d_up, grad)

    grads = pl.pallas_call(
        weights_kernel,
        out_shape=[shape(PAD, FF), shape(PAD, FF), shape(PAD, FF), shape(FF, D)],
        compiler_params=PARAMS,
        name="weight_grads",
    )(*rows_of(stored_four, kept_five, grad_at_five), *rows_of(stored_two, kept_six, grad_at_six))
    gain_sum = lax.psum(kept_five[-1] + kept_six[-1], "dp")
    shares = scatter_grads(grads, owners)
    layer_out = jnp.stack([jnp.where(first, out_four, out_two), jnp.where(first, out_two, out_four)])
    input_grad = jnp.stack([jnp.where(first, in_five, in_six), jnp.where(first, in_six, in_five)])
    return (layer_out[None], input_grad[None], *shares, gain_sum[0:1], gain_sum[1:2])


def solution(mesh):
    weights = (P("section", "dp"),) * 7
    gains = (P("section", None),) * 2
    rows = P("section", None, "dp", None)
    return jax.shard_map(
        shards,
        mesh=mesh,
        in_specs=(P(None, "dp", None), P(None, "dp", None), *weights, *gains, P(None, "dp", None)),
        out_specs=(rows, rows, *weights, *gains),
        check_vma=False,
    )
```

```python
import functools
import math

import jax
import jax.numpy as jnp
from jax import lax
from jax.experimental import pallas as pl
from jax.experimental.pallas import tpu as pltpu
from jax.sharding import PartitionSpec as P

D = 576
HEADS = 9
KV_HEADS = 3
HEAD = 64
FF = 1536
TOK_MB = 256
QW = HEADS * HEAD
KVW = KV_HEADS * HEAD
REP = HEADS // KV_HEADS

EPS = 1e-05
THETA = 100000.0
NEG = -1000000000.0

PAD = 640
COL_K = QW
COL_O = QW + KVW
COL_V = COL_O + D
COL_VX = 1280
SKIP_V = COL_V - COL_VX

BF = jnp.bfloat16
F32 = jnp.float32

PARAMS = pltpu.CompilerParams(vmem_limit_bytes=60 * 1024 * 1024)


def dot(left, right):
    return lax.dot_general(left, right, (((1,), (0,)), ((), ())), preferred_element_type=F32)


def dot_nt(left, right):
    return lax.dot_general(left, right, (((1,), (1,)), ((), ())), preferred_element_type=F32)


def dot_tn(left, right):
    return lax.dot_general(left, right, (((0,), (0,)), ((), ())), preferred_element_type=F32)


def spread(rows, place):
    return dot(rows, place).astype(BF)


def collect(rows, place):
    high = rows.astype(BF)
    low = (rows - high.astype(F32)).astype(BF)
    return dot_nt(high, place) + dot_nt(low, place)


def turned(tile):
    lane = lax.broadcasted_iota(jnp.int32, tile.shape, 1)
    return jnp.where(lane % HEAD < HEAD // 2, pltpu.roll(tile, 128 - HEAD // 2, 1), pltpu.roll(tile, HEAD // 2, 1))


def inv_rms(stream):
    return lax.rsqrt(jnp.mean(stream * stream, -1, keepdims=True) + EPS)


def norm_back(stream, gain_row, grad_normed):
    scale_r = inv_rms(stream)
    weighted = grad_normed * gain_row
    grad_stream = scale_r * weighted - stream * scale_r**3 * jnp.mean(
        stream * weighted, -1, keepdims=True
    )
    grad_gain = jnp.sum(grad_normed * stream * scale_r, 0, keepdims=True)
    return (grad_stream, grad_gain)


CHUNK = 512
CHUNKS = FF // CHUNK
HALF = TOK_MB // 2
GROUPS = 16
EACH = PAD // GROUPS
EACH_FF = FF // GROUPS
DV = QW + D + 2 * KVW - COL_VX

ANY = pl.BlockSpec(memory_space=pl.ANY)
SMEM = pl.BlockSpec(memory_space=pltpu.SMEM)
VMEM = pl.BlockSpec(memory_space=pltpu.VMEM)


def shape(*dims, dtype=BF):
    return jax.ShapeDtypeStruct(dims, dtype)


class Names:
    def __getattr__(self, name):
        return name


N = Names()


STORED = dict(
    na=shape(TOK_MB, PAD),
    qk=shape(TOK_MB, COL_O),
    v=shape(TOK_MB, KVW),
    lse=shape(TOK_MB, 128, dtype=F32),
    mx=shape(TOK_MB, PAD),
    mid=shape(TOK_MB, D, dtype=F32),
    nb=shape(TOK_MB, PAD),
    gate=shape(TOK_MB, FF, dtype=F32),
    up=shape(TOK_MB, FF, dtype=F32),
    act=shape(TOK_MB, FF),
)
FOR_BACK = (N.gate, N.up, N.mid, N.qk, N.v, N.lse)
KEPT = dict(
    dqk=shape(TOK_MB, COL_O),
    dv=shape(TOK_MB, DV),
    gattn=shape(TOK_MB, D),
    dg=shape(TOK_MB, FF),
    du=shape(TOK_MB, FF),
)
INPUTS = dict(
    agu=shape(3, PAD, FF),
    c_lo=shape(GROUPS, EACH_FF // 2, D),
    c_hi=shape(GROUPS, EACH_FF // 2, D),
    place=shape(D, PAD),
    cos=shape(2, TOK_MB, 128, dtype=F32),
    sin=shape(2, TOK_MB, 128, dtype=F32),
    mask=shape(2, TOK_MB, TOK_MB, dtype=F32),
)
HELD = dict(
    att=shape(PAD, FF),
    gw=shape(PAD, FF),
    uw=shape(PAD, FF),
    down=shape(GROUPS, EACH_FF, D),
    place=shape(D, PAD),
    cos=shape(TOK_MB, 128, dtype=F32),
    sin=shape(TOK_MB, 128, dtype=F32),
    mask=shape(TOK_MB, TOK_MB, dtype=F32),
    x=shape(TOK_MB, D),
    g=shape(TOK_MB, D),
)


class Copies:
    def __init__(self, sems):
        self.sems, self.count, self.open = sems, 0, {}

    def start(self, name, source, target):
        copy = pltpu.make_async_copy(source, target, self.sems.at[self.count])
        self.count += 1
        self.open.setdefault(name, []).append(copy)
        copy.start()

    def start_either(self, name, take_one, one, two, target):
        first = pltpu.make_async_copy(one, target, self.sems.at[self.count])
        second = pltpu.make_async_copy(two, target, self.sems.at[self.count])
        self.count += 1
        self.open.setdefault(name, []).append(first)

        @pl.when(take_one)
        def _():
            first.start()

        @pl.when(jnp.logical_not(take_one))
        def _():
            second.start()

    def wait(self, *names):
        for name in names:
            for copy in self.open.pop(name, ()):
                copy.wait()

    def wait_all(self):
        self.wait(*list(self.open))


def blocks_of_rows():
    return ((0, HALF, HALF), (HALF, TOK_MB, TOK_MB))


def forward(held, kept, copies, ga_ref, gb_ref, note):
    copies.wait(N.x, N.place)
    place = held[N.place][...]
    stream = held[N.x][...].astype(F32)
    normed_a = spread((stream * inv_rms(stream) * ga_ref[...]).astype(BF), place)
    note(N.na, normed_a)
    copies.wait(N.att, N.cos, N.sin)
    raw = dot(normed_a, held[N.att][:, :COL_O])
    cosine, sine = held[N.cos][...], held[N.sin][...]
    tiles = []
    lane = lax.broadcasted_iota(jnp.int32, (TOK_MB, 128), 1)
    for j in range(COL_O // 128):
        tile = raw[:, 128 * j : 128 * (j + 1)]
        tile = (tile * cosine + turned(tile) * sine).astype(BF)
        if 128 * (j + 1) <= QW:
            tile = tile * jnp.asarray(HEAD ** (-0.5), BF)
        elif 128 * j < QW:
            tile = jnp.where(lane < QW - 128 * j, tile.astype(F32) * HEAD ** (-0.5), tile.astype(F32)).astype(BF)
        tiles.append(tile)
    qk = jnp.concatenate(tiles, 1)
    note(N.qk, qk)
    value = dot(normed_a, held[N.att][:, COL_VX:])[:, SKIP_V:].astype(BF)
    note(N.v, value)
    copies.wait(N.mask)
    mixed = []
    for h in range(HEADS):
        kv = h // REP
        key = qk[:, COL_K + HEAD * kv : COL_K + HEAD * (kv + 1)]
        val = value[:, HEAD * kv : HEAD * (kv + 1)]
        parts = []
        for low, high, keys in blocks_of_rows():
            query = qk[low:high, HEAD * h : HEAD * (h + 1)]
            scores = jnp.where(held[N.mask][low:high, :keys] > 0.5, dot_nt(query, key[:keys]), NEG)
            row_max = jnp.max(scores, -1, keepdims=True)
            terms = jnp.exp(scores - row_max)
            total = jnp.sum(terms, -1, keepdims=True)
            attend = (terms * (1.0 / total)).astype(BF)
            parts.append(dot(attend, val[:keys]).astype(BF))
            if kept is not None:
                kept[N.lse][low:high, h : h + 1] = row_max + jnp.log(total)
        mixed.append(jnp.concatenate(parts, 0))
    note(N.lse, None)
    mixed_p = spread(jnp.concatenate(mixed, 1), place)
    note(N.mx, mixed_p)
    middle = stream + dot(mixed_p, held[N.att][:, COL_O : COL_O + D])
    note(N.mid, middle)
    normed_b = spread((middle * inv_rms(middle) * gb_ref[...]).astype(BF), place)
    note(N.nb, normed_b)
    copies.wait(N.gw, N.uw, N.down)
    result = middle
    for c in range(0, FF, CHUNK):
        gate = dot(normed_b, held[N.gw][:, c : c + CHUNK])
        up = dot(normed_b, held[N.uw][:, c : c + CHUNK])
        act = (gate * jax.nn.sigmoid(gate) * up).astype(BF)
        result = result + dot(act, down_of(held)[c : c + CHUNK])
        if kept is not None:
            kept[N.gate][:, c : c + CHUNK] = gate
            kept[N.up][:, c : c + CHUNK] = up
            kept[N.act][:, c : c + CHUNK] = act
    note(N.gate, None)
    note(N.up, None)
    note(N.act, None)
    return result.astype(BF)


def down_of(held):
    return held[N.down][...].reshape(FF, D)


def backward(held, kept, copies, ga_ref, gb_ref, note):
    copies.wait(N.g, N.down)
    grad_low = held[N.g][...]
    grad_out = grad_low.astype(F32)
    back_p = jnp.zeros((TOK_MB, PAD), F32)
    down = down_of(held)
    for c in range(0, FF, CHUNK):
        grad_act = dot_nt(grad_low, down[c : c + CHUNK])
        copies.wait(N.gate + str(c), N.up + str(c))
        gate = kept[N.gate][:, c : c + CHUNK]
        up = kept[N.up][:, c : c + CHUNK]
        sig = jax.nn.sigmoid(gate)
        acts = grad_act * sig
        d_gate = (acts * up * (1.0 + gate * (1.0 - sig))).astype(BF)
        d_up = (acts * gate).astype(BF)
        note(N.dg, d_gate, c)
        note(N.du, d_up, c)
        copies.wait(N.gw, N.uw)
        back_p = back_p + dot_nt(d_gate, held[N.gw][:, c : c + CHUNK]) + dot_nt(d_up, held[N.uw][:, c : c + CHUNK])
    copies.wait(N.place, N.mid, N.att)
    place = held[N.place][...]
    back_b, gain_b = norm_back(kept[N.mid][...], gb_ref[...], collect(back_p, place))
    grad_middle = grad_out + back_b
    grad_attn = grad_middle.astype(BF)
    note(N.gattn, grad_attn)
    grad_mixed = dot_nt(dot_nt(grad_attn, held[N.att][:, COL_O : COL_O + D]).astype(BF), place).astype(BF)
    copies.wait(N.qk, N.v, N.lse, N.mask, N.cos, N.sin, N.x)
    d_query, d_key, d_value = [], [], []
    for kv in range(KV_HEADS):
        key = kept[N.qk][:, COL_K + HEAD * kv : COL_K + HEAD * (kv + 1)]
        value = kept[N.v][:, HEAD * kv : HEAD * (kv + 1)]
        sums_k, sums_v = [None, None], [None, None]
        for h in range(kv * REP, (kv + 1) * REP):
            parts = []
            for at, (low, high, keys) in enumerate(blocks_of_rows()):
                query = kept[N.qk][low:high, HEAD * h : HEAD * (h + 1)]
                grad_h = grad_mixed[low:high, HEAD * h : HEAD * (h + 1)]
                scores = jnp.where(held[N.mask][low:high, :keys] > 0.5, dot_nt(query, key[:keys]), NEG)
                attend = jnp.exp(scores - kept[N.lse][low:high, h : h + 1])
                grad_attend = dot_nt(grad_h, value[:keys])
                inner = jnp.sum(attend * grad_attend, -1, keepdims=True)
                grad_scores = (attend * (grad_attend - inner)).astype(BF)
                part_v = dot_tn(attend.astype(BF), grad_h)
                part_k = dot_tn(grad_scores, query)
                sums_v[at] = part_v if sums_v[at] is None else sums_v[at] + part_v
                sums_k[at] = part_k if sums_k[at] is None else sums_k[at] + part_k
                parts.append(dot(grad_scores, key[:keys]) * HEAD ** (-0.5))
            d_query.append(jnp.concatenate(parts, 0))
        d_key.append(jnp.concatenate([sums_k[0] + sums_k[1][:HALF], sums_k[1][HALF:]], 0))
        d_value.append(jnp.concatenate([sums_v[0] + sums_v[1][:HALF], sums_v[1][HALF:]], 0).astype(BF))
    raw = jnp.concatenate(d_query + d_key, 1)
    cosine, sine = held[N.cos][...], held[N.sin][...]
    tiles = []
    for j in range(COL_O // 128):
        tile = raw[:, 128 * j : 128 * (j + 1)]
        tiles.append((tile * cosine - turned(tile) * sine).astype(BF))
    d_qk = jnp.concatenate(tiles, 1)
    d_v = jnp.concatenate([jnp.zeros((TOK_MB, SKIP_V), BF)] + d_value, 1)
    note(N.dqk, d_qk)
    note(N.dv, d_v)
    back_p = dot_nt(d_qk, held[N.att][:, :COL_O]) + dot_nt(d_v, held[N.att][:, COL_VX:])
    back_a, gain_a = norm_back(held[N.x][...].astype(F32), ga_ref[...], collect(back_p, place))
    return (grad_middle + back_a).astype(BF), gain_a, gain_b


SLOTS = dict(
    lead=(N.forward,),
    both=(N.forward, N.backward, N.store),
    ahead=(N.forward, N.store),
    behind=(N.backward, N.keep),
)


def layer_kernel(name, micro, names, refs):
    does = SLOTS[name]
    ref = dict(zip(names, refs))
    held = {key: ref["held_" + key] for key in HELD if "held_" + key in ref}
    kept = {key: ref["kept_" + key] for key in STORED if "kept_" + key in ref} or None
    section = ref[N.coords][3]
    index = {N.zero: 0, N.one: 1, N.same: section, N.other: 1 - section}[micro]
    copies = Copies(ref[N.sems])

    def bring(key):
        copies.start(key, ref[key].at[index], held[key])

    def bring_x():
        if N.arrived in ref:
            copies.start_either(N.x, section == 0, ref[N.tokens].at[index], ref[N.arrived], held[N.x])
        else:
            copies.start(N.x, ref[N.tokens].at[index], held[N.x])

    def bring_weights(order):
        for key in order:
            if key == N.down:
                copies.start(key, ref[N.c_lo], held[N.down].at[:, : EACH_FF // 2])
                copies.start(key, ref[N.c_hi], held[N.down].at[:, EACH_FF // 2 :])
            elif key == N.place:
                copies.start(key, ref[N.place], held[N.place])
            else:
                copies.start(key, ref[N.agu].at[(N.att, N.gw, N.uw).index(key)], held[key])

    def bring_g():
        if N.arrived_grad in ref:
            copies.start_either(N.g, section == 0, ref[N.arrived_grad], ref[N.out_grad].at[index], held[N.g])
        else:
            copies.start(N.g, ref[N.out_grad].at[index], held[N.g])

    if N.forward in does:
        bring_x()
        bring_weights([N.place, N.att])
        bring(N.cos)
        bring(N.sin)
        bring(N.mask)
        bring_weights([N.gw, N.uw, N.down])
        if N.backward in does:
            bring_g()
    else:
        bring_g()
        bring_weights([N.down])
        for c in range(0, FF, CHUNK):
            for key in (N.gate, N.up):
                copies.start(key + str(c), ref["stored_" + key].at[:, c : c + CHUNK], kept[key].at[:, c : c + CHUNK])
        bring_weights([N.gw, N.uw, N.place])
        copies.start(N.mid, ref[N.stored_mid], kept[N.mid])
        bring_weights([N.att])
        for key in (N.qk, N.v, N.lse):
            copies.start(key, ref["stored_" + key], kept[key])
        bring(N.mask)
        bring(N.cos)
        bring(N.sin)
        bring_x()

    def note_stored(key, value, column=None):
        if N.store in does:
            if value is not None:
                kept[key][...] = value
            copies.start("out_" + key, kept[key], ref["store_" + key])

    def note_kept(key, value, column=None):
        if N.keep in does:
            if column is None:
                ref["made_" + key][...] = value
            else:
                ref["made_" + key][:, column : column + CHUNK] = value
            if column in (None, FF - CHUNK):
                copies.start("out_" + key, ref["made_" + key], ref["keep_" + key])

    if N.forward in does:
        ref[N.out][...] = forward(held, kept, copies, ref[N.ga], ref[N.gb], note_stored)
    if N.backward in does:
        grad, gain_a, gain_b = backward(held, kept, copies, ref[N.ga], ref[N.gb], note_kept)
        ref[N.in_grad][...] = grad
        if N.keep in does:
            ref[N.gains][0:1, :] = gain_a
            ref[N.gains][1:2, :] = gain_b
    copies.wait_all()


def run_layer(name, micro, common, tokens, arrived=None, out_grad=None, arrived_grad=None, stored=None):
    does = SLOTS[name]
    operands = dict(coords=common[N.coords], tokens=tokens, ga=common[N.ga], gb=common[N.gb])
    operands.update({key: common[key] for key in INPUTS})
    specs = dict(coords=SMEM, ga=VMEM, gb=VMEM)
    if arrived is not None:
        operands[N.arrived] = arrived
    if N.backward in does:
        operands[N.out_grad] = out_grad
        if arrived_grad is not None:
            operands[N.arrived_grad] = arrived_grad
    if stored is not None:
        operands.update({"stored_" + key: stored[key] for key in FOR_BACK})
    outs, out_specs = {}, []
    if N.forward in does:
        outs[N.out] = shape(TOK_MB, D)
    if N.backward in does:
        outs[N.in_grad] = shape(TOK_MB, D)
    if N.keep in does:
        outs[N.gains] = shape(2, D, dtype=F32)
        outs.update({"keep_" + key: KEPT[key] for key in KEPT})
    if N.store in does:
        outs.update({"store_" + key: STORED[key] for key in STORED})
    out_specs = [ANY if key.startswith(("store_", "keep_")) else VMEM for key in outs]
    scratch = {"held_" + key: pltpu.VMEM(h.shape, h.dtype) for key, h in HELD.items() if key != N.g or N.backward in does}
    if name != N.lead:
        hold = STORED if N.forward in does else FOR_BACK
        scratch.update({"kept_" + key: pltpu.VMEM(STORED[key].shape, STORED[key].dtype) for key in hold})
    if N.keep in does:
        scratch.update({"made_" + key: pltpu.VMEM(KEPT[key].shape, BF) for key in KEPT})
    scratch[N.sems] = pltpu.SemaphoreType.DMA((40,))
    names = list(operands) + list(outs) + list(scratch)

    def kernel(*refs):
        layer_kernel(name, micro, names, refs)

    results = pl.pallas_call(
        kernel,
        out_shape=list(outs.values()),
        in_specs=[specs.get(key, ANY) for key in operands],
        out_specs=out_specs,
        scratch_shapes=list(scratch.values()),
        compiler_params=PARAMS,
        name="layer_" + name,
    )(*operands.values())
    return dict(zip(outs, results))


PAIRS = (N.act, N.g, N.nb, N.dg, N.du, N.mx, N.gattn, N.na, N.dqk, N.dv)


def slab_of(block):
    return jnp.concatenate(
        [
            jnp.concatenate([block[8 * i : 8 * i + 8, 128 * j : 128 * j + 128] for i in range(EACH_FF // 8)], 1)
            for j in range(PAD // 128)
        ],
        0,
    )


def block_of(slab):
    tiles = slab.reshape(slab.shape[:-2] + (PAD // 128, 8, EACH_FF // 8, 128))
    return jnp.moveaxis(tiles, -2, -4).swapaxes(-3, -2).reshape(slab.shape[:-2] + (EACH_FF, PAD))


def weights_kernel(names, refs):
    ref = dict(zip(names, refs))
    copies = Copies(ref[N.sems])
    own_z, own_x, own_c, section = (ref[N.coords][i] for i in range(4))
    for key in PAIRS:
        for at in range(2):
            target = ref["in_" + key].at[pl.ds(TOK_MB * at, TOK_MB)]
            if key == N.g:
                copies.start_either(
                    key, section == 0, ref["grad_%d" % at], ref[N.out_grad].at[section if at == 0 else 1 - section], target
                )
            else:
                copies.start(key, ref["%s_%d" % (key, at)], target)

    def put_pairs(keep_ref, send_ref, at, columns, blocks, pair):
        for one, two in zip(blocks[::2], blocks[1::2]):
            far, across = lax.rem(pair // 2 - own_z + 4, 4), lax.rem(pair % 2 + own_x, 2)
            index = (across, far) + at + (slice(None), columns)
            keep_ref[index] = jnp.where(own_c == 0, one, two).astype(BF)
            send_ref[index] = jnp.where(own_c == 0, two, one).astype(BF)
            pair += 1

    def put(keep_ref, send_ref, at, columns, rows):
        put_pairs(keep_ref, send_ref, at, columns, jnp.split(rows, GROUPS), 0)

    copies.wait(N.act, N.g)
    grad_down = jnp.concatenate([ref[N.in_g][...], jnp.zeros((2 * TOK_MB, PAD - D), BF)], 1)
    step = 4 * EACH_FF
    for c in range(0, FF, step):
        slabs = [slab_of(piece) for piece in jnp.split(dot_tn(ref[N.in_act][:, c : c + step], grad_down), 4)]
        put_pairs(ref[N.keep_m], ref[N.send_m], (3,), slice(0, FF), slabs, c // step * 2)
    copies.wait(N.nb, N.dg, N.du)
    normed_b = ref[N.in_nb][...]
    for at, key in ((1, N.dg), (2, N.du)):
        for c in range(0, FF, CHUNK):
            put(ref[N.keep_m], ref[N.send_m], (at,), slice(c, c + CHUNK), dot_tn(normed_b, ref["in_" + key][:, c : c + CHUNK]))
    copies.wait(N.mx, N.gattn, N.na, N.dqk, N.dv)
    normed_a, mixed = ref[N.in_na][...], ref[N.in_mx][...]
    put(ref[N.keep_m], ref[N.send_m], (0,), slice(0, COL_O), dot_tn(normed_a, ref[N.in_dqk][...]))
    put(ref[N.keep_m], ref[N.send_m], (0,), slice(COL_O, COL_VX), dot_tn(mixed, ref[N.in_gattn][:, : COL_VX - COL_O]))
    grad_o = dot_tn(mixed, ref[N.in_gattn][:, COL_VX - COL_O :])
    grad_o = jnp.concatenate([grad_o, jnp.zeros((PAD, KVW), F32)], 1)
    put(ref[N.keep_m], ref[N.send_m], (0,), slice(COL_VX, FF), dot_tn(normed_a, ref[N.in_dv][...]) + grad_o)
    copies.start(N.out, ref[N.send_m], ref[N.out_send_m])
    copies.start(N.out, ref[N.keep_m], ref[N.out_keep_m])
    copies.wait_all()


def run_weights(coords, rows, grads, out_grad):
    operands = dict(coords=coords, out_grad=out_grad)
    for at in range(2):
        operands["grad_%d" % at] = grads[at]
        operands.update({"%s_%d" % (key, at): rows[at][key] for key in PAIRS if key != N.g})
    main = shape(2, 4, 4, EACH, FF)
    outs = dict(out_keep_m=main, out_send_m=main)
    columns = {key: (STORED | KEPT | {N.g: HELD[N.g]})[key].shape[1] for key in PAIRS}
    scratch = {"in_" + key: pltpu.VMEM((2 * TOK_MB, columns[key]), BF) for key in PAIRS}
    scratch.update({key[4:]: pltpu.VMEM(out.shape, BF) for key, out in outs.items()})
    scratch[N.sems] = pltpu.SemaphoreType.DMA((32,))
    names = list(operands) + list(outs) + list(scratch)

    def kernel(*refs):
        weights_kernel(names, refs)

    results = pl.pallas_call(
        kernel,
        out_shape=list(outs.values()),
        in_specs=[SMEM] + [ANY] * (len(operands) - 1),
        out_specs=[ANY] * len(outs),
        scratch_shapes=list(scratch.values()),
        compiler_params=PARAMS,
        name=N.weight_grads,
    )(*operands.values())
    return dict(zip(outs, results))


def make_tables(seg_row):
    count_t = seg_row.shape[0]
    order_idx = jnp.arange(count_t, dtype=jnp.int32)
    same_doc = seg_row[:, None] == seg_row[None, :]
    before = order_idx[None, :] < order_idx[:, None]
    positions = jnp.sum(jnp.where(same_doc & before, jnp.float32(1.0), jnp.float32(0.0)), axis=1)
    allowed = same_doc & (order_idx[None, :] <= order_idx[:, None])
    inv_freq = jnp.exp(jnp.arange(HEAD // 2, dtype=jnp.float32) * (-2.0 * math.log(THETA) / HEAD))
    angles = positions[:, None] * inv_freq[None, :]
    cosine, sine = jnp.cos(angles), jnp.sin(angles)
    cosine = jnp.concatenate([cosine] * 4, -1)
    sine = jnp.concatenate([-sine, sine] * 2, -1)
    return (cosine, sine, allowed.astype(F32))


def placement(rows_each, rows_padded):
    row = lax.broadcasted_iota(jnp.int32, (D, PAD), 0)
    col = lax.broadcasted_iota(jnp.int32, (D, PAD), 1)
    return (col == row + (row // rows_each) * (rows_padded - rows_each)).astype(BF)


def gather_weights(shard, owners):
    w_query, w_key, w_value, w_out, w_gate, w_up, w_down = shard
    if owners == GROUPS:
        rows = D // owners
        att = jnp.concatenate(
            [w_query.reshape(rows, QW), w_key.reshape(rows, KVW), w_out.reshape(rows, D), w_value.reshape(rows, KVW)], 1
        )
        packed = jnp.stack([att, w_gate.reshape(rows, FF), w_up.reshape(rows, FF)])
        packed = jnp.pad(packed, ((0, 0), (0, EACH - rows), (0, 0)))
        agu = lax.all_gather(packed, "dp", axis=1, tiled=True)
        w_down = w_down.reshape(EACH_FF, D)
        c_lo = lax.all_gather(w_down[: EACH_FF // 2], "dp", axis=0, tiled=False)
        c_hi = lax.all_gather(w_down[EACH_FF // 2 :], "dp", axis=0, tiled=False)
        return agu, c_lo, c_hi, placement(rows, EACH)
    w_query, w_key, w_value, w_out, w_gate, w_up, w_down = (
        lax.all_gather(member[0], "dp", axis=0, tiled=True) for member in shard
    )
    att = jnp.concatenate(
        [w_query.reshape(D, QW), w_key.reshape(D, KVW), w_out.reshape(QW, D), w_value.reshape(D, KVW)], 1
    )
    agu = jnp.pad(jnp.stack([att, w_gate.reshape(D, FF), w_up.reshape(D, FF)]), ((0, 0), (0, PAD - D), (0, 0)))
    down = w_down.reshape(GROUPS, EACH_FF, D)
    return agu, down[:, : EACH_FF // 2], down[:, EACH_FF // 2 :], placement(D, D)


def cut(att):
    return att[:, :QW], att[:, COL_K:COL_O], att[:, COL_V:], att[:, COL_O:COL_V]


def place_of(z, x, c):
    return (z * 2 + x) * 2 + c


PLACES = [(z, x, c) for z in range(4) for x in range(2) for c in range(2)]


def to_core(block):
    return lax.ppermute(block, "dp", [(place_of(z, x, c), place_of(z, x, 1 - c)) for z, x, c in PLACES])


def to_across(block):
    return lax.ppermute(block, "dp", [(place_of(z, x, c), place_of(z, 1 - x, c)) for z, x, c in PLACES])


def to_far(block, far):
    return lax.ppermute(block, "dp", [(place_of(z, x, c), place_of((z + far) % 4, x, c)) for z, x, c in PLACES])


def add(*terms):
    return sum(term.astype(F32) for term in terms)


def moved(value, dz, dx, dc):
    return lax.ppermute(value, "dp", [(place_of(z, x, c), place_of(z ^ dz, x ^ dx, c ^ dc)) for z, x, c in PLACES])


def sum_of_four(value, others):
    return (value + others[0]) + (others[1] + others[2])


def reduce_blocks(keep, send, gains):
    near = [moved(gains, 0, 0, 1), moved(gains, 0, 1, 0), moved(gains, 0, 1, 1)]
    got = to_core(send)
    got, near = lax.optimization_barrier((got, near))
    gains = sum_of_four(gains, near)
    wide = [moved(gains, 1, 0, 0), moved(gains, 2, 0, 0), moved(gains, 3, 0, 0)]
    blocks = {far: add(keep[1, far], got[1, far]).astype(BF) for far in range(4)}
    one, two = to_across(blocks[2]), to_across(blocks[1])
    one, wide = lax.optimization_barrier((one, wide))
    gains = sum_of_four(gains, wide)
    term_two = add(keep[0, 2], got[0, 2], one).astype(BF)
    term_two, last = lax.optimization_barrier((term_two, blocks[3]))
    far_two, three = to_far(term_two, 2), to_across(last)
    term_one = add(keep[0, 1], got[0, 1], two).astype(BF)
    term_one, last = lax.optimization_barrier((term_one, blocks[0]))
    far_one, four = to_far(term_one, 1), to_across(last)
    three, term_one = lax.optimization_barrier((three, term_one))
    far_three = to_far(add(keep[0, 3], got[0, 3], three).astype(BF), 3)
    return add(keep[0, 0], got[0, 0], four, far_two, far_one, far_three), gains


def scatter_grads(out, gains, owners):
    if owners == GROUPS:
        main, gains = reduce_blocks(out[N.out_keep_m], out[N.out_send_m], gains)
        rows = D // owners
        att, gate, up = main[0, :rows], main[1, :rows], main[2, :rows]
        down = block_of(main[3])[:, :D]
        return tuple(piece.reshape(1, -1) for piece in cut(att) + (gate, up, down)) + (gains[0:1], gains[1:2])
    main = jnp.stack([out[N.out_keep_m], out[N.out_send_m]]).transpose(3, 2, 1, 0, 4, 5).reshape(4, GROUPS, EACH, FF)
    down = block_of(main[3])[:, :, :D].reshape(FF, D)
    main = main[:3].reshape(3, PAD, FF)[:, :D]
    pieces = cut(main[0]) + (main[1], main[2], down)
    gains = lax.psum(gains, "dp")
    return tuple(
        lax.psum_scatter(piece.reshape(owners, -1), "dp", scatter_dimension=0, tiled=True).astype(F32) for piece in pieces
    ) + (gains[0:1], gains[1:2])


def shards(
    tokens,
    segments,
    w_query,
    w_key,
    w_value,
    w_out,
    w_gate,
    w_up,
    w_down,
    attn_gain,
    mlp_gain,
    out_grad,
):
    section = lax.axis_index("section")
    first = section == 0
    owners = lax.axis_size("dp")
    me = lax.axis_index("dp") if owners == GROUPS else 0
    coords = jnp.stack([me // 4, me // 2 % 2, me % 2, section, 0, 0, 0, 0]).astype(jnp.int32)
    agu, c_lo, c_hi, place = gather_weights((w_query, w_key, w_value, w_out, w_gate, w_up, w_down), owners)
    cosine, sine, mask = jax.vmap(make_tables)(segments[:, 0])
    agu, c_lo, c_hi, place, cosine, sine, mask, tokens, out_grad, coords = lax.optimization_barrier(
        (agu, c_lo, c_hi, place, cosine, sine, mask, tokens, out_grad, coords)
    )
    common = dict(
        agu=agu, c_lo=c_lo, c_hi=c_hi, place=place, cos=cosine, sin=sine, mask=mask, coords=coords, ga=attn_gain, gb=mlp_gain
    )

    def send_on(block):
        return lax.ppermute(block, "section", [(0, 1)])

    def send_back(block):
        return lax.ppermute(block, "section", [(1, 0)])

    def stored_of(outs):
        return {key: outs["store_" + key] for key in STORED}

    def rows_of(stored, outs):
        return stored | {key: outs["keep_" + key] for key in KEPT}

    lead_zero = run_layer(N.lead, N.zero, common, tokens)[N.out]
    arrived_zero = send_on(lead_zero)
    lead_one = run_layer(N.lead, N.one, common, tokens)[N.out]
    arrived_one = send_on(lead_one)
    two = run_layer(N.both, N.other, common, tokens, arrived_zero, out_grad)
    arrived_grad = send_back(two[N.in_grad])
    four = run_layer(N.ahead, N.same, common, tokens, arrived_one)
    stored_two, stored_four = stored_of(two), stored_of(four)
    five = run_layer(N.behind, N.same, common, tokens, arrived_one, out_grad, arrived_grad, stored_four)
    last_grad = send_back(five[N.in_grad])
    six = run_layer(N.behind, N.other, common, tokens, arrived_zero, out_grad, last_grad, stored_two)
    grads = run_weights(
        coords, (rows_of(stored_four, five), rows_of(stored_two, six)), (arrived_grad, last_grad), out_grad
    )
    shares = scatter_grads(grads, five[N.gains] + six[N.gains], owners)
    layer_out = jnp.stack([jnp.where(first, four[N.out], two[N.out]), jnp.where(first, two[N.out], four[N.out])])
    input_grad = jnp.stack([jnp.where(first, five[N.in_grad], six[N.in_grad]), jnp.where(first, six[N.in_grad], five[N.in_grad])])
    return (layer_out[None], input_grad[None], *shares)


def solution(mesh):
    weights = (P("section", "dp"),) * 7
    gains = (P("section", None),) * 2
    rows = P("section", None, "dp", None)
    return jax.shard_map(
        shards,
        mesh=mesh,
        in_specs=(P(None, "dp", None), P(None, "dp", None), *weights, *gains, P(None, "dp", None)),
        out_specs=(rows, rows, *weights, *gains),
        check_vma=False,
    )
```

```python
import functools
import math

import jax
import jax.numpy as jnp
from jax import lax
from jax.experimental import pallas as pl
from jax.experimental.pallas import tpu as pltpu
from jax.sharding import PartitionSpec as P

D = 576
HEADS = 9
KV_HEADS = 3
HEAD = 64
FF = 1536
TOK_MB = 256
QW = HEADS * HEAD
KVW = KV_HEADS * HEAD
REP = HEADS // KV_HEADS

EPS = 1e-05
THETA = 100000.0
NEG = -1000000000.0

PAD = 640
COL_K = QW
COL_O = QW + KVW
COL_V = COL_O + D
COL_VX = 1280
SKIP_V = COL_V - COL_VX

BF = jnp.bfloat16
F32 = jnp.float32

PARAMS = pltpu.CompilerParams(vmem_limit_bytes=60 * 1024 * 1024)


def dot(left, right):
    return lax.dot_general(left, right, (((1,), (0,)), ((), ())), preferred_element_type=F32)


def dot_nt(left, right):
    return lax.dot_general(left, right, (((1,), (1,)), ((), ())), preferred_element_type=F32)


def dot_tn(left, right):
    return lax.dot_general(left, right, (((0,), (0,)), ((), ())), preferred_element_type=F32)


def spread(rows, place):
    return dot(rows, place).astype(BF)


def collect(rows, place):
    high = rows.astype(BF)
    low = (rows - high.astype(F32)).astype(BF)
    return dot_nt(high, place) + dot_nt(low, place)


def turned(tile):
    lane = lax.broadcasted_iota(jnp.int32, tile.shape, 1)
    return jnp.where(lane % HEAD < HEAD // 2, pltpu.roll(tile, 128 - HEAD // 2, 1), pltpu.roll(tile, HEAD // 2, 1))


def inv_rms(stream):
    return lax.rsqrt(jnp.mean(stream * stream, -1, keepdims=True) + EPS)


def norm_back(stream, gain_row, grad_normed):
    scale_r = inv_rms(stream)
    weighted = grad_normed * gain_row
    grad_stream = scale_r * weighted - stream * scale_r**3 * jnp.mean(
        stream * weighted, -1, keepdims=True
    )
    grad_gain = jnp.sum(grad_normed * stream * scale_r, 0, keepdims=True)
    return (grad_stream, grad_gain)


CHUNK = 512
CHUNKS = FF // CHUNK
HALF = TOK_MB // 2
GROUPS = 16
EACH = PAD // GROUPS
EACH_FF = FF // GROUPS
DV = QW + D + 2 * KVW - COL_VX

ANY = pl.BlockSpec(memory_space=pl.ANY)
SMEM = pl.BlockSpec(memory_space=pltpu.SMEM)
VMEM = pl.BlockSpec(memory_space=pltpu.VMEM)


def shape(*dims, dtype=BF):
    return jax.ShapeDtypeStruct(dims, dtype)


class Names:
    def __getattr__(self, name):
        return name


N = Names()


STORED = dict(
    na=shape(TOK_MB, PAD),
    qk=shape(TOK_MB, COL_O),
    v=shape(TOK_MB, KVW),
    lse=shape(TOK_MB, 128, dtype=F32),
    mx=shape(TOK_MB, PAD),
    mid=shape(TOK_MB, D, dtype=F32),
    nb=shape(TOK_MB, PAD),
    gate=shape(TOK_MB, FF, dtype=F32),
    up=shape(TOK_MB, FF, dtype=F32),
    act=shape(TOK_MB, FF),
)
FOR_BACK = (N.gate, N.up, N.mid, N.qk, N.v, N.lse)
KEPT = dict(
    dqk=shape(TOK_MB, COL_O),
    dv=shape(TOK_MB, DV),
    gattn=shape(TOK_MB, D),
    dg=shape(TOK_MB, FF),
    du=shape(TOK_MB, FF),
)
INPUTS = dict(
    agu=shape(3, PAD, FF),
    c_own=shape(GROUPS // 2, EACH_FF, D),
    c_other=shape(GROUPS // 2, EACH_FF, D),
    down=shape(GROUPS, EACH_FF, D),
    place=shape(D, PAD),
    cos=shape(2, TOK_MB, 128, dtype=F32),
    sin=shape(2, TOK_MB, 128, dtype=F32),
    mask=shape(2, TOK_MB, TOK_MB, dtype=F32),
)
HELD = dict(
    att=shape(PAD, FF),
    gw=shape(PAD, FF),
    uw=shape(PAD, FF),
    down=shape(GROUPS, EACH_FF, D),
    place=shape(D, PAD),
    cos=shape(TOK_MB, 128, dtype=F32),
    sin=shape(TOK_MB, 128, dtype=F32),
    mask=shape(TOK_MB, TOK_MB, dtype=F32),
    x=shape(TOK_MB, D),
    g=shape(TOK_MB, D),
)


class Copies:
    def __init__(self, sems):
        self.sems, self.count, self.open = sems, 0, {}

    def start(self, name, source, target):
        copy = pltpu.make_async_copy(source, target, self.sems.at[self.count])
        self.count += 1
        self.open.setdefault(name, []).append(copy)
        copy.start()

    def start_either(self, name, take_one, one, two, target):
        first = pltpu.make_async_copy(one, target, self.sems.at[self.count])
        second = pltpu.make_async_copy(two, target, self.sems.at[self.count])
        self.count += 1
        self.open.setdefault(name, []).append(first)

        @pl.when(take_one)
        def _():
            first.start()

        @pl.when(jnp.logical_not(take_one))
        def _():
            second.start()

    def wait(self, *names):
        for name in names:
            for copy in self.open.pop(name, ()):
                copy.wait()

    def wait_all(self):
        self.wait(*list(self.open))


def blocks_of_rows():
    return ((0, HALF, HALF), (HALF, TOK_MB, TOK_MB))


def forward(held, kept, copies, ga_ref, gb_ref, note):
    copies.wait(N.x, N.place)
    place = held[N.place][...]
    stream = held[N.x][...].astype(F32)
    normed_a = spread((stream * inv_rms(stream) * ga_ref[...]).astype(BF), place)
    note(N.na, normed_a)
    copies.wait(N.att, N.cos, N.sin)
    raw = dot(normed_a, held[N.att][:, :COL_O])
    cosine, sine = held[N.cos][...], held[N.sin][...]
    tiles = []
    lane = lax.broadcasted_iota(jnp.int32, (TOK_MB, 128), 1)
    for j in range(COL_O // 128):
        tile = raw[:, 128 * j : 128 * (j + 1)]
        tile = (tile * cosine + turned(tile) * sine).astype(BF)
        if 128 * (j + 1) <= QW:
            tile = tile * jnp.asarray(HEAD ** (-0.5), BF)
        elif 128 * j < QW:
            tile = jnp.where(lane < QW - 128 * j, tile.astype(F32) * HEAD ** (-0.5), tile.astype(F32)).astype(BF)
        tiles.append(tile)
    qk = jnp.concatenate(tiles, 1)
    note(N.qk, qk)
    value = dot(normed_a, held[N.att][:, COL_VX:])[:, SKIP_V:].astype(BF)
    note(N.v, value)
    copies.wait(N.mask)
    mixed = []
    for h in range(HEADS):
        kv = h // REP
        key = qk[:, COL_K + HEAD * kv : COL_K + HEAD * (kv + 1)]
        val = value[:, HEAD * kv : HEAD * (kv + 1)]
        parts = []
        for low, high, keys in blocks_of_rows():
            query = qk[low:high, HEAD * h : HEAD * (h + 1)]
            scores = jnp.where(held[N.mask][low:high, :keys] > 0.5, dot_nt(query, key[:keys]), NEG)
            row_max = jnp.max(scores, -1, keepdims=True)
            terms = jnp.exp(scores - row_max)
            total = jnp.sum(terms, -1, keepdims=True)
            attend = (terms * (1.0 / total)).astype(BF)
            parts.append(dot(attend, val[:keys]).astype(BF))
            if kept is not None:
                kept[N.lse][low:high, h : h + 1] = row_max + jnp.log(total)
        mixed.append(jnp.concatenate(parts, 0))
    note(N.lse, None)
    mixed_p = spread(jnp.concatenate(mixed, 1), place)
    note(N.mx, mixed_p)
    middle = stream + dot(mixed_p, held[N.att][:, COL_O : COL_O + D])
    note(N.mid, middle)
    normed_b = spread((middle * inv_rms(middle) * gb_ref[...]).astype(BF), place)
    note(N.nb, normed_b)
    copies.wait(N.gw, N.uw, N.down)
    note(N.laid, None)
    result = middle
    for c in range(0, FF, CHUNK):
        gate = dot(normed_b, held[N.gw][:, c : c + CHUNK])
        up = dot(normed_b, held[N.uw][:, c : c + CHUNK])
        act = (gate * jax.nn.sigmoid(gate) * up).astype(BF)
        result = result + dot(act, down_of(held)[c : c + CHUNK])
        if kept is not None:
            kept[N.gate][:, c : c + CHUNK] = gate
            kept[N.up][:, c : c + CHUNK] = up
            kept[N.act][:, c : c + CHUNK] = act
    note(N.gate, None)
    note(N.up, None)
    note(N.act, None)
    return result.astype(BF)


def down_of(held):
    return held[N.down][...].reshape(FF, D)


def backward(held, kept, copies, ga_ref, gb_ref, note):
    copies.wait(N.g, N.down)
    grad_low = held[N.g][...]
    grad_out = grad_low.astype(F32)
    back_p = jnp.zeros((TOK_MB, PAD), F32)
    down = down_of(held)
    for c in range(0, FF, CHUNK):
        grad_act = dot_nt(grad_low, down[c : c + CHUNK])
        copies.wait(N.gate + str(c), N.up + str(c))
        gate = kept[N.gate][:, c : c + CHUNK]
        up = kept[N.up][:, c : c + CHUNK]
        sig = jax.nn.sigmoid(gate)
        acts = grad_act * sig
        d_gate = (acts * up * (1.0 + gate * (1.0 - sig))).astype(BF)
        d_up = (acts * gate).astype(BF)
        note(N.dg, d_gate, c)
        note(N.du, d_up, c)
        copies.wait(N.gw, N.uw)
        back_p = back_p + dot_nt(d_gate, held[N.gw][:, c : c + CHUNK]) + dot_nt(d_up, held[N.uw][:, c : c + CHUNK])
    copies.wait(N.place, N.mid, N.att)
    place = held[N.place][...]
    back_b, gain_b = norm_back(kept[N.mid][...], gb_ref[...], collect(back_p, place))
    grad_middle = grad_out + back_b
    grad_attn = grad_middle.astype(BF)
    note(N.gattn, grad_attn)
    grad_mixed = dot_nt(dot_nt(grad_attn, held[N.att][:, COL_O : COL_O + D]).astype(BF), place).astype(BF)
    copies.wait(N.qk, N.v, N.lse, N.mask, N.cos, N.sin, N.x)
    d_query, d_key, d_value = [], [], []
    for kv in range(KV_HEADS):
        key = kept[N.qk][:, COL_K + HEAD * kv : COL_K + HEAD * (kv + 1)]
        value = kept[N.v][:, HEAD * kv : HEAD * (kv + 1)]
        sums_k, sums_v = [None, None], [None, None]
        for h in range(kv * REP, (kv + 1) * REP):
            parts = []
            for at, (low, high, keys) in enumerate(blocks_of_rows()):
                query = kept[N.qk][low:high, HEAD * h : HEAD * (h + 1)]
                grad_h = grad_mixed[low:high, HEAD * h : HEAD * (h + 1)]
                scores = jnp.where(held[N.mask][low:high, :keys] > 0.5, dot_nt(query, key[:keys]), NEG)
                attend = jnp.exp(scores - kept[N.lse][low:high, h : h + 1])
                grad_attend = dot_nt(grad_h, value[:keys])
                inner = jnp.sum(attend * grad_attend, -1, keepdims=True)
                grad_scores = (attend * (grad_attend - inner)).astype(BF)
                part_v = dot_tn(attend.astype(BF), grad_h)
                part_k = dot_tn(grad_scores, query)
                sums_v[at] = part_v if sums_v[at] is None else sums_v[at] + part_v
                sums_k[at] = part_k if sums_k[at] is None else sums_k[at] + part_k
                parts.append(dot(grad_scores, key[:keys]) * HEAD ** (-0.5))
            d_query.append(jnp.concatenate(parts, 0))
        d_key.append(jnp.concatenate([sums_k[0] + sums_k[1][:HALF], sums_k[1][HALF:]], 0))
        d_value.append(jnp.concatenate([sums_v[0] + sums_v[1][:HALF], sums_v[1][HALF:]], 0).astype(BF))
    raw = jnp.concatenate(d_query + d_key, 1)
    cosine, sine = held[N.cos][...], held[N.sin][...]
    tiles = []
    for j in range(COL_O // 128):
        tile = raw[:, 128 * j : 128 * (j + 1)]
        tiles.append((tile * cosine - turned(tile) * sine).astype(BF))
    d_qk = jnp.concatenate(tiles, 1)
    d_v = jnp.concatenate([jnp.zeros((TOK_MB, SKIP_V), BF)] + d_value, 1)
    note(N.dqk, d_qk)
    note(N.dv, d_v)
    back_p = dot_nt(d_qk, held[N.att][:, :COL_O]) + dot_nt(d_v, held[N.att][:, COL_VX:])
    back_a, gain_a = norm_back(held[N.x][...].astype(F32), ga_ref[...], collect(back_p, place))
    return (grad_middle + back_a).astype(BF), gain_a, gain_b


SLOTS = dict(
    lead=(N.forward,),
    both=(N.forward, N.backward, N.store),
    ahead=(N.forward, N.store),
    behind=(N.backward, N.keep),
)


def layer_kernel(name, micro, names, refs):
    does = SLOTS[name]
    ref = dict(zip(names, refs))
    held = {key: ref["held_" + key] for key in HELD if "held_" + key in ref}
    kept = {key: ref["kept_" + key] for key in STORED if "kept_" + key in ref} or None
    section = ref[N.coords][3]
    index = {N.zero: 0, N.one: 1, N.same: section, N.other: 1 - section}[micro]
    copies = Copies(ref[N.sems])

    def bring(key):
        copies.start(key, ref[key].at[index], held[key])

    def bring_x():
        if N.arrived in ref:
            copies.start_either(N.x, section == 0, ref[N.tokens].at[index], ref[N.arrived], held[N.x])
        else:
            copies.start(N.x, ref[N.tokens].at[index], held[N.x])

    def bring_weights(order):
        for key in order:
            if key == N.down:
                if N.down in ref:
                    copies.start(key, ref[N.down], held[N.down])
                    continue
                own_z, own_x, own_c = (ref[N.coords][i] for i in range(3))
                for at in range(GROUPS // 2):
                    chip = lax.bitwise_xor(own_z, at // 2) * 2 + lax.bitwise_xor(own_x, at % 2)
                    copies.start(key, ref[N.c_own].at[at], held[N.down].at[chip * 2 + own_c])
                    copies.start(key, ref[N.c_other].at[at], held[N.down].at[chip * 2 + 1 - own_c])
            elif key == N.place:
                copies.start(key, ref[N.place], held[N.place])
            else:
                copies.start(key, ref[N.agu].at[(N.att, N.gw, N.uw).index(key)], held[key])

    def bring_g():
        if N.arrived_grad in ref:
            copies.start_either(N.g, section == 0, ref[N.arrived_grad], ref[N.out_grad].at[index], held[N.g])
        else:
            copies.start(N.g, ref[N.out_grad].at[index], held[N.g])

    if N.forward in does:
        bring_x()
        bring_weights([N.place, N.att])
        bring(N.cos)
        bring(N.sin)
        bring(N.mask)
        bring_weights([N.gw, N.uw, N.down])
        if N.backward in does:
            bring_g()
    else:
        bring_g()
        bring_weights([N.down])
        for c in range(0, FF, CHUNK):
            for key in (N.gate, N.up):
                copies.start(key + str(c), ref["stored_" + key].at[:, c : c + CHUNK], kept[key].at[:, c : c + CHUNK])
        bring_weights([N.gw, N.uw, N.place])
        copies.start(N.mid, ref[N.stored_mid], kept[N.mid])
        bring_weights([N.att])
        for key in (N.qk, N.v, N.lse):
            copies.start(key, ref["stored_" + key], kept[key])
        bring(N.mask)
        bring(N.cos)
        bring(N.sin)
        bring_x()

    def note_stored(key, value, column=None):
        if key == N.laid:
            if N.laid in ref:
                copies.start(N.laid, held[N.down], ref[N.laid])
            return
        if N.store in does:
            if value is not None:
                kept[key][...] = value
            copies.start("out_" + key, kept[key], ref["store_" + key])

    def note_kept(key, value, column=None):
        if N.keep in does:
            if column is None:
                ref["made_" + key][...] = value
            else:
                ref["made_" + key][:, column : column + CHUNK] = value
            if column in (None, FF - CHUNK):
                copies.start("out_" + key, ref["made_" + key], ref["keep_" + key])

    if N.forward in does:
        ref[N.out][...] = forward(held, kept, copies, ref[N.ga], ref[N.gb], note_stored)
    if N.backward in does:
        grad, gain_a, gain_b = backward(held, kept, copies, ref[N.ga], ref[N.gb], note_kept)
        ref[N.in_grad][...] = grad
        if N.keep in does:
            ref[N.gains][0:1, :] = gain_a
            ref[N.gains][1:2, :] = gain_b
    copies.wait_all()


def run_layer(name, micro, common, tokens, arrived=None, out_grad=None, arrived_grad=None, stored=None):
    does = SLOTS[name]
    operands = dict(coords=common[N.coords], tokens=tokens, ga=common[N.ga], gb=common[N.gb])
    operands.update({key: common[key] for key in INPUTS if key in common})
    specs = dict(coords=SMEM, ga=VMEM, gb=VMEM)
    if arrived is not None:
        operands[N.arrived] = arrived
    if N.backward in does:
        operands[N.out_grad] = out_grad
        if arrived_grad is not None:
            operands[N.arrived_grad] = arrived_grad
    if stored is not None:
        operands.update({"stored_" + key: stored[key] for key in FOR_BACK})
    outs, out_specs = {}, []
    if N.forward in does:
        outs[N.out] = shape(TOK_MB, D)
    if N.down not in common:
        outs[N.laid] = INPUTS[N.down]
    if N.backward in does:
        outs[N.in_grad] = shape(TOK_MB, D)
    if N.keep in does:
        outs[N.gains] = shape(2, D, dtype=F32)
        outs.update({"keep_" + key: KEPT[key] for key in KEPT})
    if N.store in does:
        outs.update({"store_" + key: STORED[key] for key in STORED})
    out_specs = [ANY if key.startswith(("store_", "keep_", "laid")) else VMEM for key in outs]
    scratch = {"held_" + key: pltpu.VMEM(h.shape, h.dtype) for key, h in HELD.items() if key != N.g or N.backward in does}
    if name != N.lead:
        hold = STORED if N.forward in does else FOR_BACK
        scratch.update({"kept_" + key: pltpu.VMEM(STORED[key].shape, STORED[key].dtype) for key in hold})
    if N.keep in does:
        scratch.update({"made_" + key: pltpu.VMEM(KEPT[key].shape, BF) for key in KEPT})
    scratch[N.sems] = pltpu.SemaphoreType.DMA((28 if N.down in common else 44,))
    names = list(operands) + list(outs) + list(scratch)

    def kernel(*refs):
        layer_kernel(name, micro, names, refs)

    results = pl.pallas_call(
        kernel,
        out_shape=list(outs.values()),
        in_specs=[specs.get(key, ANY) for key in operands],
        out_specs=out_specs,
        scratch_shapes=list(scratch.values()),
        compiler_params=PARAMS,
        name="layer_" + name,
    )(*operands.values())
    return dict(zip(outs, results))


PAIRS = (N.act, N.g, N.nb, N.dg, N.du, N.mx, N.gattn, N.na, N.dqk, N.dv)


def slab_of(block):
    return jnp.concatenate(
        [
            jnp.concatenate([block[8 * i : 8 * i + 8, 128 * j : 128 * j + 128] for i in range(EACH_FF // 8)], 1)
            for j in range(PAD // 128)
        ],
        0,
    )


def block_of(slab):
    tiles = slab.reshape(slab.shape[:-2] + (PAD // 128, 8, EACH_FF // 8, 128))
    return jnp.moveaxis(tiles, -2, -4).swapaxes(-3, -2).reshape(slab.shape[:-2] + (EACH_FF, PAD))


def weights_kernel(names, refs):
    ref = dict(zip(names, refs))
    copies = Copies(ref[N.sems])
    own_z, own_x, own_c, section = (ref[N.coords][i] for i in range(4))
    for key in PAIRS:
        for at in range(2):
            target = ref["in_" + key].at[pl.ds(TOK_MB * at, TOK_MB)]
            if key == N.g:
                copies.start_either(
                    key, section == 0, ref["grad_%d" % at], ref[N.out_grad].at[section if at == 0 else 1 - section], target
                )
            else:
                copies.start(key, ref["%s_%d" % (key, at)], target)

    def put_pairs(keep_ref, send_ref, at, columns, blocks, pair):
        for one, two in zip(blocks[::2], blocks[1::2]):
            far, across = lax.bitwise_xor(own_z, pair // 2), lax.bitwise_xor(own_x, pair % 2)
            index = (across, far) + at + (slice(None), columns)
            keep_ref[index] = jnp.where(own_c == 0, one, two).astype(BF)
            send_ref[index] = jnp.where(own_c == 0, two, one).astype(BF)
            pair += 1

    def put(keep_ref, send_ref, at, columns, rows):
        put_pairs(keep_ref, send_ref, at, columns, jnp.split(rows, GROUPS), 0)

    copies.wait(N.act, N.g)
    grad_down = jnp.concatenate([ref[N.in_g][...], jnp.zeros((2 * TOK_MB, PAD - D), BF)], 1)
    step = 4 * EACH_FF
    for c in range(0, FF, step):
        slabs = [slab_of(piece) for piece in jnp.split(dot_tn(ref[N.in_act][:, c : c + step], grad_down), 4)]
        put_pairs(ref[N.keep_m], ref[N.send_m], (3,), slice(0, FF), slabs, c // step * 2)
    copies.wait(N.nb, N.dg, N.du)
    normed_b = ref[N.in_nb][...]
    for at, key in ((1, N.dg), (2, N.du)):
        for c in range(0, FF, CHUNK):
            put(ref[N.keep_m], ref[N.send_m], (at,), slice(c, c + CHUNK), dot_tn(normed_b, ref["in_" + key][:, c : c + CHUNK]))
    copies.wait(N.mx, N.gattn, N.na, N.dqk, N.dv)
    normed_a, mixed = ref[N.in_na][...], ref[N.in_mx][...]
    put(ref[N.keep_m], ref[N.send_m], (0,), slice(0, COL_O), dot_tn(normed_a, ref[N.in_dqk][...]))
    put(ref[N.keep_m], ref[N.send_m], (0,), slice(COL_O, COL_VX), dot_tn(mixed, ref[N.in_gattn][:, : COL_VX - COL_O]))
    grad_o = dot_tn(mixed, ref[N.in_gattn][:, COL_VX - COL_O :])
    grad_o = jnp.concatenate([grad_o, jnp.zeros((PAD, KVW), F32)], 1)
    put(ref[N.keep_m], ref[N.send_m], (0,), slice(COL_VX, FF), dot_tn(normed_a, ref[N.in_dv][...]) + grad_o)
    copies.start(N.out, ref[N.send_m], ref[N.out_send_m])
    copies.start(N.out, ref[N.keep_m], ref[N.out_keep_m])
    copies.wait_all()


def run_weights(coords, rows, grads, out_grad):
    operands = dict(coords=coords, out_grad=out_grad)
    for at in range(2):
        operands["grad_%d" % at] = grads[at]
        operands.update({"%s_%d" % (key, at): rows[at][key] for key in PAIRS if key != N.g})
    main = shape(2, 4, 4, EACH, FF)
    outs = dict(out_keep_m=main, out_send_m=main)
    columns = {key: (STORED | KEPT | {N.g: HELD[N.g]})[key].shape[1] for key in PAIRS}
    scratch = {"in_" + key: pltpu.VMEM((2 * TOK_MB, columns[key]), BF) for key in PAIRS}
    scratch.update({key[4:]: pltpu.VMEM(out.shape, BF) for key, out in outs.items()})
    scratch[N.sems] = pltpu.SemaphoreType.DMA((24,))
    names = list(operands) + list(outs) + list(scratch)

    def kernel(*refs):
        weights_kernel(names, refs)

    results = pl.pallas_call(
        kernel,
        out_shape=list(outs.values()),
        in_specs=[SMEM] + [ANY] * (len(operands) - 1),
        out_specs=[ANY] * len(outs),
        scratch_shapes=list(scratch.values()),
        compiler_params=PARAMS,
        name=N.weight_grads,
    )(*operands.values())
    return dict(zip(outs, results))


def make_tables(seg_row):
    count_t = seg_row.shape[0]
    order_idx = jnp.arange(count_t, dtype=jnp.int32)
    same_doc = seg_row[:, None] == seg_row[None, :]
    before = order_idx[None, :] < order_idx[:, None]
    positions = jnp.sum(jnp.where(same_doc & before, jnp.float32(1.0), jnp.float32(0.0)), axis=1)
    allowed = same_doc & (order_idx[None, :] <= order_idx[:, None])
    inv_freq = jnp.exp(jnp.arange(HEAD // 2, dtype=jnp.float32) * (-2.0 * math.log(THETA) / HEAD))
    angles = positions[:, None] * inv_freq[None, :]
    cosine, sine = jnp.cos(angles), jnp.sin(angles)
    cosine = jnp.concatenate([cosine] * 4, -1)
    sine = jnp.concatenate([-sine, sine] * 2, -1)
    return (cosine, sine, allowed.astype(F32))


def placement(rows_each, rows_padded):
    row = lax.broadcasted_iota(jnp.int32, (D, PAD), 0)
    col = lax.broadcasted_iota(jnp.int32, (D, PAD), 1)
    return (col == row + (row // rows_each) * (rows_padded - rows_each)).astype(BF)


def place_of(z, x, c):
    return (z * 2 + x) * 2 + c


PLACES = [(z, x, c) for z in range(4) for x in range(2) for c in range(2)]


def moved(value, dz, dx, dc):
    return lax.ppermute(value, "dp", [(place_of(z, x, c), place_of(z ^ dz, x ^ dx, c ^ dc)) for z, x, c in PLACES])


def gather_weights(shard, owners):
    w_query, w_key, w_value, w_out, w_gate, w_up, w_down = shard
    if owners == GROUPS:
        rows = D // owners
        att = jnp.concatenate(
            [w_query.reshape(rows, QW), w_key.reshape(rows, KVW), w_out.reshape(rows, D), w_value.reshape(rows, KVW)], 1
        )
        packed = jnp.stack([att, w_gate.reshape(rows, FF), w_up.reshape(rows, FF)])
        packed = jnp.pad(packed, ((0, 0), (0, EACH - rows), (0, 0)))
        agu = lax.all_gather(packed, "dp", axis=1, tiled=True)
        w_down = w_down.reshape(EACH_FF, D)
        lines = [w_down] + [moved(w_down, dz, 0, 0) for dz in (1, 2, 3)]
        c_own = jnp.stack([block for line in lines for block in (line, moved(line, 0, 1, 0))])
        return agu, c_own, moved(c_own, 0, 0, 1), placement(rows, EACH)
    w_query, w_key, w_value, w_out, w_gate, w_up, w_down = (
        lax.all_gather(member[0], "dp", axis=0, tiled=True) for member in shard
    )
    att = jnp.concatenate(
        [w_query.reshape(D, QW), w_key.reshape(D, KVW), w_out.reshape(QW, D), w_value.reshape(D, KVW)], 1
    )
    agu = jnp.pad(jnp.stack([att, w_gate.reshape(D, FF), w_up.reshape(D, FF)]), ((0, 0), (0, PAD - D), (0, 0)))
    down = w_down.reshape(GROUPS // 2, 2, EACH_FF, D)
    return agu, down[:, 0], down[:, 1], placement(D, D)


def cut(att):
    return att[:, :QW], att[:, COL_K:COL_O], att[:, COL_V:], att[:, COL_O:COL_V]


def add(*terms):
    return sum(term.astype(F32) for term in terms)


def sum_of_four(value, others):
    return (value + others[0]) + (others[1] + others[2])


def reduce_blocks(keep, send, gains):
    near = [moved(gains, 0, 0, 1), moved(gains, 0, 1, 0), moved(gains, 0, 1, 1)]
    got = moved(send, 0, 0, 1)
    got, near = lax.optimization_barrier((got, near))
    gains = sum_of_four(gains, near)
    wide = [moved(gains, 1, 0, 0), moved(gains, 2, 0, 0), moved(gains, 3, 0, 0)]
    blocks = [add(keep[1, far], got[1, far]).astype(BF) for far in range(4)]
    across_three, across_two = moved(blocks[3], 0, 1, 0), moved(blocks[2], 0, 1, 0)
    across_three, wide = lax.optimization_barrier((across_three, wide))
    gains = sum_of_four(gains, wide)
    three = add(keep[0, 3], got[0, 3], across_three).astype(BF)
    three, last_one = lax.optimization_barrier((three, blocks[1]))
    beside_three, across_one = moved(three, 1, 0, 0), moved(last_one, 0, 1, 0)
    across_two, last_zero = lax.optimization_barrier((across_two, blocks[0]))
    across_zero = moved(last_zero, 0, 1, 0)
    far_two = moved(add(keep[0, 2], got[0, 2], across_two, beside_three).astype(BF), 2, 0, 0)
    beside_one = moved(add(keep[0, 1], got[0, 1], across_one).astype(BF), 1, 0, 0)
    return add(keep[0, 0], got[0, 0], across_zero, far_two, beside_one), gains


def scatter_grads(out, gains, owners):
    if owners == GROUPS:
        main, gains = reduce_blocks(out[N.out_keep_m], out[N.out_send_m], gains)
        rows = D // owners
        att, gate, up = main[0, :rows], main[1, :rows], main[2, :rows]
        down = block_of(main[3])[:, :D]
        return tuple(piece.reshape(1, -1) for piece in cut(att) + (gate, up, down)) + (gains[0:1], gains[1:2])
    main = jnp.stack([out[N.out_keep_m], out[N.out_send_m]]).transpose(3, 2, 1, 0, 4, 5).reshape(4, GROUPS, EACH, FF)
    down = block_of(main[3])[:, :, :D].reshape(FF, D)
    main = main[:3].reshape(3, PAD, FF)[:, :D]
    pieces = cut(main[0]) + (main[1], main[2], down)
    gains = lax.psum(gains, "dp")
    return tuple(
        lax.psum_scatter(piece.reshape(owners, -1), "dp", scatter_dimension=0, tiled=True).astype(F32) for piece in pieces
    ) + (gains[0:1], gains[1:2])


def shards(
    tokens,
    segments,
    w_query,
    w_key,
    w_value,
    w_out,
    w_gate,
    w_up,
    w_down,
    attn_gain,
    mlp_gain,
    out_grad,
):
    section = lax.axis_index("section")
    first = section == 0
    owners = lax.axis_size("dp")
    me = lax.axis_index("dp") if owners == GROUPS else 0
    coords = jnp.stack([me // 4, me // 2 % 2, me % 2, section, 0, 0, 0, 0]).astype(jnp.int32)
    agu, c_own, c_other, place = gather_weights((w_query, w_key, w_value, w_out, w_gate, w_up, w_down), owners)
    cosine, sine, mask = jax.vmap(make_tables)(segments[:, 0])
    agu, c_own, c_other, place, cosine, sine, mask, tokens, out_grad, coords = lax.optimization_barrier(
        (agu, c_own, c_other, place, cosine, sine, mask, tokens, out_grad, coords)
    )
    common = dict(
        agu=agu, c_own=c_own, c_other=c_other, place=place, cos=cosine, sin=sine, mask=mask, coords=coords, ga=attn_gain, gb=mlp_gain
    )

    def send_on(block):
        return lax.ppermute(block, "section", [(0, 1)])

    def send_back(block):
        return lax.ppermute(block, "section", [(1, 0)])

    def stored_of(outs):
        return {key: outs["store_" + key] for key in STORED}

    def rows_of(stored, outs):
        return stored | {key: outs["keep_" + key] for key in KEPT}

    first_out = run_layer(N.lead, N.zero, common, tokens)
    lead_zero = first_out[N.out]
    common = {key: common[key] for key in common if key not in (N.c_own, N.c_other)} | {N.down: first_out[N.laid]}
    arrived_zero = send_on(lead_zero)
    lead_one = run_layer(N.lead, N.one, common, tokens)[N.out]
    arrived_one = send_on(lead_one)
    two = run_layer(N.both, N.other, common, tokens, arrived_zero, out_grad)
    arrived_grad = send_back(two[N.in_grad])
    four = run_layer(N.ahead, N.same, common, tokens, arrived_one)
    stored_two, stored_four = stored_of(two), stored_of(four)
    five = run_layer(N.behind, N.same, common, tokens, arrived_one, out_grad, arrived_grad, stored_four)
    last_grad = send_back(five[N.in_grad])
    six = run_layer(N.behind, N.other, common, tokens, arrived_zero, out_grad, last_grad, stored_two)
    grads = run_weights(
        coords, (rows_of(stored_four, five), rows_of(stored_two, six)), (arrived_grad, last_grad), out_grad
    )
    shares = scatter_grads(grads, five[N.gains] + six[N.gains], owners)
    layer_out = jnp.stack([jnp.where(first, four[N.out], two[N.out]), jnp.where(first, two[N.out], four[N.out])])
    input_grad = jnp.stack([jnp.where(first, five[N.in_grad], six[N.in_grad]), jnp.where(first, six[N.in_grad], five[N.in_grad])])
    return (layer_out[None], input_grad[None], *shares)


def solution(mesh):
    weights = (P("section", "dp"),) * 7
    gains = (P("section", None),) * 2
    rows = P("section", None, "dp", None)
    return jax.shard_map(
        shards,
        mesh=mesh,
        in_specs=(P(None, "dp", None), P(None, "dp", None), *weights, *gains, P(None, "dp", None)),
        out_specs=(rows, rows, *weights, *gains),
        check_vma=False,
    )
```

```python
import functools
import math

import jax
import jax.numpy as jnp
from jax import lax
from jax.experimental import pallas as pl
from jax.experimental.pallas import tpu as pltpu
from jax.sharding import PartitionSpec as P

D = 576
HEADS = 9
KV_HEADS = 3
HEAD = 64
FF = 1536
TOK_MB = 256
QW = HEADS * HEAD
KVW = KV_HEADS * HEAD
REP = HEADS // KV_HEADS

EPS = 1e-05
THETA = 100000.0
NEG = -1000000000.0

PAD = 640
COL_K = QW
COL_O = QW + KVW
COL_V = COL_O + D
COL_VX = 1280
SKIP_V = COL_V - COL_VX

BF = jnp.bfloat16
F32 = jnp.float32

PARAMS = pltpu.CompilerParams(vmem_limit_bytes=60 * 1024 * 1024)


def dot(left, right):
    return lax.dot_general(left, right, (((1,), (0,)), ((), ())), preferred_element_type=F32)


def dot_nt(left, right):
    return lax.dot_general(left, right, (((1,), (1,)), ((), ())), preferred_element_type=F32)


def dot_tn(left, right):
    return lax.dot_general(left, right, (((0,), (0,)), ((), ())), preferred_element_type=F32)


def spread(rows, place):
    return dot(rows, place).astype(BF)


def collect(rows, place):
    high = rows.astype(BF)
    low = (rows - high.astype(F32)).astype(BF)
    return dot_nt(high, place) + dot_nt(low, place)


def turned(tile):
    lane = lax.broadcasted_iota(jnp.int32, tile.shape, 1)
    return jnp.where(lane % HEAD < HEAD // 2, pltpu.roll(tile, 128 - HEAD // 2, 1), pltpu.roll(tile, HEAD // 2, 1))


def inv_rms(stream):
    return lax.rsqrt(jnp.mean(stream * stream, -1, keepdims=True) + EPS)


def norm_back(stream, gain_row, grad_normed):
    scale_r = inv_rms(stream)
    weighted = grad_normed * gain_row
    grad_stream = scale_r * weighted - stream * scale_r**3 * jnp.mean(
        stream * weighted, -1, keepdims=True
    )
    grad_gain = jnp.sum(grad_normed * stream * scale_r, 0, keepdims=True)
    return (grad_stream, grad_gain)


CHUNK = 768
CHUNKS = FF // CHUNK
HALF = TOK_MB // 2
GROUPS = 16
EACH = PAD // GROUPS
EACH_FF = FF // GROUPS
DV = QW + D + 2 * KVW - COL_VX

ANY = pl.BlockSpec(memory_space=pl.ANY)
SMEM = pl.BlockSpec(memory_space=pltpu.SMEM)
VMEM = pl.BlockSpec(memory_space=pltpu.VMEM)


def shape(*dims, dtype=BF):
    return jax.ShapeDtypeStruct(dims, dtype)


class Names:
    def __getattr__(self, name):
        return name


N = Names()


STORED = dict(
    na=shape(TOK_MB, PAD),
    qk=shape(TOK_MB, COL_O),
    v=shape(TOK_MB, KVW),
    lse=shape(TOK_MB, 128, dtype=F32),
    mx=shape(TOK_MB, PAD),
    mid=shape(TOK_MB, D, dtype=F32),
    nb=shape(TOK_MB, PAD),
    gate=shape(TOK_MB, FF, dtype=F32),
    up=shape(TOK_MB, FF, dtype=F32),
    act=shape(TOK_MB, FF),
)
FOR_BACK = (N.gate, N.up, N.mid, N.qk, N.v, N.lse)
KEPT = dict(
    dqk=shape(TOK_MB, COL_O),
    dv=shape(TOK_MB, DV),
    gattn=shape(TOK_MB, D),
    dg=shape(TOK_MB, FF),
    du=shape(TOK_MB, FF),
)
INPUTS = dict(
    agu=shape(3, PAD, FF),
    c_own=shape(GROUPS // 2, EACH_FF, D),
    c_other=shape(GROUPS // 2, EACH_FF, D),
    down=shape(GROUPS, EACH_FF, D),
    place=shape(D, PAD),
    cos=shape(2, TOK_MB, 128, dtype=F32),
    sin=shape(2, TOK_MB, 128, dtype=F32),
    mask=shape(2, TOK_MB, TOK_MB, dtype=F32),
)
HELD = dict(
    att=shape(PAD, FF),
    gw=shape(PAD, FF),
    uw=shape(PAD, FF),
    down=shape(GROUPS, EACH_FF, D),
    place=shape(D, PAD),
    cos=shape(TOK_MB, 128, dtype=F32),
    sin=shape(TOK_MB, 128, dtype=F32),
    mask=shape(TOK_MB, TOK_MB, dtype=F32),
    x=shape(TOK_MB, D),
    g=shape(TOK_MB, D),
)


class Copies:
    def __init__(self, sems):
        self.sems, self.count, self.open = sems, 0, {}

    def start(self, name, source, target):
        copy = pltpu.make_async_copy(source, target, self.sems.at[self.count])
        self.count += 1
        self.open.setdefault(name, []).append(copy)
        copy.start()

    def start_either(self, name, take_one, one, two, target):
        first = pltpu.make_async_copy(one, target, self.sems.at[self.count])
        second = pltpu.make_async_copy(two, target, self.sems.at[self.count])
        self.count += 1
        self.open.setdefault(name, []).append(first)

        @pl.when(take_one)
        def _():
            first.start()

        @pl.when(jnp.logical_not(take_one))
        def _():
            second.start()

    def wait(self, *names):
        for name in names:
            for copy in self.open.pop(name, ()):
                copy.wait()

    def wait_all(self):
        self.wait(*list(self.open))


def blocks_of_rows():
    return ((0, HALF, HALF), (HALF, TOK_MB, TOK_MB))


def forward(held, kept, copies, ga_ref, gb_ref, note):
    copies.wait(N.x, N.place)
    place = held[N.place][...]
    stream = held[N.x][...].astype(F32)
    normed_a = spread((stream * inv_rms(stream) * ga_ref[...]).astype(BF), place)
    note(N.na, normed_a)
    copies.wait(N.att, N.cos, N.sin)
    raw = dot(normed_a, held[N.att][:, :COL_O])
    cosine, sine = held[N.cos][...], held[N.sin][...]
    tiles = []
    lane = lax.broadcasted_iota(jnp.int32, (TOK_MB, 128), 1)
    for j in range(COL_O // 128):
        tile = raw[:, 128 * j : 128 * (j + 1)]
        tile = (tile * cosine + turned(tile) * sine).astype(BF)
        if 128 * (j + 1) <= QW:
            tile = tile * jnp.asarray(HEAD ** (-0.5), BF)
        elif 128 * j < QW:
            tile = jnp.where(lane < QW - 128 * j, tile.astype(F32) * HEAD ** (-0.5), tile.astype(F32)).astype(BF)
        tiles.append(tile)
    qk = jnp.concatenate(tiles, 1)
    note(N.qk, qk)
    value = dot(normed_a, held[N.att][:, COL_VX:])[:, SKIP_V:].astype(BF)
    note(N.v, value)
    copies.wait(N.mask)
    mixed = []
    for h in range(HEADS):
        kv = h // REP
        key = qk[:, COL_K + HEAD * kv : COL_K + HEAD * (kv + 1)]
        val = value[:, HEAD * kv : HEAD * (kv + 1)]
        parts = []
        for low, high, keys in blocks_of_rows():
            query = qk[low:high, HEAD * h : HEAD * (h + 1)]
            scores = jnp.where(held[N.mask][low:high, :keys] > 0.5, dot_nt(query, key[:keys]), NEG)
            row_max = jnp.max(scores, -1, keepdims=True)
            terms = jnp.exp(scores - row_max)
            total = jnp.sum(terms, -1, keepdims=True)
            attend = (terms * (1.0 / total)).astype(BF)
            parts.append(dot(attend, val[:keys]).astype(BF))
            if kept is not None:
                kept[N.lse][low:high, h : h + 1] = row_max + jnp.log(total)
        mixed.append(jnp.concatenate(parts, 0))
    note(N.lse, None)
    mixed_p = spread(jnp.concatenate(mixed, 1), place)
    note(N.mx, mixed_p)
    middle = stream + dot(mixed_p, held[N.att][:, COL_O : COL_O + D])
    note(N.mid, middle)
    normed_b = spread((middle * inv_rms(middle) * gb_ref[...]).astype(BF), place)
    note(N.nb, normed_b)
    copies.wait(N.gw, N.uw, N.down)
    note(N.laid, None)
    result = middle
    for c in range(0, FF, CHUNK):
        gate = dot(normed_b, held[N.gw][:, c : c + CHUNK])
        up = dot(normed_b, held[N.uw][:, c : c + CHUNK])
        act = (gate * jax.nn.sigmoid(gate) * up).astype(BF)
        result = result + dot(act, down_of(held)[c : c + CHUNK])
        if kept is not None:
            kept[N.gate][:, c : c + CHUNK] = gate
            kept[N.up][:, c : c + CHUNK] = up
            kept[N.act][:, c : c + CHUNK] = act
    note(N.gate, None)
    note(N.up, None)
    note(N.act, None)
    return result.astype(BF)


def down_of(held):
    return held[N.down][...].reshape(FF, D)


def backward(held, kept, copies, ga_ref, gb_ref, note):
    copies.wait(N.g, N.down)
    grad_low = held[N.g][...]
    grad_out = grad_low.astype(F32)
    back_p = jnp.zeros((TOK_MB, PAD), F32)
    down = down_of(held)
    for c in range(0, FF, CHUNK):
        grad_act = dot_nt(grad_low, down[c : c + CHUNK])
        copies.wait(N.gate + str(c), N.up + str(c))
        gate = kept[N.gate][:, c : c + CHUNK]
        up = kept[N.up][:, c : c + CHUNK]
        sig = jax.nn.sigmoid(gate)
        acts = grad_act * sig
        d_gate = (acts * up * (1.0 + gate * (1.0 - sig))).astype(BF)
        d_up = (acts * gate).astype(BF)
        note(N.dg, d_gate, c)
        note(N.du, d_up, c)
        copies.wait(N.gw, N.uw)
        back_p = back_p + dot_nt(d_gate, held[N.gw][:, c : c + CHUNK]) + dot_nt(d_up, held[N.uw][:, c : c + CHUNK])
    copies.wait(N.place, N.mid, N.att)
    place = held[N.place][...]
    back_b, gain_b = norm_back(kept[N.mid][...], gb_ref[...], collect(back_p, place))
    grad_middle = grad_out + back_b
    grad_attn = grad_middle.astype(BF)
    note(N.gattn, grad_attn)
    grad_mixed = dot_nt(dot_nt(grad_attn, held[N.att][:, COL_O : COL_O + D]).astype(BF), place).astype(BF)
    copies.wait(N.qk, N.v, N.lse, N.mask, N.cos, N.sin, N.x)
    d_query, d_key, d_value = [], [], []
    for kv in range(KV_HEADS):
        key = kept[N.qk][:, COL_K + HEAD * kv : COL_K + HEAD * (kv + 1)]
        value = kept[N.v][:, HEAD * kv : HEAD * (kv + 1)]
        sums_k, sums_v = [None, None], [None, None]
        for h in range(kv * REP, (kv + 1) * REP):
            parts = []
            for at, (low, high, keys) in enumerate(blocks_of_rows()):
                query = kept[N.qk][low:high, HEAD * h : HEAD * (h + 1)]
                grad_h = grad_mixed[low:high, HEAD * h : HEAD * (h + 1)]
                scores = jnp.where(held[N.mask][low:high, :keys] > 0.5, dot_nt(query, key[:keys]), NEG)
                attend = jnp.exp(scores - kept[N.lse][low:high, h : h + 1])
                grad_attend = dot_nt(grad_h, value[:keys])
                inner = jnp.sum(attend * grad_attend, -1, keepdims=True)
                grad_scores = (attend * (grad_attend - inner)).astype(BF)
                part_v = dot_tn(attend.astype(BF), grad_h)
                part_k = dot_tn(grad_scores, query)
                sums_v[at] = part_v if sums_v[at] is None else sums_v[at] + part_v
                sums_k[at] = part_k if sums_k[at] is None else sums_k[at] + part_k
                parts.append(dot(grad_scores, key[:keys]) * HEAD ** (-0.5))
            d_query.append(jnp.concatenate(parts, 0))
        d_key.append(jnp.concatenate([sums_k[0] + sums_k[1][:HALF], sums_k[1][HALF:]], 0))
        d_value.append(jnp.concatenate([sums_v[0] + sums_v[1][:HALF], sums_v[1][HALF:]], 0).astype(BF))
    raw = jnp.concatenate(d_query + d_key, 1)
    cosine, sine = held[N.cos][...], held[N.sin][...]
    tiles = []
    for j in range(COL_O // 128):
        tile = raw[:, 128 * j : 128 * (j + 1)]
        tiles.append((tile * cosine - turned(tile) * sine).astype(BF))
    d_qk = jnp.concatenate(tiles, 1)
    d_v = jnp.concatenate([jnp.zeros((TOK_MB, SKIP_V), BF)] + d_value, 1)
    note(N.dqk, d_qk)
    note(N.dv, d_v)
    back_p = dot_nt(d_qk, held[N.att][:, :COL_O]) + dot_nt(d_v, held[N.att][:, COL_VX:])
    back_a, gain_a = norm_back(held[N.x][...].astype(F32), ga_ref[...], collect(back_p, place))
    return (grad_middle + back_a).astype(BF), gain_a, gain_b


SLOTS = dict(
    lead=(N.forward,),
    both=(N.forward, N.backward, N.store),
    ahead=(N.forward, N.store),
    behind=(N.backward, N.keep),
)


def layer_kernel(name, micro, names, refs):
    does = SLOTS[name]
    ref = dict(zip(names, refs))
    held = {key: ref["held_" + key] for key in HELD if "held_" + key in ref}
    kept = {key: ref["kept_" + key] for key in STORED if "kept_" + key in ref} or None
    section = ref[N.coords][3]
    index = {N.zero: 0, N.one: 1, N.same: section, N.other: 1 - section}[micro]
    copies = Copies(ref[N.sems])

    def bring(key):
        copies.start(key, ref[key].at[index], held[key])

    def bring_x():
        if N.arrived in ref:
            copies.start_either(N.x, section == 0, ref[N.tokens].at[index], ref[N.arrived], held[N.x])
        else:
            copies.start(N.x, ref[N.tokens].at[index], held[N.x])

    def bring_weights(order):
        for key in order:
            if key == N.down:
                if N.down in ref:
                    copies.start(key, ref[N.down], held[N.down])
                    continue
                own_z, own_x, own_c = (ref[N.coords][i] for i in range(3))
                for at in range(GROUPS // 2):
                    chip = lax.bitwise_xor(own_z, at // 2) * 2 + lax.bitwise_xor(own_x, at % 2)
                    copies.start(key, ref[N.c_own].at[at], held[N.down].at[chip * 2 + own_c])
                    copies.start(key, ref[N.c_other].at[at], held[N.down].at[chip * 2 + 1 - own_c])
            elif key == N.place:
                copies.start(key, ref[N.place], held[N.place])
            else:
                copies.start(key, ref[N.agu].at[(N.att, N.gw, N.uw).index(key)], held[key])

    def bring_g():
        if N.arrived_grad in ref:
            copies.start_either(N.g, section == 0, ref[N.arrived_grad], ref[N.out_grad].at[index], held[N.g])
        else:
            copies.start(N.g, ref[N.out_grad].at[index], held[N.g])

    if N.forward in does:
        bring_x()
        bring_weights([N.place, N.att])
        bring(N.cos)
        bring(N.sin)
        bring(N.mask)
        bring_weights([N.gw, N.uw, N.down])
        if N.backward in does:
            bring_g()
    else:
        bring_g()
        bring_weights([N.down])
        for c in range(0, FF, CHUNK):
            for key in (N.gate, N.up):
                copies.start(key + str(c), ref["stored_" + key].at[:, c : c + CHUNK], kept[key].at[:, c : c + CHUNK])
        bring_weights([N.gw, N.uw, N.place])
        copies.start(N.mid, ref[N.stored_mid], kept[N.mid])
        bring_weights([N.att])
        for key in (N.qk, N.v, N.lse):
            copies.start(key, ref["stored_" + key], kept[key])
        bring(N.mask)
        bring(N.cos)
        bring(N.sin)
        bring_x()

    def note_stored(key, value, column=None):
        if key == N.laid:
            if N.laid in ref:
                copies.start(N.laid, held[N.down], ref[N.laid])
            return
        if N.store in does:
            if value is not None:
                kept[key][...] = value
            copies.start("out_" + key, kept[key], ref["store_" + key])

    def note_kept(key, value, column=None):
        if N.keep in does:
            if column is None:
                ref["made_" + key][...] = value
            else:
                ref["made_" + key][:, column : column + CHUNK] = value
            if column in (None, FF - CHUNK):
                copies.start("out_" + key, ref["made_" + key], ref["keep_" + key])

    if N.forward in does:
        ref[N.out][...] = forward(held, kept, copies, ref[N.ga], ref[N.gb], note_stored)
    if N.backward in does:
        grad, gain_a, gain_b = backward(held, kept, copies, ref[N.ga], ref[N.gb], note_kept)
        ref[N.in_grad][...] = grad
        if N.keep in does:
            ref[N.gains][0:1, :] = gain_a
            ref[N.gains][1:2, :] = gain_b
    copies.wait_all()


def run_layer(name, micro, common, tokens, arrived=None, out_grad=None, arrived_grad=None, stored=None):
    does = SLOTS[name]
    operands = dict(coords=common[N.coords], tokens=tokens, ga=common[N.ga], gb=common[N.gb])
    operands.update({key: common[key] for key in INPUTS if key in common})
    specs = dict(coords=SMEM, ga=VMEM, gb=VMEM)
    if arrived is not None:
        operands[N.arrived] = arrived
    if N.backward in does:
        operands[N.out_grad] = out_grad
        if arrived_grad is not None:
            operands[N.arrived_grad] = arrived_grad
    if stored is not None:
        operands.update({"stored_" + key: stored[key] for key in FOR_BACK})
    outs, out_specs = {}, []
    if N.forward in does:
        outs[N.out] = shape(TOK_MB, D)
    if N.down not in common:
        outs[N.laid] = INPUTS[N.down]
    if N.backward in does:
        outs[N.in_grad] = shape(TOK_MB, D)
    if N.keep in does:
        outs[N.gains] = shape(2, D, dtype=F32)
        outs.update({"keep_" + key: KEPT[key] for key in KEPT})
    if N.store in does:
        outs.update({"store_" + key: STORED[key] for key in STORED})
    out_specs = [ANY if key.startswith(("store_", "keep_", "laid")) else VMEM for key in outs]
    scratch = {"held_" + key: pltpu.VMEM(h.shape, h.dtype) for key, h in HELD.items() if key != N.g or N.backward in does}
    if name != N.lead:
        hold = STORED if N.forward in does else FOR_BACK
        scratch.update({"kept_" + key: pltpu.VMEM(STORED[key].shape, STORED[key].dtype) for key in hold})
    if N.keep in does:
        scratch.update({"made_" + key: pltpu.VMEM(KEPT[key].shape, BF) for key in KEPT})
    scratch[N.sems] = pltpu.SemaphoreType.DMA((28 if N.down in common else 44,))
    names = list(operands) + list(outs) + list(scratch)

    def kernel(*refs):
        layer_kernel(name, micro, names, refs)

    results = pl.pallas_call(
        kernel,
        out_shape=list(outs.values()),
        in_specs=[specs.get(key, ANY) for key in operands],
        out_specs=out_specs,
        scratch_shapes=list(scratch.values()),
        compiler_params=PARAMS,
        name="layer_" + name,
    )(*operands.values())
    return dict(zip(outs, results))


PAIRS = (N.act, N.g, N.nb, N.dg, N.du, N.mx, N.gattn, N.na, N.dqk, N.dv)


def slab_of(block):
    return jnp.concatenate(
        [
            jnp.concatenate([block[8 * i : 8 * i + 8, 128 * j : 128 * j + 128] for i in range(EACH_FF // 8)], 1)
            for j in range(PAD // 128)
        ],
        0,
    )


def block_of(slab):
    tiles = slab.reshape(slab.shape[:-2] + (PAD // 128, 8, EACH_FF // 8, 128))
    return jnp.moveaxis(tiles, -2, -4).swapaxes(-3, -2).reshape(slab.shape[:-2] + (EACH_FF, PAD))


def weights_kernel(names, refs):
    ref = dict(zip(names, refs))
    copies = Copies(ref[N.sems])
    own_z, own_x, own_c, section = (ref[N.coords][i] for i in range(4))
    for key in PAIRS:
        for at in range(2):
            target = ref["in_" + key].at[pl.ds(TOK_MB * at, TOK_MB)]
            if key == N.g:
                copies.start_either(
                    key, section == 0, ref["grad_%d" % at], ref[N.out_grad].at[section if at == 0 else 1 - section], target
                )
            else:
                copies.start(key, ref["%s_%d" % (key, at)], target)

    def put_pairs(keep_ref, send_ref, at, columns, blocks, pair):
        for one, two in zip(blocks[::2], blocks[1::2]):
            far, across = lax.bitwise_xor(own_z, pair // 2), lax.bitwise_xor(own_x, pair % 2)
            index = (across, far) + at + (slice(None), columns)
            keep_ref[index] = jnp.where(own_c == 0, one, two).astype(BF)
            send_ref[index] = jnp.where(own_c == 0, two, one).astype(BF)
            pair += 1

    def put(keep_ref, send_ref, at, columns, rows):
        put_pairs(keep_ref, send_ref, at, columns, jnp.split(rows, GROUPS), 0)

    copies.wait(N.act, N.g)
    grad_down = jnp.concatenate([ref[N.in_g][...], jnp.zeros((2 * TOK_MB, PAD - D), BF)], 1)
    step = 4 * EACH_FF
    for c in range(0, FF, step):
        slabs = [slab_of(piece) for piece in jnp.split(dot_tn(ref[N.in_act][:, c : c + step], grad_down), 4)]
        put_pairs(ref[N.keep_m], ref[N.send_m], (3,), slice(0, FF), slabs, c // step * 2)
    copies.wait(N.nb, N.dg, N.du)
    normed_b = ref[N.in_nb][...]
    for at, key in ((1, N.dg), (2, N.du)):
        for c in range(0, FF, CHUNK):
            put(ref[N.keep_m], ref[N.send_m], (at,), slice(c, c + CHUNK), dot_tn(normed_b, ref["in_" + key][:, c : c + CHUNK]))
    copies.wait(N.mx, N.gattn, N.na, N.dqk, N.dv)
    normed_a, mixed = ref[N.in_na][...], ref[N.in_mx][...]
    put(ref[N.keep_m], ref[N.send_m], (0,), slice(0, COL_O), dot_tn(normed_a, ref[N.in_dqk][...]))
    put(ref[N.keep_m], ref[N.send_m], (0,), slice(COL_O, COL_VX), dot_tn(mixed, ref[N.in_gattn][:, : COL_VX - COL_O]))
    grad_o = dot_tn(mixed, ref[N.in_gattn][:, COL_VX - COL_O :])
    grad_o = jnp.concatenate([grad_o, jnp.zeros((PAD, KVW), F32)], 1)
    put(ref[N.keep_m], ref[N.send_m], (0,), slice(COL_VX, FF), dot_tn(normed_a, ref[N.in_dv][...]) + grad_o)
    copies.start(N.out, ref[N.send_m], ref[N.out_send_m])
    copies.start(N.out, ref[N.keep_m], ref[N.out_keep_m])
    copies.wait_all()


def run_weights(coords, rows, grads, out_grad):
    operands = dict(coords=coords, out_grad=out_grad)
    for at in range(2):
        operands["grad_%d" % at] = grads[at]
        operands.update({"%s_%d" % (key, at): rows[at][key] for key in PAIRS if key != N.g})
    main = shape(2, 4, 4, EACH, FF)
    outs = dict(out_keep_m=main, out_send_m=main)
    columns = {key: (STORED | KEPT | {N.g: HELD[N.g]})[key].shape[1] for key in PAIRS}
    scratch = {"in_" + key: pltpu.VMEM((2 * TOK_MB, columns[key]), BF) for key in PAIRS}
    scratch.update({key[4:]: pltpu.VMEM(out.shape, BF) for key, out in outs.items()})
    scratch[N.sems] = pltpu.SemaphoreType.DMA((24,))
    names = list(operands) + list(outs) + list(scratch)

    def kernel(*refs):
        weights_kernel(names, refs)

    results = pl.pallas_call(
        kernel,
        out_shape=list(outs.values()),
        in_specs=[SMEM] + [ANY] * (len(operands) - 1),
        out_specs=[ANY] * len(outs),
        scratch_shapes=list(scratch.values()),
        compiler_params=PARAMS,
        name=N.weight_grads,
    )(*operands.values())
    return dict(zip(outs, results))


def make_tables(seg_row):
    count_t = seg_row.shape[0]
    order_idx = jnp.arange(count_t, dtype=jnp.int32)
    same_doc = seg_row[:, None] == seg_row[None, :]
    before = order_idx[None, :] < order_idx[:, None]
    positions = jnp.sum(jnp.where(same_doc & before, jnp.float32(1.0), jnp.float32(0.0)), axis=1)
    allowed = same_doc & (order_idx[None, :] <= order_idx[:, None])
    inv_freq = jnp.exp(jnp.arange(HEAD // 2, dtype=jnp.float32) * (-2.0 * math.log(THETA) / HEAD))
    angles = positions[:, None] * inv_freq[None, :]
    cosine, sine = jnp.cos(angles), jnp.sin(angles)
    cosine = jnp.concatenate([cosine] * 4, -1)
    sine = jnp.concatenate([-sine, sine] * 2, -1)
    return (cosine, sine, allowed.astype(F32))


def placement(rows_each, rows_padded):
    row = lax.broadcasted_iota(jnp.int32, (D, PAD), 0)
    col = lax.broadcasted_iota(jnp.int32, (D, PAD), 1)
    return (col == row + (row // rows_each) * (rows_padded - rows_each)).astype(BF)


def place_of(z, x, c):
    return (z * 2 + x) * 2 + c


PLACES = [(z, x, c) for z in range(4) for x in range(2) for c in range(2)]


def moved(value, dz, dx, dc):
    return lax.ppermute(value, "dp", [(place_of(z, x, c), place_of(z ^ dz, x ^ dx, c ^ dc)) for z, x, c in PLACES])


def gather_weights(shard, owners):
    w_query, w_key, w_value, w_out, w_gate, w_up, w_down = shard
    if owners == GROUPS:
        rows = D // owners
        att = jnp.concatenate(
            [w_query.reshape(rows, QW), w_key.reshape(rows, KVW), w_out.reshape(rows, D), w_value.reshape(rows, KVW)], 1
        )
        packed = jnp.stack([att, w_gate.reshape(rows, FF), w_up.reshape(rows, FF)])
        packed = jnp.pad(packed, ((0, 0), (0, EACH - rows), (0, 0)))
        agu = lax.all_gather(packed, "dp", axis=1, tiled=True)
        w_down = w_down.reshape(EACH_FF, D)
        lines = [w_down] + [moved(w_down, dz, 0, 0) for dz in (1, 2, 3)]
        c_own = jnp.stack([block for line in lines for block in (line, moved(line, 0, 1, 0))])
        c_other = moved(c_own, 0, 0, 1)
        c_own, c_other, corner = lax.optimization_barrier((c_own, c_other, w_down[:8, :128]))
        met = lax.all_gather(corner, "dp", axis=0, tiled=False)
        corner = lax.dynamic_index_in_dim(met, lax.axis_index("dp"), 0, keepdims=False)
        c_own = c_own.at[0, :8, :128].set(corner)
        return agu, c_own, c_other, placement(rows, EACH)
    w_query, w_key, w_value, w_out, w_gate, w_up, w_down = (
        lax.all_gather(member[0], "dp", axis=0, tiled=True) for member in shard
    )
    att = jnp.concatenate(
        [w_query.reshape(D, QW), w_key.reshape(D, KVW), w_out.reshape(QW, D), w_value.reshape(D, KVW)], 1
    )
    agu = jnp.pad(jnp.stack([att, w_gate.reshape(D, FF), w_up.reshape(D, FF)]), ((0, 0), (0, PAD - D), (0, 0)))
    down = w_down.reshape(GROUPS // 2, 2, EACH_FF, D)
    return agu, down[:, 0], down[:, 1], placement(D, D)


def cut(att):
    return att[:, :QW], att[:, COL_K:COL_O], att[:, COL_V:], att[:, COL_O:COL_V]


def add(*terms):
    return sum(term.astype(F32) for term in terms)


def sum_of_four(value, others):
    return (value + others[0]) + (others[1] + others[2])


def reduce_blocks(keep, send, gains):
    near = [moved(gains, 0, 0, 1), moved(gains, 0, 1, 0), moved(gains, 0, 1, 1)]
    got = moved(send, 0, 0, 1)
    got, near = lax.optimization_barrier((got, near))
    gains = sum_of_four(gains, near)
    wide = [moved(gains, 1, 0, 0), moved(gains, 2, 0, 0), moved(gains, 3, 0, 0)]
    blocks = [add(keep[1, far], got[1, far]).astype(BF) for far in range(4)]
    across_three, across_two = moved(blocks[3], 0, 1, 0), moved(blocks[2], 0, 1, 0)
    across_three, wide = lax.optimization_barrier((across_three, wide))
    gains = sum_of_four(gains, wide)
    three = add(keep[0, 3], got[0, 3], across_three).astype(BF)
    three, last_one = lax.optimization_barrier((three, blocks[1]))
    beside_three, across_one = moved(three, 1, 0, 0), moved(last_one, 0, 1, 0)
    across_two, last_zero = lax.optimization_barrier((across_two, blocks[0]))
    across_zero = moved(last_zero, 0, 1, 0)
    far_two = moved(add(keep[0, 2], got[0, 2], across_two, beside_three).astype(BF), 2, 0, 0)
    beside_one = moved(add(keep[0, 1], got[0, 1], across_one).astype(BF), 1, 0, 0)
    return add(keep[0, 0], got[0, 0], across_zero, far_two, beside_one), gains


def scatter_grads(out, gains, owners):
    if owners == GROUPS:
        main, gains = reduce_blocks(out[N.out_keep_m], out[N.out_send_m], gains)
        rows = D // owners
        att, gate, up = main[0, :rows], main[1, :rows], main[2, :rows]
        down = block_of(main[3])[:, :D]
        return tuple(piece.reshape(1, -1) for piece in cut(att) + (gate, up, down)) + (gains[0:1], gains[1:2])
    main = jnp.stack([out[N.out_keep_m], out[N.out_send_m]]).transpose(3, 2, 1, 0, 4, 5).reshape(4, GROUPS, EACH, FF)
    down = block_of(main[3])[:, :, :D].reshape(FF, D)
    main = main[:3].reshape(3, PAD, FF)[:, :D]
    pieces = cut(main[0]) + (main[1], main[2], down)
    gains = lax.psum(gains, "dp")
    return tuple(
        lax.psum_scatter(piece.reshape(owners, -1), "dp", scatter_dimension=0, tiled=True).astype(F32) for piece in pieces
    ) + (gains[0:1], gains[1:2])


def shards(
    tokens,
    segments,
    w_query,
    w_key,
    w_value,
    w_out,
    w_gate,
    w_up,
    w_down,
    attn_gain,
    mlp_gain,
    out_grad,
):
    section = lax.axis_index("section")
    first = section == 0
    owners = lax.axis_size("dp")
    me = lax.axis_index("dp") if owners == GROUPS else 0
    coords = jnp.stack([me // 4, me // 2 % 2, me % 2, section, 0, 0, 0, 0]).astype(jnp.int32)
    agu, c_own, c_other, place = gather_weights((w_query, w_key, w_value, w_out, w_gate, w_up, w_down), owners)
    cosine, sine, mask = jax.vmap(make_tables)(segments[:, 0])
    agu, c_own, c_other, place, cosine, sine, mask, tokens, out_grad, coords = lax.optimization_barrier(
        (agu, c_own, c_other, place, cosine, sine, mask, tokens, out_grad, coords)
    )
    common = dict(
        agu=agu, c_own=c_own, c_other=c_other, place=place, cos=cosine, sin=sine, mask=mask, coords=coords, ga=attn_gain, gb=mlp_gain
    )

    def send_on(block):
        return lax.ppermute(block, "section", [(0, 1)])

    def send_back(block):
        return lax.ppermute(block, "section", [(1, 0)])

    def stored_of(outs):
        return {key: outs["store_" + key] for key in STORED}

    def rows_of(stored, outs):
        return stored | {key: outs["keep_" + key] for key in KEPT}

    first_out = run_layer(N.lead, N.zero, common, tokens)
    lead_zero = first_out[N.out]
    common = {key: common[key] for key in common if key not in (N.c_own, N.c_other)} | {N.down: first_out[N.laid]}
    arrived_zero = send_on(lead_zero)
    lead_one = run_layer(N.lead, N.one, common, tokens)[N.out]
    arrived_one = send_on(lead_one)
    two = run_layer(N.both, N.other, common, tokens, arrived_zero, out_grad)
    arrived_grad = send_back(two[N.in_grad])
    four = run_layer(N.ahead, N.same, common, tokens, arrived_one)
    stored_two, stored_four = stored_of(two), stored_of(four)
    five = run_layer(N.behind, N.same, common, tokens, arrived_one, out_grad, arrived_grad, stored_four)
    last_grad = send_back(five[N.in_grad])
    six = run_layer(N.behind, N.other, common, tokens, arrived_zero, out_grad, last_grad, stored_two)
    grads = run_weights(
        coords, (rows_of(stored_four, five), rows_of(stored_two, six)), (arrived_grad, last_grad), out_grad
    )
    shares = scatter_grads(grads, five[N.gains] + six[N.gains], owners)
    layer_out = jnp.stack([jnp.where(first, four[N.out], two[N.out]), jnp.where(first, two[N.out], four[N.out])])
    input_grad = jnp.stack([jnp.where(first, five[N.in_grad], six[N.in_grad]), jnp.where(first, six[N.in_grad], five[N.in_grad])])
    return (layer_out[None], input_grad[None], *shares)


def solution(mesh):
    weights = (P("section", "dp"),) * 7
    gains = (P("section", None),) * 2
    rows = P("section", None, "dp", None)
    return jax.shard_map(
        shards,
        mesh=mesh,
        in_specs=(P(None, "dp", None), P(None, "dp", None), *weights, *gains, P(None, "dp", None)),
        out_specs=(rows, rows, *weights, *gains),
        check_vma=False,
    )
```

```python
import functools
import math

import jax
import jax.numpy as jnp
from jax import lax
from jax.experimental import pallas as pl
from jax.experimental.pallas import tpu as pltpu
from jax.sharding import PartitionSpec as P

D = 576
HEADS = 9
KV_HEADS = 3
HEAD = 64
FF = 1536
TOK_MB = 256
QW = HEADS * HEAD
KVW = KV_HEADS * HEAD
REP = HEADS // KV_HEADS

EPS = 1e-05
THETA = 100000.0
NEG = -1000000000.0

PAD = 640
COL_K = QW
COL_O = QW + KVW
COL_V = COL_O + D
COL_VX = 1280
SKIP_V = COL_V - COL_VX

BF = jnp.bfloat16
F32 = jnp.float32

PARAMS = pltpu.CompilerParams(vmem_limit_bytes=60 * 1024 * 1024)


def dot(left, right):
    return lax.dot_general(left, right, (((1,), (0,)), ((), ())), preferred_element_type=F32)


def dot_nt(left, right):
    return lax.dot_general(left, right, (((1,), (1,)), ((), ())), preferred_element_type=F32)


def dot_tn(left, right):
    return lax.dot_general(left, right, (((0,), (0,)), ((), ())), preferred_element_type=F32)


def spread(rows, place):
    return dot(rows, place).astype(BF)


def collect(rows, place):
    high = rows.astype(BF)
    low = (rows - high.astype(F32)).astype(BF)
    return dot_nt(high, place) + dot_nt(low, place)


def turned(tile):
    lane = lax.broadcasted_iota(jnp.int32, tile.shape, 1)
    return jnp.where(lane % HEAD < HEAD // 2, pltpu.roll(tile, 128 - HEAD // 2, 1), pltpu.roll(tile, HEAD // 2, 1))


def inv_rms(stream):
    return lax.rsqrt(jnp.mean(stream * stream, -1, keepdims=True) + EPS)


def norm_back(stream, gain_row, grad_normed):
    scale_r = inv_rms(stream)
    weighted = grad_normed * gain_row
    grad_stream = scale_r * weighted - stream * scale_r**3 * jnp.mean(
        stream * weighted, -1, keepdims=True
    )
    grad_gain = jnp.sum(grad_normed * stream * scale_r, 0, keepdims=True)
    return (grad_stream, grad_gain)


CHUNK = 768
CHUNKS = FF // CHUNK
HALF = TOK_MB // 2
GROUPS = 16
EACH = PAD // GROUPS
EACH_FF = FF // GROUPS
DV = QW + D + 2 * KVW - COL_VX

ANY = pl.BlockSpec(memory_space=pl.ANY)
SMEM = pl.BlockSpec(memory_space=pltpu.SMEM)
VMEM = pl.BlockSpec(memory_space=pltpu.VMEM)


def shape(*dims, dtype=BF):
    return jax.ShapeDtypeStruct(dims, dtype)


class Names:
    def __getattr__(self, name):
        return name


N = Names()


STORED = dict(
    na=shape(TOK_MB, PAD),
    qk=shape(TOK_MB, COL_O),
    v=shape(TOK_MB, KVW),
    lse=shape(TOK_MB, 128, dtype=F32),
    mx=shape(TOK_MB, PAD),
    mid=shape(TOK_MB, D, dtype=F32),
    nb=shape(TOK_MB, PAD),
    gate=shape(TOK_MB, FF, dtype=F32),
    up=shape(TOK_MB, FF, dtype=F32),
    act=shape(TOK_MB, FF),
)
FOR_BACK = (N.gate, N.up, N.mid, N.qk, N.v, N.lse)
KEPT = dict(
    dqk=shape(TOK_MB, COL_O),
    dv=shape(TOK_MB, DV),
    gattn=shape(TOK_MB, D),
    dg=shape(TOK_MB, FF),
    du=shape(TOK_MB, FF),
)
INPUTS = dict(
    agu=shape(3, PAD, FF),
    c_own=shape(GROUPS // 2, EACH_FF, D),
    c_other=shape(GROUPS // 2, EACH_FF, D),
    down=shape(GROUPS, EACH_FF, D),
    place=shape(D, PAD),
    cos=shape(2, TOK_MB, 128, dtype=F32),
    sin=shape(2, TOK_MB, 128, dtype=F32),
    mask=shape(2, TOK_MB, TOK_MB, dtype=F32),
)
HELD = dict(
    att=shape(PAD, FF),
    gw=shape(PAD, FF),
    uw=shape(PAD, FF),
    down=shape(GROUPS, EACH_FF, D),
    place=shape(D, PAD),
    cos=shape(TOK_MB, 128, dtype=F32),
    sin=shape(TOK_MB, 128, dtype=F32),
    mask=shape(TOK_MB, TOK_MB, dtype=F32),
    x=shape(TOK_MB, D),
    g=shape(TOK_MB, D),
)


class Copies:
    def __init__(self, sems):
        self.sems, self.count, self.open = sems, 0, {}

    def start(self, name, source, target):
        copy = pltpu.make_async_copy(source, target, self.sems.at[self.count])
        self.count += 1
        self.open.setdefault(name, []).append(copy)
        copy.start()

    def start_either(self, name, take_one, one, two, target):
        first = pltpu.make_async_copy(one, target, self.sems.at[self.count])
        second = pltpu.make_async_copy(two, target, self.sems.at[self.count])
        self.count += 1
        self.open.setdefault(name, []).append(first)

        @pl.when(take_one)
        def _():
            first.start()

        @pl.when(jnp.logical_not(take_one))
        def _():
            second.start()

    def wait(self, *names):
        for name in names:
            for copy in self.open.pop(name, ()):
                copy.wait()

    def wait_all(self):
        self.wait(*list(self.open))


def blocks_of_rows():
    return ((0, HALF, HALF), (HALF, TOK_MB, TOK_MB))


def forward(held, kept, copies, ga_ref, gb_ref, note):
    copies.wait(N.x, N.place)
    place = held[N.place][...]
    stream = held[N.x][...].astype(F32)
    normed_a = spread((stream * inv_rms(stream) * ga_ref[...]).astype(BF), place)
    note(N.na, normed_a)
    copies.wait(N.att, N.cos, N.sin)
    raw = dot(normed_a, held[N.att][:, :COL_O])
    cosine, sine = held[N.cos][...], held[N.sin][...]
    tiles = []
    lane = lax.broadcasted_iota(jnp.int32, (TOK_MB, 128), 1)
    for j in range(COL_O // 128):
        tile = raw[:, 128 * j : 128 * (j + 1)]
        tile = (tile * cosine + turned(tile) * sine).astype(BF)
        if 128 * (j + 1) <= QW:
            tile = tile * jnp.asarray(HEAD ** (-0.5), BF)
        elif 128 * j < QW:
            tile = jnp.where(lane < QW - 128 * j, tile.astype(F32) * HEAD ** (-0.5), tile.astype(F32)).astype(BF)
        tiles.append(tile)
    qk = jnp.concatenate(tiles, 1)
    note(N.qk, qk)
    value = dot(normed_a, held[N.att][:, COL_VX:])[:, SKIP_V:].astype(BF)
    note(N.v, value)
    copies.wait(N.mask)
    mixed = []
    for h in range(HEADS):
        kv = h // REP
        key = qk[:, COL_K + HEAD * kv : COL_K + HEAD * (kv + 1)]
        val = value[:, HEAD * kv : HEAD * (kv + 1)]
        parts = []
        for low, high, keys in blocks_of_rows():
            query = qk[low:high, HEAD * h : HEAD * (h + 1)]
            scores = jnp.where(held[N.mask][low:high, :keys] > 0.5, dot_nt(query, key[:keys]), NEG)
            row_max = jnp.max(scores, -1, keepdims=True)
            terms = jnp.exp(scores - row_max)
            total = jnp.sum(terms, -1, keepdims=True)
            attend = (terms * (1.0 / total)).astype(BF)
            parts.append(dot(attend, val[:keys]).astype(BF))
            if kept is not None:
                kept[N.lse][low:high, h : h + 1] = row_max + jnp.log(total)
        mixed.append(jnp.concatenate(parts, 0))
    note(N.lse, None)
    mixed_p = spread(jnp.concatenate(mixed, 1), place)
    note(N.mx, mixed_p)
    middle = stream + dot(mixed_p, held[N.att][:, COL_O : COL_O + D])
    note(N.mid, middle)
    normed_b = spread((middle * inv_rms(middle) * gb_ref[...]).astype(BF), place)
    note(N.nb, normed_b)
    copies.wait(N.gw, N.uw, N.down)
    note(N.laid, None)
    result = middle
    for c in range(0, FF, CHUNK):
        gate = dot(normed_b, held[N.gw][:, c : c + CHUNK])
        up = dot(normed_b, held[N.uw][:, c : c + CHUNK])
        act = (gate * jax.nn.sigmoid(gate) * up).astype(BF)
        result = result + dot(act, down_of(held)[c : c + CHUNK])
        if kept is not None:
            kept[N.gate][:, c : c + CHUNK] = gate
            kept[N.up][:, c : c + CHUNK] = up
            kept[N.act][:, c : c + CHUNK] = act
    note(N.gate, None)
    note(N.up, None)
    note(N.act, None)
    return result.astype(BF)


def down_of(held):
    return held[N.down][...].reshape(FF, D)


def backward(held, kept, copies, ga_ref, gb_ref, note):
    copies.wait(N.g, N.down)
    grad_low = held[N.g][...]
    grad_out = grad_low.astype(F32)
    back_p = jnp.zeros((TOK_MB, PAD), F32)
    down = down_of(held)
    for c in range(0, FF, CHUNK):
        grad_act = dot_nt(grad_low, down[c : c + CHUNK])
        copies.wait(N.gate + str(c), N.up + str(c))
        gate = kept[N.gate][:, c : c + CHUNK]
        up = kept[N.up][:, c : c + CHUNK]
        sig = jax.nn.sigmoid(gate)
        acts = grad_act * sig
        d_gate = (acts * up * (1.0 + gate * (1.0 - sig))).astype(BF)
        d_up = (acts * gate).astype(BF)
        note(N.dg, d_gate, c)
        note(N.du, d_up, c)
        copies.wait(N.gw, N.uw)
        back_p = back_p + dot_nt(d_gate, held[N.gw][:, c : c + CHUNK]) + dot_nt(d_up, held[N.uw][:, c : c + CHUNK])
    copies.wait(N.place, N.mid, N.att)
    place = held[N.place][...]
    back_b, gain_b = norm_back(kept[N.mid][...], gb_ref[...], collect(back_p, place))
    grad_middle = grad_out + back_b
    grad_attn = grad_middle.astype(BF)
    note(N.gattn, grad_attn)
    grad_mixed = dot_nt(dot_nt(grad_attn, held[N.att][:, COL_O : COL_O + D]).astype(BF), place).astype(BF)
    copies.wait(N.qk, N.v, N.lse, N.mask, N.cos, N.sin, N.x)
    d_query, d_key, d_value = [], [], []
    for kv in range(KV_HEADS):
        key = kept[N.qk][:, COL_K + HEAD * kv : COL_K + HEAD * (kv + 1)]
        value = kept[N.v][:, HEAD * kv : HEAD * (kv + 1)]
        sums_k, sums_v = [None, None], [None, None]
        for h in range(kv * REP, (kv + 1) * REP):
            parts = []
            for at, (low, high, keys) in enumerate(blocks_of_rows()):
                query = kept[N.qk][low:high, HEAD * h : HEAD * (h + 1)]
                grad_h = grad_mixed[low:high, HEAD * h : HEAD * (h + 1)]
                scores = jnp.where(held[N.mask][low:high, :keys] > 0.5, dot_nt(query, key[:keys]), NEG)
                attend = jnp.exp(scores - kept[N.lse][low:high, h : h + 1])
                grad_attend = dot_nt(grad_h, value[:keys])
                inner = jnp.sum(attend * grad_attend, -1, keepdims=True)
                grad_scores = (attend * (grad_attend - inner)).astype(BF)
                part_v = dot_tn(attend.astype(BF), grad_h)
                part_k = dot_tn(grad_scores, query)
                sums_v[at] = part_v if sums_v[at] is None else sums_v[at] + part_v
                sums_k[at] = part_k if sums_k[at] is None else sums_k[at] + part_k
                parts.append(dot(grad_scores, key[:keys]) * HEAD ** (-0.5))
            d_query.append(jnp.concatenate(parts, 0))
        d_key.append(jnp.concatenate([sums_k[0] + sums_k[1][:HALF], sums_k[1][HALF:]], 0))
        d_value.append(jnp.concatenate([sums_v[0] + sums_v[1][:HALF], sums_v[1][HALF:]], 0).astype(BF))
    raw = jnp.concatenate(d_query + d_key, 1)
    cosine, sine = held[N.cos][...], held[N.sin][...]
    tiles = []
    for j in range(COL_O // 128):
        tile = raw[:, 128 * j : 128 * (j + 1)]
        tiles.append((tile * cosine - turned(tile) * sine).astype(BF))
    d_qk = jnp.concatenate(tiles, 1)
    d_v = jnp.concatenate([jnp.zeros((TOK_MB, SKIP_V), BF)] + d_value, 1)
    note(N.dqk, d_qk)
    note(N.dv, d_v)
    back_p = dot_nt(d_qk, held[N.att][:, :COL_O]) + dot_nt(d_v, held[N.att][:, COL_VX:])
    back_a, gain_a = norm_back(held[N.x][...].astype(F32), ga_ref[...], collect(back_p, place))
    return (grad_middle + back_a).astype(BF), gain_a, gain_b


SLOTS = dict(
    lead=(N.forward,),
    both=(N.forward, N.backward, N.store),
    ahead=(N.forward, N.store),
    behind=(N.backward, N.keep),
    last=(N.backward, N.weights),
)


def layer_kernel(name, micro, names, refs):
    does = SLOTS[name]
    ref = dict(zip(names, refs))
    held = {key: ref["held_" + key] for key in HELD if "held_" + key in ref}
    kept = {key: ref["kept_" + key] for key in STORED if "kept_" + key in ref} or None
    section = ref[N.coords][3]
    index = {N.zero: 0, N.one: 1, N.same: section, N.other: 1 - section}[micro]
    copies = Copies(ref[N.sems])

    def bring(key):
        copies.start(key, ref[key].at[index], held[key])

    def bring_x():
        if N.arrived in ref:
            copies.start_either(N.x, section == 0, ref[N.tokens].at[index], ref[N.arrived], held[N.x])
        else:
            copies.start(N.x, ref[N.tokens].at[index], held[N.x])

    def bring_weights(order):
        for key in order:
            if key == N.down:
                if N.down in ref:
                    copies.start(key, ref[N.down], held[N.down])
                    continue
                own_z, own_x, own_c = (ref[N.coords][i] for i in range(3))
                for at in range(GROUPS // 2):
                    chip = lax.bitwise_xor(own_z, at // 2) * 2 + lax.bitwise_xor(own_x, at % 2)
                    copies.start(key, ref[N.c_own].at[at], held[N.down].at[chip * 2 + own_c])
                    copies.start(key, ref[N.c_other].at[at], held[N.down].at[chip * 2 + 1 - own_c])
            elif key == N.place:
                copies.start(key, ref[N.place], held[N.place])
            else:
                copies.start(key, ref[N.agu].at[(N.att, N.gw, N.uw).index(key)], held[key])

    def bring_g():
        if N.arrived_grad in ref:
            copies.start_either(N.g, section == 0, ref[N.arrived_grad], ref[N.out_grad].at[index], held[N.g])
        else:
            copies.start(N.g, ref[N.out_grad].at[index], held[N.g])

    if N.forward in does:
        bring_x()
        bring_weights([N.place, N.att])
        bring(N.cos)
        bring(N.sin)
        bring(N.mask)
        bring_weights([N.gw, N.uw, N.down])
        if N.backward in does:
            bring_g()
    else:
        bring_g()
        bring_weights([N.down])
        for c in range(0, FF, CHUNK):
            for key in (N.gate, N.up):
                copies.start(key + str(c), ref["stored_" + key].at[:, c : c + CHUNK], kept[key].at[:, c : c + CHUNK])
        bring_weights([N.gw, N.uw, N.place])
        copies.start(N.mid, ref[N.stored_mid], kept[N.mid])
        bring_weights([N.att])
        for key in (N.qk, N.v, N.lse):
            copies.start(key, ref["stored_" + key], kept[key])
        bring(N.mask)
        bring(N.cos)
        bring(N.sin)
        bring_x()

    def note_stored(key, value, column=None):
        if key == N.laid:
            if N.laid in ref:
                copies.start(N.laid, held[N.down], ref[N.laid])
            return
        if N.store in does:
            if value is not None:
                kept[key][...] = value
            copies.start("out_" + key, kept[key], ref["store_" + key])

    if N.weights in does:
        for key in PAIRS:
            half = ref["in_" + key].at[pl.ds(0, TOK_MB)]
            if key == N.g:
                copies.start_either(key + "_0", section == 0, ref[N.grad_0], ref[N.out_grad].at[section], half)
            else:
                copies.start(key, ref[key + "_0"], half)
        for key in (N.act, N.nb, N.mx, N.na):
            copies.start(key, ref[key + "_1"], ref["in_" + key].at[pl.ds(TOK_MB, TOK_MB)])
        feed_forward, attention = weight_parts(ref, copies)

    def note_kept(key, value, column=None):
        if N.weights in does:
            columns = slice(None) if column is None else slice(column, column + CHUNK)
            ref["in_" + key][TOK_MB:, columns] = value
            if key == N.gattn:
                copies.wait(N.g + "_0")
                ref[N.in_g][TOK_MB:, :] = held[N.g][...]
                feed_forward()
        if N.keep in does:
            if column is None:
                ref["made_" + key][...] = value
            else:
                ref["made_" + key][:, column : column + CHUNK] = value
            if column in (None, FF - CHUNK):
                copies.start("out_" + key, ref["made_" + key], ref["keep_" + key])

    if N.forward in does:
        ref[N.out][...] = forward(held, kept, copies, ref[N.ga], ref[N.gb], note_stored)
    if N.backward in does:
        grad, gain_a, gain_b = backward(held, kept, copies, ref[N.ga], ref[N.gb], note_kept)
        ref[N.in_grad][...] = grad
        if N.weights in does:
            attention()
        if N.keep in does or N.weights in does:
            ref[N.gains][0:1, :] = gain_a
            ref[N.gains][1:2, :] = gain_b
    copies.wait_all()


def run_layer(name, micro, common, tokens, arrived=None, out_grad=None, arrived_grad=None, stored=None, rows=None, first_grad=None):
    does = SLOTS[name]
    operands = dict(coords=common[N.coords], tokens=tokens, ga=common[N.ga], gb=common[N.gb])
    operands.update({key: common[key] for key in INPUTS if key in common})
    specs = dict(coords=SMEM, ga=VMEM, gb=VMEM)
    if arrived is not None:
        operands[N.arrived] = arrived
    if N.backward in does:
        operands[N.out_grad] = out_grad
        if arrived_grad is not None:
            operands[N.arrived_grad] = arrived_grad
    if stored is not None:
        operands.update({"stored_" + key: stored[key] for key in FOR_BACK})
    if N.weights in does:
        operands.update({key + "_0": rows[key] for key in PAIRS if key != N.g})
        operands.update({key + "_1": stored[key] for key in (N.act, N.nb, N.mx, N.na)})
        operands[N.grad_0] = first_grad
    outs, out_specs = {}, []
    if N.forward in does:
        outs[N.out] = shape(TOK_MB, D)
    if N.down not in common:
        outs[N.laid] = INPUTS[N.down]
    if N.backward in does:
        outs[N.in_grad] = shape(TOK_MB, D)
    if N.weights in does:
        outs[N.gains] = shape(2, D, dtype=F32)
        outs.update({key: shape(2, 4, 4, EACH, FF) for key in (N.out_keep_m, N.out_send_m)})
    if N.keep in does:
        outs[N.gains] = shape(2, D, dtype=F32)
        outs.update({"keep_" + key: KEPT[key] for key in KEPT})
    if N.store in does:
        outs.update({"store_" + key: STORED[key] for key in STORED})
    out_specs = [ANY if key.startswith(("store_", "keep_", "laid", "out_")) else VMEM for key in outs]
    scratch = {"held_" + key: pltpu.VMEM(h.shape, h.dtype) for key, h in HELD.items() if key != N.g or N.backward in does}
    if name != N.lead:
        hold = STORED if N.forward in does else FOR_BACK
        scratch.update({"kept_" + key: pltpu.VMEM(STORED[key].shape, STORED[key].dtype) for key in hold})
    if N.keep in does:
        scratch.update({"made_" + key: pltpu.VMEM(KEPT[key].shape, BF) for key in KEPT})
    if N.weights in does:
        columns = {key: (STORED | KEPT | {N.g: HELD[N.g]})[key].shape[1] for key in PAIRS}
        scratch.update({"in_" + key: pltpu.VMEM((2 * TOK_MB, columns[key]), BF) for key in PAIRS})
        scratch.update({key: pltpu.VMEM((2, 4, 4, EACH, FF), BF) for key in (N.keep_m, N.send_m)})
    scratch[N.sems] = pltpu.SemaphoreType.DMA((48 if N.weights in does else 28 if N.down in common else 44,))
    names = list(operands) + list(outs) + list(scratch)

    def kernel(*refs):
        layer_kernel(name, micro, names, refs)

    results = pl.pallas_call(
        kernel,
        out_shape=list(outs.values()),
        in_specs=[specs.get(key, ANY) for key in operands],
        out_specs=out_specs,
        scratch_shapes=list(scratch.values()),
        compiler_params=PARAMS,
        name="layer_" + name,
    )(*operands.values())
    return dict(zip(outs, results))


PAIRS = (N.act, N.g, N.nb, N.dg, N.du, N.mx, N.gattn, N.na, N.dqk, N.dv)


def slab_of(block):
    return jnp.concatenate(
        [
            jnp.concatenate([block[8 * i : 8 * i + 8, 128 * j : 128 * j + 128] for i in range(EACH_FF // 8)], 1)
            for j in range(PAD // 128)
        ],
        0,
    )


def block_of(slab):
    tiles = slab.reshape(slab.shape[:-2] + (PAD // 128, 8, EACH_FF // 8, 128))
    return jnp.moveaxis(tiles, -2, -4).swapaxes(-3, -2).reshape(slab.shape[:-2] + (EACH_FF, PAD))


def weight_parts(ref, copies):
    own_z, own_x, own_c = (ref[N.coords][i] for i in range(3))

    def put_pairs(keep_ref, send_ref, at, columns, blocks, pair):
        for one, two in zip(blocks[::2], blocks[1::2]):
            far, across = lax.bitwise_xor(own_z, pair // 2), lax.bitwise_xor(own_x, pair % 2)
            index = (across, far) + at + (slice(None), columns)
            keep_ref[index] = jnp.where(own_c == 0, one, two).astype(BF)
            send_ref[index] = jnp.where(own_c == 0, two, one).astype(BF)
            pair += 1

    def put(keep_ref, send_ref, at, columns, rows):
        put_pairs(keep_ref, send_ref, at, columns, jnp.split(rows, GROUPS), 0)

    def feed_forward():
        copies.wait(N.act, N.g)
        grad_down = jnp.concatenate([ref[N.in_g][...], jnp.zeros((2 * TOK_MB, PAD - D), BF)], 1)
        step = 4 * EACH_FF
        for c in range(0, FF, step):
            slabs = [slab_of(piece) for piece in jnp.split(dot_tn(ref[N.in_act][:, c : c + step], grad_down), 4)]
            put_pairs(ref[N.keep_m], ref[N.send_m], (3,), slice(0, FF), slabs, c // step * 2)
        copies.wait(N.nb, N.dg, N.du)
        normed_b = ref[N.in_nb][...]
        for at, key in ((1, N.dg), (2, N.du)):
            for c in range(0, FF, CHUNK):
                put(ref[N.keep_m], ref[N.send_m], (at,), slice(c, c + CHUNK), dot_tn(normed_b, ref["in_" + key][:, c : c + CHUNK]))
        for slab in range(1, 4):
            copies.start(N.out, ref[N.send_m].at[:, :, slab], ref[N.out_send_m].at[:, :, slab])
            copies.start(N.out, ref[N.keep_m].at[:, :, slab], ref[N.out_keep_m].at[:, :, slab])

    def attention():
        copies.wait(N.mx, N.gattn, N.na, N.dqk, N.dv)
        normed_a, mixed = ref[N.in_na][...], ref[N.in_mx][...]
        put(ref[N.keep_m], ref[N.send_m], (0,), slice(0, COL_O), dot_tn(normed_a, ref[N.in_dqk][...]))
        put(ref[N.keep_m], ref[N.send_m], (0,), slice(COL_O, COL_VX), dot_tn(mixed, ref[N.in_gattn][:, : COL_VX - COL_O]))
        grad_o = dot_tn(mixed, ref[N.in_gattn][:, COL_VX - COL_O :])
        grad_o = jnp.concatenate([grad_o, jnp.zeros((PAD, KVW), F32)], 1)
        put(ref[N.keep_m], ref[N.send_m], (0,), slice(COL_VX, FF), dot_tn(normed_a, ref[N.in_dv][...]) + grad_o)
        copies.start(N.out, ref[N.send_m].at[:, :, 0], ref[N.out_send_m].at[:, :, 0])
        copies.start(N.out, ref[N.keep_m].at[:, :, 0], ref[N.out_keep_m].at[:, :, 0])

    return feed_forward, attention


def make_tables(seg_row):
    count_t = seg_row.shape[0]
    order_idx = jnp.arange(count_t, dtype=jnp.int32)
    same_doc = seg_row[:, None] == seg_row[None, :]
    before = order_idx[None, :] < order_idx[:, None]
    positions = jnp.sum(jnp.where(same_doc & before, jnp.float32(1.0), jnp.float32(0.0)), axis=1)
    allowed = same_doc & (order_idx[None, :] <= order_idx[:, None])
    inv_freq = jnp.exp(jnp.arange(HEAD // 2, dtype=jnp.float32) * (-2.0 * math.log(THETA) / HEAD))
    angles = positions[:, None] * inv_freq[None, :]
    cosine, sine = jnp.cos(angles), jnp.sin(angles)
    cosine = jnp.concatenate([cosine] * 4, -1)
    sine = jnp.concatenate([-sine, sine] * 2, -1)
    return (cosine, sine, allowed.astype(F32))


def placement(rows_each, rows_padded):
    row = lax.broadcasted_iota(jnp.int32, (D, PAD), 0)
    col = lax.broadcasted_iota(jnp.int32, (D, PAD), 1)
    return (col == row + (row // rows_each) * (rows_padded - rows_each)).astype(BF)


def place_of(z, x, c):
    return (z * 2 + x) * 2 + c


PLACES = [(z, x, c) for z in range(4) for x in range(2) for c in range(2)]


def moved(value, dz, dx, dc):
    return lax.ppermute(value, "dp", [(place_of(z, x, c), place_of(z ^ dz, x ^ dx, c ^ dc)) for z, x, c in PLACES])


def gather_weights(shard, owners):
    w_query, w_key, w_value, w_out, w_gate, w_up, w_down = shard
    if owners == GROUPS:
        rows = D // owners
        att = jnp.concatenate(
            [w_query.reshape(rows, QW), w_key.reshape(rows, KVW), w_out.reshape(rows, D), w_value.reshape(rows, KVW)], 1
        )
        packed = jnp.stack([att, w_gate.reshape(rows, FF), w_up.reshape(rows, FF)])
        packed = jnp.pad(packed, ((0, 0), (0, EACH - rows), (0, 0)))
        agu = lax.all_gather(packed, "dp", axis=1, tiled=True)
        w_down = w_down.reshape(EACH_FF, D)
        lines = [w_down] + [moved(w_down, dz, 0, 0) for dz in (1, 2, 3)]
        c_own = jnp.stack([block for line in lines for block in (line, moved(line, 0, 1, 0))])
        c_other = moved(c_own, 0, 0, 1)
        c_own, c_other, corner = lax.optimization_barrier((c_own, c_other, w_down[:8, :128]))
        met = lax.all_gather(corner, "dp", axis=0, tiled=False)
        corner = lax.dynamic_index_in_dim(met, lax.axis_index("dp"), 0, keepdims=False)
        c_own = c_own.at[0, :8, :128].set(corner)
        return agu, c_own, c_other, placement(rows, EACH)
    w_query, w_key, w_value, w_out, w_gate, w_up, w_down = (
        lax.all_gather(member[0], "dp", axis=0, tiled=True) for member in shard
    )
    att = jnp.concatenate(
        [w_query.reshape(D, QW), w_key.reshape(D, KVW), w_out.reshape(QW, D), w_value.reshape(D, KVW)], 1
    )
    agu = jnp.pad(jnp.stack([att, w_gate.reshape(D, FF), w_up.reshape(D, FF)]), ((0, 0), (0, PAD - D), (0, 0)))
    down = w_down.reshape(GROUPS // 2, 2, EACH_FF, D)
    return agu, down[:, 0], down[:, 1], placement(D, D)


def cut(att):
    return att[:, :QW], att[:, COL_K:COL_O], att[:, COL_V:], att[:, COL_O:COL_V]


def add(*terms):
    return sum(term.astype(F32) for term in terms)


def sum_of_four(value, others):
    return (value + others[0]) + (others[1] + others[2])


def reduce_blocks(keep, send, gains):
    near = [moved(gains, 0, 0, 1), moved(gains, 0, 1, 0), moved(gains, 0, 1, 1)]
    got = moved(send, 0, 0, 1)
    got, near = lax.optimization_barrier((got, near))
    gains = sum_of_four(gains, near)
    wide = [moved(gains, 1, 0, 0), moved(gains, 2, 0, 0), moved(gains, 3, 0, 0)]
    blocks = [add(keep[1, far], got[1, far]).astype(BF) for far in range(4)]
    across_three, across_two = moved(blocks[3], 0, 1, 0), moved(blocks[2], 0, 1, 0)
    across_three, wide = lax.optimization_barrier((across_three, wide))
    gains = sum_of_four(gains, wide)
    three = add(keep[0, 3], got[0, 3], across_three).astype(BF)
    three, last_one = lax.optimization_barrier((three, blocks[1]))
    beside_three, across_one = moved(three, 1, 0, 0), moved(last_one, 0, 1, 0)
    across_two, last_zero = lax.optimization_barrier((across_two, blocks[0]))
    across_zero = moved(last_zero, 0, 1, 0)
    far_two = moved(add(keep[0, 2], got[0, 2], across_two, beside_three).astype(BF), 2, 0, 0)
    beside_one = moved(add(keep[0, 1], got[0, 1], across_one).astype(BF), 1, 0, 0)
    return add(keep[0, 0], got[0, 0], across_zero, far_two, beside_one), gains


def scatter_grads(out, gains, owners):
    if owners == GROUPS:
        main, gains = reduce_blocks(out[N.out_keep_m], out[N.out_send_m], gains)
        rows = D // owners
        att, gate, up = main[0, :rows], main[1, :rows], main[2, :rows]
        down = block_of(main[3])[:, :D]
        return tuple(piece.reshape(1, -1) for piece in cut(att) + (gate, up, down)) + (gains[0:1], gains[1:2])
    main = jnp.stack([out[N.out_keep_m], out[N.out_send_m]]).transpose(3, 2, 1, 0, 4, 5).reshape(4, GROUPS, EACH, FF)
    down = block_of(main[3])[:, :, :D].reshape(FF, D)
    main = main[:3].reshape(3, PAD, FF)[:, :D]
    pieces = cut(main[0]) + (main[1], main[2], down)
    gains = lax.psum(gains, "dp")
    return tuple(
        lax.psum_scatter(piece.reshape(owners, -1), "dp", scatter_dimension=0, tiled=True).astype(F32) for piece in pieces
    ) + (gains[0:1], gains[1:2])


def shards(
    tokens,
    segments,
    w_query,
    w_key,
    w_value,
    w_out,
    w_gate,
    w_up,
    w_down,
    attn_gain,
    mlp_gain,
    out_grad,
):
    section = lax.axis_index("section")
    first = section == 0
    owners = lax.axis_size("dp")
    me = lax.axis_index("dp") if owners == GROUPS else 0
    coords = jnp.stack([me // 4, me // 2 % 2, me % 2, section, 0, 0, 0, 0]).astype(jnp.int32)
    agu, c_own, c_other, place = gather_weights((w_query, w_key, w_value, w_out, w_gate, w_up, w_down), owners)
    cosine, sine, mask = jax.vmap(make_tables)(segments[:, 0])
    agu, c_own, c_other, place, cosine, sine, mask, tokens, out_grad, coords = lax.optimization_barrier(
        (agu, c_own, c_other, place, cosine, sine, mask, tokens, out_grad, coords)
    )
    common = dict(
        agu=agu, c_own=c_own, c_other=c_other, place=place, cos=cosine, sin=sine, mask=mask, coords=coords, ga=attn_gain, gb=mlp_gain
    )

    def send_on(block):
        return lax.ppermute(block, "section", [(0, 1)])

    def send_back(block):
        return lax.ppermute(block, "section", [(1, 0)])

    def stored_of(outs):
        return {key: outs["store_" + key] for key in STORED}

    def rows_of(stored, outs):
        return stored | {key: outs["keep_" + key] for key in KEPT}

    first_out = run_layer(N.lead, N.zero, common, tokens)
    lead_zero = first_out[N.out]
    common = {key: common[key] for key in common if key not in (N.c_own, N.c_other)} | {N.down: first_out[N.laid]}
    arrived_zero = send_on(lead_zero)
    lead_one = run_layer(N.lead, N.one, common, tokens)[N.out]
    arrived_one = send_on(lead_one)
    two = run_layer(N.both, N.other, common, tokens, arrived_zero, out_grad)
    arrived_grad = send_back(two[N.in_grad])
    four = run_layer(N.ahead, N.same, common, tokens, arrived_one)
    stored_two, stored_four = stored_of(two), stored_of(four)
    five = run_layer(N.behind, N.same, common, tokens, arrived_one, out_grad, arrived_grad, stored_four)
    last_grad = send_back(five[N.in_grad])
    six = run_layer(
        N.last, N.other, common, tokens, arrived_zero, out_grad, last_grad, stored_two, rows_of(stored_four, five), arrived_grad
    )
    grads = six
    shares = scatter_grads(grads, five[N.gains] + six[N.gains], owners)
    layer_out = jnp.stack([jnp.where(first, four[N.out], two[N.out]), jnp.where(first, two[N.out], four[N.out])])
    input_grad = jnp.stack([jnp.where(first, five[N.in_grad], six[N.in_grad]), jnp.where(first, six[N.in_grad], five[N.in_grad])])
    return (layer_out[None], input_grad[None], *shares)


def solution(mesh):
    weights = (P("section", "dp"),) * 7
    gains = (P("section", None),) * 2
    rows = P("section", None, "dp", None)
    return jax.shard_map(
        shards,
        mesh=mesh,
        in_specs=(P(None, "dp", None), P(None, "dp", None), *weights, *gains, P(None, "dp", None)),
        out_specs=(rows, rows, *weights, *gains),
        check_vma=False,
    )
```

```python
import functools
import math

import jax
import jax.numpy as jnp
from jax import lax
from jax.experimental import pallas as pl
from jax.experimental.pallas import tpu as pltpu
from jax.sharding import PartitionSpec as P

D = 576
HEADS = 9
KV_HEADS = 3
HEAD = 64
FF = 1536
TOK_MB = 256
QW = HEADS * HEAD
KVW = KV_HEADS * HEAD
REP = HEADS // KV_HEADS

EPS = 1e-05
THETA = 100000.0
NEG = -1000000000.0

PAD = 640
COL_K = QW
COL_O = QW + KVW
COL_V = COL_O + D
COL_VX = 1280
SKIP_V = COL_V - COL_VX

BF = jnp.bfloat16
F32 = jnp.float32

PARAMS = pltpu.CompilerParams(vmem_limit_bytes=60 * 1024 * 1024)


def dot(left, right):
    return lax.dot_general(left, right, (((1,), (0,)), ((), ())), preferred_element_type=F32)


def dot_nt(left, right):
    return lax.dot_general(left, right, (((1,), (1,)), ((), ())), preferred_element_type=F32)


def dot_tn(left, right):
    return lax.dot_general(left, right, (((0,), (0,)), ((), ())), preferred_element_type=F32)


def spread(rows, place):
    return dot(rows, place).astype(BF)


def collect(rows, place):
    high = rows.astype(BF)
    low = (rows - high.astype(F32)).astype(BF)
    return dot_nt(high, place) + dot_nt(low, place)


def turned(tile):
    lane = lax.broadcasted_iota(jnp.int32, tile.shape, 1)
    return jnp.where(lane % HEAD < HEAD // 2, pltpu.roll(tile, 128 - HEAD // 2, 1), pltpu.roll(tile, HEAD // 2, 1))


def inv_rms(stream):
    return lax.rsqrt(jnp.mean(stream * stream, -1, keepdims=True) + EPS)


def norm_back(stream, gain_row, grad_normed):
    scale_r = inv_rms(stream)
    weighted = grad_normed * gain_row
    grad_stream = scale_r * weighted - stream * scale_r**3 * jnp.mean(
        stream * weighted, -1, keepdims=True
    )
    grad_gain = jnp.sum(grad_normed * stream * scale_r, 0, keepdims=True)
    return (grad_stream, grad_gain)


CHUNK = 768
CHUNKS = FF // CHUNK
HALF = TOK_MB // 2
GROUPS = 16
EACH = PAD // GROUPS
EACH_FF = FF // GROUPS
DV = QW + D + 2 * KVW - COL_VX

ANY = pl.BlockSpec(memory_space=pl.ANY)
SMEM = pl.BlockSpec(memory_space=pltpu.SMEM)
VMEM = pl.BlockSpec(memory_space=pltpu.VMEM)


def shape(*dims, dtype=BF):
    return jax.ShapeDtypeStruct(dims, dtype)


class Names:
    def __getattr__(self, name):
        return name


N = Names()


STORED = dict(
    na=shape(TOK_MB, PAD),
    qk=shape(TOK_MB, COL_O),
    v=shape(TOK_MB, KVW),
    lse=shape(TOK_MB, 128, dtype=F32),
    mx=shape(TOK_MB, PAD),
    mid=shape(TOK_MB, D, dtype=F32),
    nb=shape(TOK_MB, PAD),
    gate=shape(TOK_MB, FF, dtype=F32),
    up=shape(TOK_MB, FF, dtype=F32),
    act=shape(TOK_MB, FF),
)
FOR_BACK = (N.gate, N.up, N.mid, N.qk, N.v, N.lse)
KEPT = dict(
    dqk=shape(TOK_MB, COL_O),
    dv=shape(TOK_MB, DV),
    gattn=shape(TOK_MB, D),
    dg=shape(TOK_MB, FF),
    du=shape(TOK_MB, FF),
)
INPUTS = dict(
    agu=shape(3, PAD, FF),
    c_own=shape(GROUPS // 2, EACH_FF, D),
    c_other=shape(GROUPS // 2, EACH_FF, D),
    down=shape(GROUPS, EACH_FF, D),
    place=shape(D, PAD),
    cos=shape(2, TOK_MB, 128, dtype=F32),
    sin=shape(2, TOK_MB, 128, dtype=F32),
    mask=shape(2, TOK_MB, TOK_MB, dtype=F32),
)
HELD = dict(
    att=shape(PAD, FF),
    gw=shape(PAD, FF),
    uw=shape(PAD, FF),
    down=shape(GROUPS, EACH_FF, D),
    place=shape(D, PAD),
    cos=shape(TOK_MB, 128, dtype=F32),
    sin=shape(TOK_MB, 128, dtype=F32),
    mask=shape(TOK_MB, TOK_MB, dtype=F32),
    x=shape(TOK_MB, D),
    g=shape(TOK_MB, D),
)


class Copies:
    def __init__(self, sems):
        self.sems, self.count, self.open = sems, 0, {}

    def start(self, name, source, target):
        copy = pltpu.make_async_copy(source, target, self.sems.at[self.count])
        self.count += 1
        self.open.setdefault(name, []).append(copy)
        copy.start()

    def start_either(self, name, take_one, one, two, target):
        first = pltpu.make_async_copy(one, target, self.sems.at[self.count])
        second = pltpu.make_async_copy(two, target, self.sems.at[self.count])
        self.count += 1
        self.open.setdefault(name, []).append(first)

        @pl.when(take_one)
        def _():
            first.start()

        @pl.when(jnp.logical_not(take_one))
        def _():
            second.start()

    def wait(self, *names):
        for name in names:
            for copy in self.open.pop(name, ()):
                copy.wait()

    def wait_all(self):
        self.wait(*list(self.open))


def blocks_of_rows():
    return ((0, HALF, HALF), (HALF, TOK_MB, TOK_MB))


def forward(held, kept, copies, ga_ref, gb_ref, note):
    copies.wait(N.x, N.place)
    place = held[N.place][...]
    stream = held[N.x][...].astype(F32)
    normed_a = spread((stream * inv_rms(stream) * ga_ref[...]).astype(BF), place)
    note(N.na, normed_a)
    copies.wait(N.att, N.cos, N.sin)
    raw = dot(normed_a, held[N.att][:, :COL_O])
    cosine, sine = held[N.cos][...], held[N.sin][...]
    tiles = []
    lane = lax.broadcasted_iota(jnp.int32, (TOK_MB, 128), 1)
    for j in range(COL_O // 128):
        tile = raw[:, 128 * j : 128 * (j + 1)]
        tile = (tile * cosine + turned(tile) * sine).astype(BF)
        if 128 * (j + 1) <= QW:
            tile = tile * jnp.asarray(HEAD ** (-0.5), BF)
        elif 128 * j < QW:
            tile = jnp.where(lane < QW - 128 * j, tile.astype(F32) * HEAD ** (-0.5), tile.astype(F32)).astype(BF)
        tiles.append(tile)
    qk = jnp.concatenate(tiles, 1)
    note(N.qk, qk)
    value = dot(normed_a, held[N.att][:, COL_VX:])[:, SKIP_V:].astype(BF)
    note(N.v, value)
    copies.wait(N.mask)
    mixed = []
    for h in range(HEADS):
        kv = h // REP
        key = qk[:, COL_K + HEAD * kv : COL_K + HEAD * (kv + 1)]
        val = value[:, HEAD * kv : HEAD * (kv + 1)]
        parts = []
        for low, high, keys in blocks_of_rows():
            query = qk[low:high, HEAD * h : HEAD * (h + 1)]
            scores = jnp.where(held[N.mask][low:high, :keys] > 0.5, dot_nt(query, key[:keys]), NEG)
            row_max = jnp.max(scores, -1, keepdims=True)
            terms = jnp.exp(scores - row_max)
            total = jnp.sum(terms, -1, keepdims=True)
            attend = (terms * (1.0 / total)).astype(BF)
            parts.append(dot(attend, val[:keys]).astype(BF))
            if kept is not None:
                kept[N.lse][low:high, h : h + 1] = row_max + jnp.log(total)
        mixed.append(jnp.concatenate(parts, 0))
    note(N.lse, None)
    mixed_p = spread(jnp.concatenate(mixed, 1), place)
    note(N.mx, mixed_p)
    middle = stream + dot(mixed_p, held[N.att][:, COL_O : COL_O + D])
    note(N.mid, middle)
    normed_b = spread((middle * inv_rms(middle) * gb_ref[...]).astype(BF), place)
    note(N.nb, normed_b)
    copies.wait(N.gw, N.uw, N.down)
    note(N.laid, None)
    result = middle
    for c in range(0, FF, CHUNK):
        gate = dot(normed_b, held[N.gw][:, c : c + CHUNK])
        up = dot(normed_b, held[N.uw][:, c : c + CHUNK])
        act = (gate * jax.nn.sigmoid(gate) * up).astype(BF)
        result = result + dot(act, down_of(held)[c : c + CHUNK])
        if kept is not None:
            kept[N.gate][:, c : c + CHUNK] = gate
            kept[N.up][:, c : c + CHUNK] = up
            kept[N.act][:, c : c + CHUNK] = act
    note(N.gate, None)
    note(N.up, None)
    note(N.act, None)
    return result.astype(BF)


def down_of(held):
    return held[N.down][...].reshape(FF, D)


def backward(held, kept, copies, ga_ref, gb_ref, note):
    copies.wait(N.g, N.down)
    grad_low = held[N.g][...]
    grad_out = grad_low.astype(F32)
    back_p = jnp.zeros((TOK_MB, PAD), F32)
    down = down_of(held)
    for c in range(0, FF, CHUNK):
        grad_act = dot_nt(grad_low, down[c : c + CHUNK])
        copies.wait(N.gate + str(c), N.up + str(c))
        gate = kept[N.gate][:, c : c + CHUNK]
        up = kept[N.up][:, c : c + CHUNK]
        sig = jax.nn.sigmoid(gate)
        acts = grad_act * sig
        d_gate = (acts * up * (1.0 + gate * (1.0 - sig))).astype(BF)
        d_up = (acts * gate).astype(BF)
        note(N.dg, d_gate, c)
        note(N.du, d_up, c)
        copies.wait(N.gw, N.uw)
        back_p = back_p + dot_nt(d_gate, held[N.gw][:, c : c + CHUNK]) + dot_nt(d_up, held[N.uw][:, c : c + CHUNK])
    copies.wait(N.place, N.mid, N.att)
    place = held[N.place][...]
    back_b, gain_b = norm_back(kept[N.mid][...], gb_ref[...], collect(back_p, place))
    grad_middle = grad_out + back_b
    grad_attn = grad_middle.astype(BF)
    note(N.gattn, grad_attn)
    grad_mixed = dot_nt(dot_nt(grad_attn, held[N.att][:, COL_O : COL_O + D]).astype(BF), place).astype(BF)
    copies.wait(N.qk, N.v, N.lse, N.mask, N.cos, N.sin, N.x)
    d_query, d_key, d_value = [], [], []
    for kv in range(KV_HEADS):
        key = kept[N.qk][:, COL_K + HEAD * kv : COL_K + HEAD * (kv + 1)]
        value = kept[N.v][:, HEAD * kv : HEAD * (kv + 1)]
        sums_k, sums_v = [None, None], [None, None]
        for h in range(kv * REP, (kv + 1) * REP):
            parts = []
            for at, (low, high, keys) in enumerate(blocks_of_rows()):
                query = kept[N.qk][low:high, HEAD * h : HEAD * (h + 1)]
                grad_h = grad_mixed[low:high, HEAD * h : HEAD * (h + 1)]
                scores = jnp.where(held[N.mask][low:high, :keys] > 0.5, dot_nt(query, key[:keys]), NEG)
                attend = jnp.exp(scores - kept[N.lse][low:high, h : h + 1])
                grad_attend = dot_nt(grad_h, value[:keys])
                inner = jnp.sum(attend * grad_attend, -1, keepdims=True)
                grad_scores = (attend * (grad_attend - inner)).astype(BF)
                part_v = dot_tn(attend.astype(BF), grad_h)
                part_k = dot_tn(grad_scores, query)
                sums_v[at] = part_v if sums_v[at] is None else sums_v[at] + part_v
                sums_k[at] = part_k if sums_k[at] is None else sums_k[at] + part_k
                parts.append(dot(grad_scores, key[:keys]) * HEAD ** (-0.5))
            d_query.append(jnp.concatenate(parts, 0))
        d_key.append(jnp.concatenate([sums_k[0] + sums_k[1][:HALF], sums_k[1][HALF:]], 0))
        d_value.append(jnp.concatenate([sums_v[0] + sums_v[1][:HALF], sums_v[1][HALF:]], 0).astype(BF))
    raw = jnp.concatenate(d_query + d_key, 1)
    cosine, sine = held[N.cos][...], held[N.sin][...]
    tiles = []
    for j in range(COL_O // 128):
        tile = raw[:, 128 * j : 128 * (j + 1)]
        tiles.append((tile * cosine - turned(tile) * sine).astype(BF))
    d_qk = jnp.concatenate(tiles, 1)
    d_v = jnp.concatenate([jnp.zeros((TOK_MB, SKIP_V), BF)] + d_value, 1)
    note(N.dqk, d_qk)
    note(N.dv, d_v)
    back_p = dot_nt(d_qk, held[N.att][:, :COL_O]) + dot_nt(d_v, held[N.att][:, COL_VX:])
    back_a, gain_a = norm_back(held[N.x][...].astype(F32), ga_ref[...], collect(back_p, place))
    return (grad_middle + back_a).astype(BF), gain_a, gain_b


SLOTS = dict(
    lead=(N.forward,),
    both=(N.forward, N.backward, N.store),
    ahead=(N.forward, N.store),
    behind=(N.backward, N.keep),
    last=(N.backward, N.weights),
)


def layer_kernel(name, micro, names, refs):
    does = SLOTS[name]
    ref = dict(zip(names, refs))
    held = {key: ref["held_" + key] for key in HELD if "held_" + key in ref}
    kept = {key: ref["kept_" + key] for key in STORED if "kept_" + key in ref} or None
    section = ref[N.coords][3]
    index = {N.zero: 0, N.one: 1, N.same: section, N.other: 1 - section}[micro]
    copies = Copies(ref[N.sems])

    def bring(key):
        copies.start(key, ref[key].at[index], held[key])

    def bring_x():
        if N.arrived in ref:
            copies.start_either(N.x, section == 0, ref[N.tokens].at[index], ref[N.arrived], held[N.x])
        else:
            copies.start(N.x, ref[N.tokens].at[index], held[N.x])

    def bring_weights(order):
        for key in order:
            if key == N.down:
                if N.down in ref:
                    copies.start(key, ref[N.down], held[N.down])
                    continue
                own_z, own_x, own_c = (ref[N.coords][i] for i in range(3))
                for at in range(GROUPS // 2):
                    chip = lax.bitwise_xor(own_z, at // 2) * 2 + lax.bitwise_xor(own_x, at % 2)
                    copies.start(key, ref[N.c_own].at[at], held[N.down].at[chip * 2 + own_c])
                    copies.start(key, ref[N.c_other].at[at], held[N.down].at[chip * 2 + 1 - own_c])
            elif key == N.place:
                copies.start(key, ref[N.place], held[N.place])
            else:
                copies.start(key, ref[N.agu].at[(N.att, N.gw, N.uw).index(key)], held[key])

    def bring_g():
        if N.arrived_grad in ref:
            copies.start_either(N.g, section == 0, ref[N.arrived_grad], ref[N.out_grad].at[index], held[N.g])
        else:
            copies.start(N.g, ref[N.out_grad].at[index], held[N.g])

    if N.forward in does:
        bring_x()
        bring_weights([N.place, N.att])
        bring(N.cos)
        bring(N.sin)
        bring(N.mask)
        bring_weights([N.gw, N.uw, N.down])
        if N.backward in does:
            bring_g()
    else:
        bring_g()
        bring_weights([N.down])
        for c in range(0, FF, CHUNK):
            for key in (N.gate, N.up):
                copies.start(key + str(c), ref["stored_" + key].at[:, c : c + CHUNK], kept[key].at[:, c : c + CHUNK])
        bring_weights([N.gw, N.uw, N.place])
        copies.start(N.mid, ref[N.stored_mid], kept[N.mid])
        bring_weights([N.att])
        for key in (N.qk, N.v, N.lse):
            copies.start(key, ref["stored_" + key], kept[key])
        bring(N.mask)
        bring(N.cos)
        bring(N.sin)
        bring_x()

    def note_stored(key, value, column=None):
        if key == N.laid:
            if N.laid in ref:
                copies.start(N.laid, held[N.down], ref[N.laid])
            return
        if N.store in does:
            if value is not None:
                kept[key][...] = value
            copies.start("out_" + key, kept[key], ref["store_" + key])

    if N.weights in does:
        for key in PAIRS:
            half = ref["in_" + key].at[pl.ds(0, TOK_MB)]
            if key == N.g:
                copies.start_either(key + "_0", section == 0, ref[N.grad_0], ref[N.out_grad].at[section], half)
            else:
                copies.start(key, ref[key + "_0"], half)
        for key in (N.act, N.nb, N.mx, N.na):
            copies.start(key, ref[key + "_1"], ref["in_" + key].at[pl.ds(TOK_MB, TOK_MB)])
        feed_forward, attention = weight_parts(ref, copies)

    def note_kept(key, value, column=None):
        if N.weights in does:
            columns = slice(None) if column is None else slice(column, column + CHUNK)
            ref["in_" + key][TOK_MB:, columns] = value
            if key == N.gattn:
                copies.wait(N.g + "_0")
                ref[N.in_g][TOK_MB:, :] = held[N.g][...]
                feed_forward()
        if N.keep in does:
            if column is None:
                ref["made_" + key][...] = value
            else:
                ref["made_" + key][:, column : column + CHUNK] = value
            if column in (None, FF - CHUNK):
                copies.start("out_" + key, ref["made_" + key], ref["keep_" + key])

    if N.forward in does:
        ref[N.out][...] = forward(held, kept, copies, ref[N.ga], ref[N.gb], note_stored)
    if N.backward in does:
        grad, gain_a, gain_b = backward(held, kept, copies, ref[N.ga], ref[N.gb], note_kept)
        ref[N.in_grad][...] = grad
        if N.weights in does:
            attention()
        if N.keep in does or N.weights in does:
            ref[N.gains][0:1, :] = gain_a
            ref[N.gains][1:2, :] = gain_b
    copies.wait_all()


def run_layer(name, micro, common, tokens, arrived=None, out_grad=None, arrived_grad=None, stored=None, rows=None, first_grad=None):
    does = SLOTS[name]
    operands = dict(coords=common[N.coords], tokens=tokens, ga=common[N.ga], gb=common[N.gb])
    operands.update({key: common[key] for key in INPUTS if key in common})
    specs = dict(coords=SMEM, ga=VMEM, gb=VMEM)
    if arrived is not None:
        operands[N.arrived] = arrived
    if N.backward in does:
        operands[N.out_grad] = out_grad
        if arrived_grad is not None:
            operands[N.arrived_grad] = arrived_grad
    if stored is not None:
        operands.update({"stored_" + key: stored[key] for key in FOR_BACK})
    if N.weights in does:
        operands.update({key + "_0": rows[key] for key in PAIRS if key != N.g})
        operands.update({key + "_1": stored[key] for key in (N.act, N.nb, N.mx, N.na)})
        operands[N.grad_0] = first_grad
    outs, out_specs = {}, []
    if N.forward in does:
        outs[N.out] = shape(TOK_MB, D)
    if N.down not in common:
        outs[N.laid] = INPUTS[N.down]
    if N.backward in does:
        outs[N.in_grad] = shape(TOK_MB, D)
    if N.weights in does:
        outs[N.gains] = shape(2, D, dtype=F32)
        outs.update({key: shape(2, 4, 4, EACH, FF) for key in (N.out_keep_m, N.out_send_m)})
    if N.keep in does:
        outs[N.gains] = shape(2, D, dtype=F32)
        outs.update({"keep_" + key: KEPT[key] for key in KEPT})
    if N.store in does:
        outs.update({"store_" + key: STORED[key] for key in STORED})
    out_specs = [ANY if key.startswith(("store_", "keep_", "laid", "out_")) else VMEM for key in outs]
    scratch = {"held_" + key: pltpu.VMEM(h.shape, h.dtype) for key, h in HELD.items() if key != N.g or N.backward in does}
    if name != N.lead:
        hold = STORED if N.forward in does else FOR_BACK
        scratch.update({"kept_" + key: pltpu.VMEM(STORED[key].shape, STORED[key].dtype) for key in hold})
    if N.keep in does:
        scratch.update({"made_" + key: pltpu.VMEM(KEPT[key].shape, BF) for key in KEPT})
    if N.weights in does:
        columns = {key: (STORED | KEPT | {N.g: HELD[N.g]})[key].shape[1] for key in PAIRS}
        scratch.update({"in_" + key: pltpu.VMEM((2 * TOK_MB, columns[key]), BF) for key in PAIRS})
        scratch.update({key: pltpu.VMEM((2, 4, 4, EACH, FF), BF) for key in (N.keep_m, N.send_m)})
    scratch[N.sems] = pltpu.SemaphoreType.DMA((48 if N.weights in does else 28 if N.down in common else 44,))
    names = list(operands) + list(outs) + list(scratch)

    def kernel(*refs):
        layer_kernel(name, micro, names, refs)

    results = pl.pallas_call(
        kernel,
        out_shape=list(outs.values()),
        in_specs=[specs.get(key, ANY) for key in operands],
        out_specs=out_specs,
        scratch_shapes=list(scratch.values()),
        compiler_params=PARAMS,
        name="layer_" + name,
    )(*operands.values())
    return dict(zip(outs, results))


PAIRS = (N.act, N.g, N.nb, N.dg, N.du, N.mx, N.gattn, N.na, N.dqk, N.dv)


def slab_of(block):
    return jnp.concatenate(
        [
            jnp.concatenate([block[8 * i : 8 * i + 8, 128 * j : 128 * j + 128] for i in range(EACH_FF // 8)], 1)
            for j in range(PAD // 128)
        ],
        0,
    )


def block_of(slab):
    tiles = slab.reshape(slab.shape[:-2] + (PAD // 128, 8, EACH_FF // 8, 128))
    return jnp.moveaxis(tiles, -2, -4).swapaxes(-3, -2).reshape(slab.shape[:-2] + (EACH_FF, PAD))


def weight_parts(ref, copies):
    own_z, own_x, own_c = (ref[N.coords][i] for i in range(3))

    def put_pairs(keep_ref, send_ref, at, columns, blocks, pair):
        for one, two in zip(blocks[::2], blocks[1::2]):
            far, across = lax.bitwise_xor(own_z, pair // 2), lax.bitwise_xor(own_x, pair % 2)
            index = (across, far) + at + (slice(None), columns)
            keep_ref[index] = jnp.where(own_c == 0, one, two).astype(BF)
            send_ref[index] = jnp.where(own_c == 0, two, one).astype(BF)
            pair += 1

    def put(keep_ref, send_ref, at, columns, rows):
        put_pairs(keep_ref, send_ref, at, columns, jnp.split(rows, GROUPS), 0)

    def feed_forward():
        copies.wait(N.act, N.g)
        grad_down = jnp.concatenate([ref[N.in_g][...], jnp.zeros((2 * TOK_MB, PAD - D), BF)], 1)
        step = 4 * EACH_FF
        for c in range(0, FF, step):
            slabs = [slab_of(piece) for piece in jnp.split(dot_tn(ref[N.in_act][:, c : c + step], grad_down), 4)]
            put_pairs(ref[N.keep_m], ref[N.send_m], (3,), slice(0, FF), slabs, c // step * 2)
        copies.wait(N.nb, N.dg, N.du)
        normed_b = ref[N.in_nb][...]
        for at, key in ((1, N.dg), (2, N.du)):
            for c in range(0, FF, CHUNK):
                put(ref[N.keep_m], ref[N.send_m], (at,), slice(c, c + CHUNK), dot_tn(normed_b, ref["in_" + key][:, c : c + CHUNK]))
        for slab in range(1, 4):
            copies.start(N.out, ref[N.send_m].at[:, :, slab], ref[N.out_send_m].at[:, :, slab])
            copies.start(N.out, ref[N.keep_m].at[:, :, slab], ref[N.out_keep_m].at[:, :, slab])

    def attention():
        copies.wait(N.mx, N.gattn, N.na, N.dqk, N.dv)
        normed_a, mixed = ref[N.in_na][...], ref[N.in_mx][...]
        put(ref[N.keep_m], ref[N.send_m], (0,), slice(0, COL_O), dot_tn(normed_a, ref[N.in_dqk][...]))
        put(ref[N.keep_m], ref[N.send_m], (0,), slice(COL_O, COL_VX), dot_tn(mixed, ref[N.in_gattn][:, : COL_VX - COL_O]))
        grad_o = dot_tn(mixed, ref[N.in_gattn][:, COL_VX - COL_O :])
        grad_o = jnp.concatenate([grad_o, jnp.zeros((PAD, KVW), F32)], 1)
        put(ref[N.keep_m], ref[N.send_m], (0,), slice(COL_VX, FF), dot_tn(normed_a, ref[N.in_dv][...]) + grad_o)
        copies.start(N.out, ref[N.send_m].at[:, :, 0], ref[N.out_send_m].at[:, :, 0])
        copies.start(N.out, ref[N.keep_m].at[:, :, 0], ref[N.out_keep_m].at[:, :, 0])

    return feed_forward, attention


def make_tables(seg_row):
    count_t = seg_row.shape[0]
    order_idx = jnp.arange(count_t, dtype=jnp.int32)
    same_doc = seg_row[:, None] == seg_row[None, :]
    before = order_idx[None, :] < order_idx[:, None]
    positions = jnp.sum(jnp.where(same_doc & before, jnp.float32(1.0), jnp.float32(0.0)), axis=1)
    allowed = same_doc & (order_idx[None, :] <= order_idx[:, None])
    inv_freq = jnp.exp(jnp.arange(HEAD // 2, dtype=jnp.float32) * (-2.0 * math.log(THETA) / HEAD))
    angles = positions[:, None] * inv_freq[None, :]
    cosine, sine = jnp.cos(angles), jnp.sin(angles)
    cosine = jnp.concatenate([cosine] * 4, -1)
    sine = jnp.concatenate([-sine, sine] * 2, -1)
    return (cosine, sine, allowed.astype(F32))


def placement(rows_each, rows_padded):
    row = lax.broadcasted_iota(jnp.int32, (D, PAD), 0)
    col = lax.broadcasted_iota(jnp.int32, (D, PAD), 1)
    return (col == row + (row // rows_each) * (rows_padded - rows_each)).astype(BF)


def place_of(z, x, c):
    return (z * 2 + x) * 2 + c


PLACES = [(z, x, c) for z in range(4) for x in range(2) for c in range(2)]


def moved(value, dz, dx, dc):
    return lax.ppermute(value, "dp", [(place_of(z, x, c), place_of(z ^ dz, x ^ dx, c ^ dc)) for z, x, c in PLACES])


def gather_weights(shard, owners):
    w_query, w_key, w_value, w_out, w_gate, w_up, w_down = shard
    if owners == GROUPS:
        rows = D // owners
        att = jnp.concatenate(
            [w_query.reshape(rows, QW), w_key.reshape(rows, KVW), w_out.reshape(rows, D), w_value.reshape(rows, KVW)], 1
        )
        packed = jnp.stack([att, w_gate.reshape(rows, FF), w_up.reshape(rows, FF)])
        packed = jnp.pad(packed, ((0, 0), (0, EACH - rows), (0, 0)))
        agu = lax.all_gather(packed, "dp", axis=1, tiled=True)
        w_down = w_down.reshape(EACH_FF, D)
        lines = [w_down] + [moved(w_down, dz, 0, 0) for dz in (1, 2, 3)]
        c_own = jnp.stack([block for line in lines for block in (line, moved(line, 0, 1, 0))])
        c_other = moved(c_own, 0, 0, 1)
        c_own, c_other, corner = lax.optimization_barrier((c_own, c_other, w_down[:8, :128]))
        met = lax.all_gather(corner, "dp", axis=0, tiled=False)
        corner = lax.dynamic_index_in_dim(met, lax.axis_index("dp"), 0, keepdims=False)
        c_own = c_own.at[0, :8, :128].set(corner)
        return agu, c_own, c_other, placement(rows, EACH)
    w_query, w_key, w_value, w_out, w_gate, w_up, w_down = (
        lax.all_gather(member[0], "dp", axis=0, tiled=True) for member in shard
    )
    att = jnp.concatenate(
        [w_query.reshape(D, QW), w_key.reshape(D, KVW), w_out.reshape(QW, D), w_value.reshape(D, KVW)], 1
    )
    agu = jnp.pad(jnp.stack([att, w_gate.reshape(D, FF), w_up.reshape(D, FF)]), ((0, 0), (0, PAD - D), (0, 0)))
    down = w_down.reshape(GROUPS // 2, 2, EACH_FF, D)
    return agu, down[:, 0], down[:, 1], placement(D, D)


def cut(att):
    return att[:, :QW], att[:, COL_K:COL_O], att[:, COL_V:], att[:, COL_O:COL_V]


def add(*terms):
    return sum(term.astype(F32) for term in terms)


def sum_of_four(value, others):
    return (value + others[0]) + (others[1] + others[2])


def reduce_blocks(keep, send, gains):
    near = [moved(gains, 0, 0, 1), moved(gains, 0, 1, 0), moved(gains, 0, 1, 1)]
    got = moved(send, 0, 0, 1)
    got, near = lax.optimization_barrier((got, near))
    gains = sum_of_four(gains, near)
    wide = [moved(gains, 1, 0, 0), moved(gains, 2, 0, 0), moved(gains, 3, 0, 0)]
    blocks = [add(keep[1, far], got[1, far]).astype(BF) for far in range(4)]
    part_one = add(keep[0, 1], got[0, 1])
    across_three, across_two = moved(blocks[3], 0, 1, 0), moved(blocks[2], 0, 1, 0)
    across_three, wide = lax.optimization_barrier((across_three, wide))
    gains = sum_of_four(gains, wide)
    three = add(keep[0, 3], got[0, 3], across_three).astype(BF)
    three, last_one = lax.optimization_barrier((three, blocks[1]))
    beside_three, across_one = moved(three, 1, 0, 0), moved(last_one, 0, 1, 0)
    across_two, last_zero = lax.optimization_barrier((across_two, blocks[0]))
    across_zero = moved(last_zero, 0, 1, 0)
    two = add(keep[0, 2], got[0, 2], across_two, beside_three).astype(BF)
    two, part_one = lax.optimization_barrier((two, part_one))
    far_two = moved(two, 2, 0, 0)
    beside_one = moved((part_one + across_one).astype(BF), 1, 0, 0)
    return add(keep[0, 0], got[0, 0], across_zero, far_two, beside_one), gains


def scatter_grads(out, gains, owners):
    if owners == GROUPS:
        main, gains = reduce_blocks(out[N.out_keep_m], out[N.out_send_m], gains)
        rows = D // owners
        att, gate, up = main[0, :rows], main[1, :rows], main[2, :rows]
        down = block_of(main[3])[:, :D]
        return tuple(piece.reshape(1, -1) for piece in cut(att) + (gate, up, down)) + (gains[0:1], gains[1:2])
    main = jnp.stack([out[N.out_keep_m], out[N.out_send_m]]).transpose(3, 2, 1, 0, 4, 5).reshape(4, GROUPS, EACH, FF)
    down = block_of(main[3])[:, :, :D].reshape(FF, D)
    main = main[:3].reshape(3, PAD, FF)[:, :D]
    pieces = cut(main[0]) + (main[1], main[2], down)
    gains = lax.psum(gains, "dp")
    return tuple(
        lax.psum_scatter(piece.reshape(owners, -1), "dp", scatter_dimension=0, tiled=True).astype(F32) for piece in pieces
    ) + (gains[0:1], gains[1:2])


def shards(
    tokens,
    segments,
    w_query,
    w_key,
    w_value,
    w_out,
    w_gate,
    w_up,
    w_down,
    attn_gain,
    mlp_gain,
    out_grad,
):
    section = lax.axis_index("section")
    first = section == 0
    owners = lax.axis_size("dp")
    me = lax.axis_index("dp") if owners == GROUPS else 0
    coords = jnp.stack([me // 4, me // 2 % 2, me % 2, section, 0, 0, 0, 0]).astype(jnp.int32)
    agu, c_own, c_other, place = gather_weights((w_query, w_key, w_value, w_out, w_gate, w_up, w_down), owners)
    cosine, sine, mask = jax.vmap(make_tables)(segments[:, 0])
    agu, c_own, c_other, place, cosine, sine, mask, tokens, out_grad, coords = lax.optimization_barrier(
        (agu, c_own, c_other, place, cosine, sine, mask, tokens, out_grad, coords)
    )
    common = dict(
        agu=agu, c_own=c_own, c_other=c_other, place=place, cos=cosine, sin=sine, mask=mask, coords=coords, ga=attn_gain, gb=mlp_gain
    )

    def send_on(block):
        return lax.ppermute(block, "section", [(0, 1)])

    def send_back(block):
        return lax.ppermute(block, "section", [(1, 0)])

    def stored_of(outs):
        return {key: outs["store_" + key] for key in STORED}

    def rows_of(stored, outs):
        return stored | {key: outs["keep_" + key] for key in KEPT}

    first_out = run_layer(N.lead, N.zero, common, tokens)
    lead_zero = first_out[N.out]
    common = {key: common[key] for key in common if key not in (N.c_own, N.c_other)} | {N.down: first_out[N.laid]}
    arrived_zero = send_on(lead_zero)
    lead_one = run_layer(N.lead, N.one, common, tokens)[N.out]
    arrived_one = send_on(lead_one)
    two = run_layer(N.both, N.other, common, tokens, arrived_zero, out_grad)
    arrived_grad = send_back(two[N.in_grad])
    four = run_layer(N.ahead, N.same, common, tokens, arrived_one)
    stored_two, stored_four = stored_of(two), stored_of(four)
    five = run_layer(N.behind, N.same, common, tokens, arrived_one, out_grad, arrived_grad, stored_four)
    last_grad = send_back(five[N.in_grad])
    six = run_layer(
        N.last, N.other, common, tokens, arrived_zero, out_grad, last_grad, stored_two, rows_of(stored_four, five), arrived_grad
    )
    grads = six
    shares = scatter_grads(grads, five[N.gains] + six[N.gains], owners)
    layer_out = jnp.stack([jnp.where(first, four[N.out], two[N.out]), jnp.where(first, two[N.out], four[N.out])])
    input_grad = jnp.stack([jnp.where(first, five[N.in_grad], six[N.in_grad]), jnp.where(first, six[N.in_grad], five[N.in_grad])])
    return (layer_out[None], input_grad[None], *shares)


def solution(mesh):
    weights = (P("section", "dp"),) * 7
    gains = (P("section", None),) * 2
    rows = P("section", None, "dp", None)
    return jax.shard_map(
        shards,
        mesh=mesh,
        in_specs=(P(None, "dp", None), P(None, "dp", None), *weights, *gains, P(None, "dp", None)),
        out_specs=(rows, rows, *weights, *gains),
        check_vma=False,
    )
```
